32 devices in a mesh: scene: 2 (over y), tok: 8 (over z, x), hid: 2 (over core).
Axes of the slice: x: 2, y: 2, z: 4, core: 2. Of those that a mesh axis runs over, the one named last changes fastest.
Arguments:
- input_keys: bfloat16 [16384, 384], P(('scene', 'tok'), 'hid'), parts along dimension 0, may hold values from -6 to 6
- input_values: bfloat16 [16384, 384], P(('scene', 'tok'), 'hid'), parts along dimension 0, may hold values from -6 to 6
- input_lr: float32 [16384], P(('scene', 'tok')), parts along dimension 0, may hold values from 0.1 to 1
- gate_weight: bfloat16 [384, 1536], P('tok', 'hid'), may hold values from -0.3125 to 0.3125
- up_weight: bfloat16 [384, 1536], P('tok', 'hid'), may hold values from -0.3125 to 0.3125
- down_weight: bfloat16 [384, 1536], P('tok', 'hid'), may hold values from -0.15625 to 0.15625
- queries: bfloat16 [2048, 384], P(('scene', 'tok'), 'hid'), parts along dimension 0, may hold values from -6 to 6
- out_grad: bfloat16 [2048, 384], P(('scene', 'tok'), 'hid'), parts along dimension 0, may hold values from -6 to 6
Outputs:
- target_out: bfloat16 [2048, 384], P(('scene', 'tok'), 'hid'), parts along dimension 0
- query_grad: bfloat16 [2048, 384], P(('scene', 'tok'), 'hid'), parts along dimension 0
The draws below stay inside these ranges and needn't reach their ends.
There are 2 independent parts, one for each index of `scene`. The reference program is written for one: setup_inputs(seed, part) draws one part's arguments, and reference() takes and returns one part's arrays. A program takes and returns all parts, laid end to end along the dimension named above; an argument that names none is the same for every part. Nothing has to cross between parts.
All inputs are finite; a program needn't handle non-finite values.
Results may differ from the reference program's by a relative error of at most 0.009.
Values may be sent and summed in bfloat16 or wider, within the bound.
No kernel may reach another device: no remote copies, remote signals or barrier semaphores. Data moves between devices by JAX's collectives and lax.ppermute only.
A program may use at most 64 MiB of HBM per device.

```python
import math
import jax
import jax.numpy as jnp
from jax import lax

D = 384
HID = 1536
TIN = 8192
TTG = 1024


def raised(drawn, stream_key, source, target, blocks, factor):
    def block_of(position):
        return (jnp.arange(drawn.shape[position]) // (drawn.shape[position] // blocks)).reshape((-1,) + (1,) * (drawn.ndim - 1 - position))

    near = jax.random.permutation(stream_key, blocks)[block_of(target)]
    far = (block_of(target) + blocks // 2) % blocks
    return jnp.where((block_of(source) == near) | (block_of(source) == far), factor * drawn, drawn)


def block_levels(own_key, shape, shards, low, high):
    def one(position, blocks):
        heights = jax.random.uniform(jax.random.fold_in(jax.random.fold_in(own_key, 6), position), (blocks,), jnp.float32, low / len(shards), high / len(shards))
        return jnp.repeat(jnp.exp(heights), shape[position] // blocks).reshape((-1,) + (1,) * (len(shape) - position - 1))

    loudness = one(*shards[0])
    for cut in shards[1:]:
        loudness = loudness * one(*cut)
    return loudness


def noise(rng, dims, scale, limit, cuts=(), held_as=jnp.bfloat16):
    drawn = scale * jax.random.normal(rng, dims, jnp.float32)
    if cuts:
        drawn = drawn * block_levels(rng, dims, cuts, -0.22, 0.18)
    return jnp.clip(drawn, -limit, limit).astype(held_as)


def bell_draw_with(own_key, extent, spread, reach, pieces, heavy, held_as=jnp.bfloat16):
    result = spread * jax.random.normal(own_key, extent, jnp.float32)
    if pieces:
        result = result * block_levels(own_key, extent, pieces, -0.22, 0.18)
    return jnp.clip(raised(result, jax.random.fold_in(own_key, 3), *heavy), -reach, reach).astype(held_as)


def setup_inputs(seed: int = 0, part: int = 0) -> dict:
    splits = jax.random.split(jax.random.key(seed), 9)
    part_keys = jax.random.split(jax.random.fold_in(splits[8], part), 9)
    return {
        "input_keys": bell_draw_with(part_keys[0], (TIN, D), 1.0, 6.0, ((0, 8), (1, 2)), (0, 1, 8, 2.0)),
        "input_values": bell_draw_with(part_keys[1], (TIN, D), 1.0, 6.0, ((0, 8), (1, 2)), (0, 1, 8, 2.0)),
        "input_lr": jnp.clip(jnp.exp(math.log(1.0) - 2.3025851 * jax.random.uniform(part_keys[2], (TIN,), jnp.float32) ** block_levels(part_keys[2], (TIN,), ((0, 8),), -0.2, 0.2)), 0.1, 1.0),
        "gate_weight": noise(splits[3], (D, HID), D ** -0.5, 0.3125, ((0, 8), (1, 2))),
        "up_weight": noise(splits[4], (D, HID), D ** -0.5, 0.3125, ((0, 8), (1, 2))),
        "down_weight": noise(splits[5], (D, HID), HID ** -0.5, 0.15625, ((0, 8), (1, 2))),
        "queries": noise(part_keys[6], (TTG, D), 1.0, 6.0, ((0, 8), (1, 2))),
        "out_grad": noise(part_keys[7], (TTG, D), 1.0, 6.0, ((0, 8), (1, 2))),
    }


step_ratio = 0.5
epsilon = 1e-06

def silu_slope(pre):
    sigma = jax.nn.sigmoid(pre)
    return sigma * (1.0 + pre * (1.0 - sigma))

def contract_rows(left, right):
    return lax.dot_general(left, right, (((0,), (0,)), ((), ())), preferred_element_type=jnp.float32)

def contract_cols(left, right):
    return lax.dot_general(left, right, (((1,), (1,)), ((), ())), preferred_element_type=jnp.float32)

def renew(weight, grad):
    base = weight.astype(jnp.float32)
    wsq = lax.optimization_barrier(jnp.sum(base * base, axis=1)) / HID
    gsq = lax.optimization_barrier(jnp.sum(grad * grad, axis=1)) / HID
    scale = step_ratio * jnp.sqrt(wsq) / jnp.sqrt(gsq + epsilon)
    moved = base - scale[:, None] * grad
    msq = lax.optimization_barrier(jnp.sum(moved * moved, axis=1)) / HID
    return (moved * (jnp.sqrt(wsq) / jnp.sqrt(msq + epsilon))[:, None]).astype(jnp.bfloat16)

def reference(input_keys, input_values, input_lr, gate_weight, up_weight, down_weight, queries, out_grad):
    total_in = input_keys.shape[0]
    block_in = min(total_in, 4096)
    count_in = total_in // block_in
    key_blocks = input_keys.reshape(count_in, block_in, D)
    value_blocks = input_values.reshape(count_in, block_in, D)
    rate_blocks = input_lr.reshape(count_in, block_in)

    def accumulate(carry, item):
        keys, values, rates = item
        scaled = (rates[:, None] * values.astype(jnp.float32)).astype(jnp.bfloat16)
        key_gate = jnp.dot(keys, gate_weight, preferred_element_type=jnp.float32)
        key_up = jnp.dot(keys, up_weight, preferred_element_type=jnp.float32)
        gate_act = jax.nn.silu(key_gate)
        key_act = (gate_act * key_up).astype(jnp.bfloat16)
        back = jnp.dot(scaled, down_weight, preferred_element_type=jnp.float32)
        d_gate = (-back * key_up * silu_slope(key_gate)).astype(jnp.bfloat16)
        d_up = (-back * gate_act).astype(jnp.bfloat16)
        grad_gate = carry[0] + contract_rows(keys, d_gate)
        grad_up = carry[1] + contract_rows(keys, d_up)
        grad_down = carry[2] - contract_rows(scaled, key_act)
        return ((grad_gate, grad_up, grad_down), None)
    zeros = jnp.zeros((D, HID), jnp.float32)
    (grad_gate, grad_up, grad_down), _ = lax.scan(accumulate, (zeros, zeros, zeros), (key_blocks, value_blocks, rate_blocks))
    new_gate = renew(gate_weight, grad_gate)
    new_up = renew(up_weight, grad_up)
    new_down = renew(down_weight, grad_down)
    total_tg = queries.shape[0]
    block_tg = min(total_tg, 4096)
    count_tg = total_tg // block_tg

    def apply_block(item):
        query_rows, grad_rows = item
        query_gate = jnp.dot(query_rows, new_gate, preferred_element_type=jnp.float32)
        query_up = jnp.dot(query_rows, new_up, preferred_element_type=jnp.float32)
        gate_act = jax.nn.silu(query_gate)
        query_act = (gate_act * query_up).astype(jnp.bfloat16)
        target_out = contract_cols(query_act, new_down).astype(jnp.bfloat16)
        query_back = jnp.dot(grad_rows, new_down, preferred_element_type=jnp.float32)
        q_gate_grad = (query_back * query_up * silu_slope(query_gate)).astype(jnp.bfloat16)
        q_up_grad = (query_back * gate_act).astype(jnp.bfloat16)
        query_grad = (contract_cols(q_gate_grad, new_gate) + contract_cols(q_up_grad, new_up)).astype(jnp.bfloat16)
        return (target_out, query_grad)
    outs_blocks, grad_blocks = lax.map(apply_block, (queries.reshape(count_tg, block_tg, D), out_grad.reshape(count_tg, block_tg, D)))
    return (outs_blocks.reshape(total_tg, D), grad_blocks.reshape(total_tg, D))
```

```python
import functools

import jax
import jax.numpy as jnp
from jax import lax
from jax.experimental import pallas as pl
from jax.experimental.pallas import tpu as pltpu
from jax.sharding import PartitionSpec as P

step_ratio = 0.5
epsilon = 1e-06
f32, bf16 = jnp.float32, jnp.bfloat16


def contract(left, right, left_dim, right_dim):
    return lax.dot_general(
        left, right, (((left_dim,), (right_dim,)), ((), ())), preferred_element_type=f32
    )


def gated(gate, up):
    sigma = jax.nn.sigmoid(gate)
    silu = gate * sigma
    slope = sigma * (1.0 + gate * (1.0 - sigma))
    return silu, slope * up, silu * up


def token_kernel(groups, place, *refs):
    (key_a, key_b, key_c, key_d, val_a, val_b, val_c, val_d), refs = refs[:8], refs[8:]
    own_w, pair_w, refs = refs[0], refs[1], refs[2:]
    first, second, refs = refs[: groups - 1], refs[groups - 1 : 2 * groups - 2], refs[2 * groups - 2 :]
    weights, own_grad, sends, (keys, vals, grads) = refs[0], refs[1], refs[2 : groups + 1], refs[groups + 1 :]
    group, side, half = place[0], place[1], place[2]
    feats, toks = key_a.shape
    rows = own_w.shape[1]

    for full, parts in ((keys, (key_a, key_b, key_c, key_d)), (vals, (val_a, val_b, val_c, val_d))):
        here = pl.ds(pl.multiple_of(half * feats, feats), feats)
        there = pl.ds(pl.multiple_of((1 - half) * feats, feats), feats)
        full[here, :toks] = parts[0][...]
        full[there, :toks] = parts[1][...]
        full[here, toks:] = parts[2][...]
        full[there, toks:] = parts[3][...]

    def place_rows(source, owner, sided):
        start = pl.multiple_of((owner * 2 + sided) * rows, rows)
        weights[:, pl.ds(start, rows), :] = source[...]

    place_rows(own_w, group, side)
    place_rows(pair_w, group, 1 - side)
    for step in range(1, groups):
        place_rows(first[step - 1], group ^ step, side)
        place_rows(second[step - 1], group ^ step, 1 - side)

    total = 2 * toks
    chunk = min(512, total)
    for start in range(0, total, chunk):
        key = keys[:, start : start + chunk]
        val = vals[:, start : start + chunk]
        gate = contract(weights[0], key, 0, 0)
        up = contract(weights[1], key, 0, 0)
        back = contract(weights[2], val, 0, 0)
        silu, slope_up, act = gated(gate, up)
        d_gate = (back * slope_up).astype(bf16)
        d_up = (back * silu).astype(bf16)
        parts = (
            contract(key, d_gate, 1, 1),
            contract(key, d_up, 1, 1),
            contract(val, act.astype(bf16), 1, 1),
        )
        for index, part in enumerate(parts):
            if start == 0:
                grads[index] = part
            else:
                grads[index] += part

    def rows_of(owner):
        return grads[:, pl.ds(pl.multiple_of(owner * 2 * rows, 2 * rows), 2 * rows), :]

    own_grad[...] = rows_of(group)
    for step in range(1, groups):
        sends[step - 1][...] = rows_of(group ^ step).astype(bf16)


def sum_kernel(groups, place, weights, own, *refs):
    arrived, (total_out, stats_out) = refs[: groups - 1], refs[groups - 1 :]
    rows = own.shape[1]
    mine = pl.ds(pl.multiple_of(place[0] * rows, rows), rows)
    lane = lax.broadcasted_iota(jnp.int32, stats_out.shape, 1)
    stats = jnp.zeros(stats_out.shape, f32)
    for index in range(3):
        grad = own[index]
        for other in arrived:
            grad = grad + other[index].astype(f32)
        total_out[index] = grad.astype(bf16)
        weight = weights[index, mine, :].astype(f32)
        for slot, product in enumerate((weight * weight, weight * grad, grad * grad)):
            row_sum = jnp.sum(product, axis=1, keepdims=True)
            stats = jnp.where(lane == 3 * index + slot, row_sum, stats)
    stats_out[...] = stats


def query_kernel(groups, hidden, place, weights, *refs):
    grads, refs = refs[:groups], refs[groups:]
    stats, refs = refs[:groups], refs[groups:]
    quests, refs = refs[:4], refs[4:]
    own_out, sends, (renewed, query, cotangent) = refs[0], refs[1:4], refs[4:]
    group, side, half = place[0], place[1], place[2]
    rows = grads[0].shape[1]
    feats, count = quests[0].shape[1:]

    for step in range(groups):
        where = pl.ds(pl.multiple_of((group ^ step) * rows, rows), rows)
        sums = stats[step][...] * (1.0 / hidden)
        for index in range(3):
            wsq = sums[:, 3 * index : 3 * index + 1]
            cross = sums[:, 3 * index + 1 : 3 * index + 2]
            gsq = sums[:, 3 * index + 2 : 3 * index + 3]
            scale = step_ratio * jnp.sqrt(wsq) / jnp.sqrt(gsq + epsilon)
            msq = wsq + 2.0 * scale * cross + scale * scale * gsq
            factor = jnp.sqrt(wsq) / jnp.sqrt(msq + epsilon)
            moved = weights[index, where, :].astype(f32) + scale * grads[step][index].astype(f32)
            renewed[index, where, :] = (moved * factor).astype(bf16)

    for flip in range(4):
        feat = pl.ds(pl.multiple_of((half ^ (flip & 1)) * feats, feats), feats)
        span = pl.ds(pl.multiple_of((side ^ (flip >> 1)) * count, count), count)
        query[feat, span] = quests[flip][0]
        cotangent[feat, span] = quests[flip][1]

    gate = contract(renewed[0], query[...], 0, 0)
    up = contract(renewed[1], query[...], 0, 0)
    back = contract(renewed[2], cotangent[...], 0, 0)
    silu, slope_up, act = gated(gate, up)
    out = contract(renewed[2], act.astype(bf16), 1, 0)
    grad = contract(renewed[0], (back * slope_up).astype(bf16), 1, 0) + contract(
        renewed[1], (back * silu).astype(bf16), 1, 0
    )
    query_out = (out, grad)
    for index in range(2):
        stage = query_out[index]
        result_at(stage, index, own_out, sends, side, half, feats, count)


def result_at(stage, index, own_out, sends, side, half, feats, count):
    def pick(sided, halved):
        left = jnp.where(halved == 0, stage[:feats], stage[feats:])
        return jnp.where(sided == 0, left[:, :count], left[:, count:])

    own_out[index] = pick(side, half)
    for flip in range(1, 4):
        sends[flip - 1][index] = pick(side ^ (flip >> 1), half ^ (flip & 1)).astype(bf16)


def call(body, n_in, outs, scratch, flops, moved):
    return pl.pallas_call(
        body,
        out_shape=outs,
        in_specs=[pl.BlockSpec(memory_space=pltpu.SMEM)]
        + [pl.BlockSpec(memory_space=pltpu.VMEM)] * n_in,
        out_specs=[pl.BlockSpec(memory_space=pltpu.VMEM)] * len(outs),
        scratch_shapes=scratch,
        compiler_params=pltpu.CompilerParams(vmem_limit_bytes=48 * 1024 * 1024),
        cost_estimate=pl.CostEstimate(flops=flops, bytes_accessed=moved, transcendentals=0),
    )


def direct(
    input_keys, input_values, input_lr, gate_weight, up_weight, down_weight, queries, out_grad,
    n_tok, n_hid,
):
    groups = n_tok // 2
    tok, half = lax.axis_index("tok"), lax.axis_index("hid")
    group, side = tok // 2, tok % 2
    place = jnp.stack([group, side, half]).astype(jnp.int32)

    def swap(array, flip):
        pairs = [(i, i ^ flip) for i in range(n_tok * n_hid)]
        return lax.ppermute(array, ("tok", "hid"), pairs)

    core, pair = 1, 2
    zed = [4 * step for step in range(1, groups)]

    keys = input_keys.T
    vals = (input_lr[None, :] * input_values.T.astype(f32)).astype(bf16)
    stacked = jnp.stack([gate_weight, up_weight, down_weight])
    cols = stacked.shape[2] // 2
    own_w = lax.dynamic_slice_in_dim(stacked, side * cols, cols, 2)
    give_w = lax.dynamic_slice_in_dim(stacked, (1 - side) * cols, cols, 2)
    pair_w = swap(give_w, pair)
    first = [swap(own_w, flip) for flip in zed]
    key_c = swap(keys, pair)
    val_c = swap(vals, pair)
    second = [swap(pair_w, flip) for flip in zed]
    key_b, val_b = swap(keys, core), swap(vals, core)
    key_d, val_d = swap(key_c, core), swap(val_c, core)

    feats, toks = keys.shape
    width = n_hid * feats
    rows = width // groups
    block = (3, rows, cols)
    token_flops = 6 * 2 * 2 * toks * width * cols
    token_step = call(
        functools.partial(token_kernel, groups),
        8 + 2 + 2 * (groups - 1),
        [jax.ShapeDtypeStruct((3, width, cols), bf16), jax.ShapeDtypeStruct(block, f32)]
        + [jax.ShapeDtypeStruct(block, bf16)] * (groups - 1),
        [
            pltpu.VMEM((width, 2 * toks), bf16),
            pltpu.VMEM((width, 2 * toks), bf16),
            pltpu.VMEM((3, width, cols), f32),
        ],
        token_flops,
        8 * feats * toks * 2 + 3 * width * cols * 4,
    )
    weights, own_grad, *sends = token_step(
        place, keys, key_b, key_c, key_d, vals, val_b, val_c, val_d, own_w, pair_w, *first, *second
    )
    arrived = [swap(send, flip) for send, flip in zip(sends, zed)]

    quest = jnp.stack([queries.T, out_grad.T])
    quest, _ = lax.optimization_barrier((quest, sends[0]))
    quests = [quest] + [swap(quest, flip) for flip in (1, 2, 3)]

    grad, stats = call(
        functools.partial(sum_kernel, groups),
        groups + 1,
        [jax.ShapeDtypeStruct(block, bf16), jax.ShapeDtypeStruct((rows, 128), f32)],
        [],
        30 * 3 * rows * cols,
        3 * rows * cols * 16,
    )(place, weights, own_grad, *arrived)
    grads = [grad] + [swap(grad, flip) for flip in zed]
    stats = stats + swap(stats, 1) + swap(stats, 2) + swap(stats, 3)
    stats = [stats] + [swap(stats, flip) for flip in zed]

    count = queries.shape[0]
    piece = (2, feats, count)
    own_out, *out_sends = call(
        functools.partial(query_kernel, groups, 2 * n_hid * cols),
        1 + 2 * groups + 4,
        [jax.ShapeDtypeStruct(piece, f32)] + [jax.ShapeDtypeStruct(piece, bf16)] * 3,
        [
            pltpu.VMEM((3, width, cols), bf16),
            pltpu.VMEM((width, 2 * count), bf16),
            pltpu.VMEM((width, 2 * count), bf16),
        ],
        6 * 2 * 2 * count * width * cols,
        6 * width * cols * 2,
    )(place, weights, *grads, *stats, *quests)
    total = own_out
    for send, flip in zip(out_sends, (1, 2, 3)):
        total = total + swap(send, flip).astype(f32)
    return total[0].astype(bf16).T, total[1].astype(bf16).T


def silu_slope(pre):
    sigma = jax.nn.sigmoid(pre)
    return sigma * (1.0 + pre * (1.0 - sigma))


def contract_rows(left, right):
    return lax.dot_general(
        left, right, (((0,), (0,)), ((), ())), preferred_element_type=jnp.float32
    )


def contract_cols(left, right):
    return lax.dot_general(
        left, right, (((1,), (1,)), ((), ())), preferred_element_type=jnp.float32
    )


def finish(moved, wsq, msq):
    return (moved * (jnp.sqrt(wsq) / jnp.sqrt(msq + epsilon))[:, None]).astype(jnp.bfloat16)


def general(
    input_keys, input_values, input_lr, gate_weight, up_weight, down_weight, queries, out_grad, n_hid
):
    keys, values = (
        lax.all_gather(input_keys, "hid", axis=1, tiled=True),
        lax.all_gather(input_values, "hid", axis=1, tiled=True),
    )
    w_gate, w_up, w_down = (
        lax.all_gather(gate_weight, "tok", axis=0, tiled=True),
        lax.all_gather(up_weight, "tok", axis=0, tiled=True),
        lax.all_gather(down_weight, "tok", axis=0, tiled=True),
    )
    scaled = (input_lr[:, None] * values.astype(jnp.float32)).astype(jnp.bfloat16)
    key_gate = jnp.dot(keys, w_gate, preferred_element_type=jnp.float32)
    key_up = jnp.dot(keys, w_up, preferred_element_type=jnp.float32)
    gate_act = jax.nn.silu(key_gate)
    key_act = (gate_act * key_up).astype(jnp.bfloat16)
    back = jnp.dot(scaled, w_down, preferred_element_type=jnp.float32)
    d_gate = (-back * key_up * silu_slope(key_gate)).astype(jnp.bfloat16)
    d_up = (-back * gate_act).astype(jnp.bfloat16)
    width = gate_weight.shape[1]
    hidden = width * n_hid
    grads = lax.psum(
        jnp.concatenate(
            [
                contract_rows(keys, d_gate),
                contract_rows(keys, d_up),
                -contract_rows(scaled, key_act),
            ],
            axis=1,
        ),
        "tok",
    )
    olds = (w_gate, w_up, w_down)
    pieces = [grads[:, :width], grads[:, width : 2 * width], grads[:, 2 * width :]]
    weights = [old.astype(jnp.float32) for old in olds]
    renewed = []
    stats = []
    for weight, grad in zip(weights, pieces):
        stats.append(jnp.sum(weight * weight, axis=1))
        stats.append(jnp.sum(weight * grad, axis=1))
        stats.append(jnp.sum(grad * grad, axis=1))
    totals = lax.psum(
        (stats[0], stats[1], stats[2], stats[3], stats[4], stats[5], stats[6], stats[7], stats[8]),
        "hid",
    )
    for index in range(3):
        wsq = totals[3 * index] / hidden
        cross = totals[3 * index + 1] / hidden
        gsq = totals[3 * index + 2] / hidden
        scale = step_ratio * jnp.sqrt(wsq) / jnp.sqrt(gsq + epsilon)
        moved = weights[index] - scale[:, None] * pieces[index]
        msq = wsq - 2.0 * scale * cross + scale * scale * gsq
        renewed.append(finish(moved, wsq, msq))
    new_gate, new_up, new_down = (renewed[0], renewed[1], renewed[2])
    query_rows, grad_rows = (
        lax.all_gather(queries, "hid", axis=1, tiled=True),
        lax.all_gather(out_grad, "hid", axis=1, tiled=True),
    )
    query_gate = jnp.dot(query_rows, new_gate, preferred_element_type=jnp.float32)
    query_up = jnp.dot(query_rows, new_up, preferred_element_type=jnp.float32)
    query_silu = jax.nn.silu(query_gate)
    query_act = (query_silu * query_up).astype(jnp.bfloat16)
    out_part = contract_cols(query_act, new_down)
    query_back = jnp.dot(grad_rows, new_down, preferred_element_type=jnp.float32)
    q_gate_grad = (query_back * query_up * silu_slope(query_gate)).astype(jnp.bfloat16)
    q_up_grad = (query_back * query_silu).astype(jnp.bfloat16)
    grad_part = contract_cols(q_gate_grad, new_gate) + contract_cols(q_up_grad, new_up)
    out_sum, grad_sum = (
        lax.psum_scatter(
            out_part.astype(jnp.bfloat16), "hid", scatter_dimension=1, tiled=True
        ).astype(jnp.float32),
        lax.psum_scatter(
            grad_part.astype(jnp.bfloat16), "hid", scatter_dimension=1, tiled=True
        ).astype(jnp.float32),
    )
    return (out_sum.astype(jnp.bfloat16), grad_sum.astype(jnp.bfloat16))


def solution(mesh):
    n_tok, n_hid = mesh.shape["tok"], mesh.shape["hid"]

    def shards(*args):
        rows, cols = args[3].shape
        toks, count = args[0].shape[0], args[6].shape[0]
        fits = (
            n_hid == 2
            and 2 <= n_tok <= 8
            and n_tok & (n_tok - 1) == 0
            and rows % 16 == 0
            and cols % 256 == 0
            and toks % 256 == 0
            and count % 128 == 0
        )
        if fits:
            return direct(*args, n_tok, n_hid)
        return general(*args, n_hid)

    return jax.shard_map(
        shards,
        mesh=mesh,
        in_specs=(
            P(("scene", "tok"), "hid"),
            P(("scene", "tok"), "hid"),
            P(("scene", "tok")),
            P("tok", "hid"),
            P("tok", "hid"),
            P("tok", "hid"),
            P(("scene", "tok"), "hid"),
            P(("scene", "tok"), "hid"),
        ),
        out_specs=(P(("scene", "tok"), "hid"), P(("scene", "tok"), "hid")),
        check_vma=False,
    )
```

```python
import functools

import jax
import jax.numpy as jnp
from jax import lax
from jax.experimental import pallas as pl
from jax.experimental.pallas import tpu as pltpu
from jax.sharding import PartitionSpec as P

step_ratio = 0.5
epsilon = 1e-06
f32, bf16 = jnp.float32, jnp.bfloat16


def contract(left, right, left_dim, right_dim):
    return lax.dot_general(
        left, right, (((left_dim,), (right_dim,)), ((), ())), preferred_element_type=f32
    )


def gated(gate, up):
    sigma = jax.nn.sigmoid(gate)
    silu = gate * sigma
    slope = sigma * (1.0 + gate * (1.0 - sigma))
    return silu, slope * up, silu * up


def join(full, mine, other, half):
    feats = mine.shape[-2]
    full[:, pl.ds(pl.multiple_of(half * feats, feats), feats), :] = mine[...]
    full[:, pl.ds(pl.multiple_of((1 - half) * feats, feats), feats), :] = other[...]


def add_grads(tokens, weights, grads, fresh):
    total = tokens.shape[2]
    chunk = min(512, total)
    for start in range(0, total, chunk):
        key = tokens[0, :, start : start + chunk]
        val = tokens[1, :, start : start + chunk]
        gate = contract(weights[0], key, 0, 0)
        up = contract(weights[1], key, 0, 0)
        back = contract(weights[2], val, 0, 0)
        silu, slope_up, act = gated(gate, up)
        parts = (
            contract(key, (back * slope_up).astype(bf16), 1, 1),
            contract(key, (back * silu).astype(bf16), 1, 1),
            contract(val, act.astype(bf16), 1, 1),
        )
        for index, part in enumerate(parts):
            if fresh and start == 0:
                grads[index] = part
            else:
                grads[index] += part


def rows_kernel(groups, place, *refs):
    blocks, (weights,) = refs[: 2 * groups], refs[2 * groups :]
    group, side = place[0], place[1]
    for index, block in enumerate(blocks):
        flip, sided = index % groups, (side if index < groups else 1 - side)
        weights[:, rows_of((group ^ flip) * 2 + sided, block.shape[1]), :] = block[...]


def own_kernel(place, mine, other, weights, grads, tokens):
    join(tokens, mine, other, place[2])
    add_grads(tokens, weights, grads, True)


def pair_kernel(groups, place, mine, other, weights, before, *refs):
    outs, (grads, tokens) = refs[:groups], refs[groups:]
    group, half = place[0], place[2]
    grads[...] = before[...]
    join(tokens, mine, other, half)
    add_grads(tokens, weights, grads, False)
    for flip, out in enumerate(outs):
        out[...] = grads[:, rows_of(group ^ flip, out.shape[1]), :].astype(out.dtype)


def rows_of(owner, rows):
    return pl.ds(pl.multiple_of(owner * rows, rows), rows)


def sum_kernel(arrivals, place, weights, own, *refs):
    arrived, (grad_out, stats_out) = refs[:arrivals], refs[arrivals:]
    where = rows_of(place[0], own.shape[1])
    lane = lax.broadcasted_iota(jnp.int32, stats_out.shape, 1)
    stats = jnp.zeros(stats_out.shape, f32)
    for index in range(3):
        grad = own[index]
        for other in arrived:
            grad = grad + other[index].astype(f32)
        grad_out[index] = grad.astype(bf16)
        weight = weights[index, where, :].astype(f32)
        for slot, product in enumerate((weight * weight, weight * grad, grad * grad)):
            row_sum = jnp.sum(product, axis=1, keepdims=True)
            stats = jnp.where(lane == 3 * index + slot, row_sum, stats)
    stats_out[...] = stats


def query_kernel(groups, hidden, place, weights, *refs):
    grads, stats, quests, refs = (
        refs[:groups],
        refs[groups : 2 * groups],
        refs[2 * groups : 2 * groups + 4],
        refs[2 * groups + 4 :],
    )
    own_out, sends, (renewed, query) = refs[0], refs[1:4], refs[4:]
    group, side, half = place[0], place[1], place[2]
    feats, count = quests[0].shape[1:]

    for flip in range(groups):
        where = rows_of(group ^ flip, grads[0].shape[1])
        sums = stats[flip][...] * (1.0 / hidden)
        for index in range(3):
            wsq = sums[:, 3 * index : 3 * index + 1]
            cross = sums[:, 3 * index + 1 : 3 * index + 2]
            gsq = sums[:, 3 * index + 2 : 3 * index + 3]
            scale = step_ratio * jnp.sqrt(wsq) / jnp.sqrt(gsq + epsilon)
            msq = wsq + 2.0 * scale * cross + scale * scale * gsq
            factor = jnp.sqrt(wsq) / jnp.sqrt(msq + epsilon)
            moved = weights[index, where, :].astype(f32) + scale * grads[flip][index].astype(f32)
            renewed[index, where, :] = (moved * factor).astype(bf16)
    for flip in range(4):
        feat = pl.ds(pl.multiple_of((half ^ (flip & 1)) * feats, feats), feats)
        span = pl.ds(pl.multiple_of((side ^ (flip >> 1)) * count, count), count)
        query[:, feat, span] = quests[flip][...]

    gate = contract(renewed[0], query[0], 0, 0)
    up = contract(renewed[1], query[0], 0, 0)
    back = contract(renewed[2], query[1], 0, 0)
    silu, slope_up, act = gated(gate, up)
    out = contract(renewed[2], act.astype(bf16), 1, 0)
    grad = contract(renewed[0], (back * slope_up).astype(bf16), 1, 0) + contract(
        renewed[1], (back * silu).astype(bf16), 1, 0
    )
    for index, whole in enumerate((out, grad)):
        for flip, target in enumerate((own_out, *sends)):
            left = jnp.where((half ^ (flip & 1)) == 0, whole[:feats], whole[feats:])
            piece = jnp.where((side ^ (flip >> 1)) == 0, left[:, :count], left[:, count:])
            target[index] = piece.astype(target.dtype)


def last_kernel(own, first, second, third, out, grad):
    for index, target in enumerate((out, grad)):
        total = own[index] + first[index].astype(f32) + second[index].astype(f32)
        target[...] = (total + third[index].astype(f32)).astype(bf16)


def call(body, operands, outs, scratch=(), flops=0, place=None, mib=4):
    specs = [pl.BlockSpec(memory_space=pltpu.VMEM)] * len(operands)
    if place is not None:
        specs, operands = [pl.BlockSpec(memory_space=pltpu.SMEM)] + specs, (place, *operands)
    moved = sum(4 * leaf.size for leaf in (*operands, *outs))
    return pl.pallas_call(
        body,
        out_shape=list(outs),
        in_specs=specs,
        out_specs=[pl.BlockSpec(memory_space=pltpu.VMEM)] * len(outs),
        scratch_shapes=list(scratch),
        compiler_params=pltpu.CompilerParams(vmem_limit_bytes=mib * 1024 * 1024),
        cost_estimate=pl.CostEstimate(flops=flops, bytes_accessed=moved, transcendentals=0),
    )(*operands)


def direct(
    input_keys, input_values, input_lr, gate_weight, up_weight, down_weight, queries, out_grad,
    n_tok, n_hid,
):
    groups = n_tok // 2
    tok, half = lax.axis_index("tok"), lax.axis_index("hid")
    group, side = tok // 2, tok % 2
    place = jnp.stack([group, side, half]).astype(jnp.int32)
    core, pair, zed = 1, 2, 4

    def swap(array, flip):
        pairs = [(i, i ^ flip) for i in range(n_tok * n_hid)]
        return lax.ppermute(array, ("tok", "hid"), pairs)

    def gather(block, beside=()):
        bits = [1 << place for place in range(groups.bit_length() - 1)]
        came = {bit: swap(block, zed * bit) for bit in reversed(bits)}
        came, _ = lax.optimization_barrier((came, beside))
        held = {0: block, **came}
        for flip in range(groups):
            if flip not in held:
                low = flip & -flip
                held[flip] = swap(held[flip ^ low], zed * low)
        return [held[flip] for flip in range(groups)]

    stacked = jnp.stack([gate_weight, up_weight, down_weight])
    cols = stacked.shape[2] // 2
    own_w = lax.dynamic_slice_in_dim(stacked, side * cols, cols, 2)
    give_w = lax.dynamic_slice_in_dim(stacked, (1 - side) * cols, cols, 2)
    vals = (input_lr[None, :] * input_values.T.astype(f32)).astype(bf16)
    tokens = jnp.stack([input_keys.T, vals])
    _, feats, toks = tokens.shape
    tokens, pair_w = lax.optimization_barrier((tokens, swap(give_w, pair)))
    first = gather(own_w)
    pair_w, _ = lax.optimization_barrier((pair_w, first[1]))
    second = gather(pair_w)
    pair_tokens = swap(tokens, pair)

    width = n_hid * feats
    rows = width // groups
    whole = (3, width, cols)
    block = (3, rows, cols)
    token_flops = 6 * 2 * toks * width * cols
    joined = pltpu.VMEM((2, width, toks), bf16)
    (weights,) = call(
        functools.partial(rows_kernel, groups),
        (*first, *second),
        (jax.ShapeDtypeStruct(whole, bf16),),
        place=place,
    )
    pair_tokens, weights = lax.optimization_barrier((pair_tokens, weights))
    (grads,) = call(
        own_kernel,
        (tokens, swap(tokens, core), weights),
        (jax.ShapeDtypeStruct(whole, f32),),
        [joined],
        token_flops,
        place,
        16,
    )
    shares = call(
        functools.partial(pair_kernel, groups),
        (pair_tokens, swap(pair_tokens, core), weights, grads),
        [jax.ShapeDtypeStruct(block, bf16 if flip else f32) for flip in range(groups)],
        [pltpu.VMEM(whole, f32), joined],
        token_flops,
        place,
        16,
    )
    quest = jnp.stack([queries.T, out_grad.T])
    quest, shares = lax.optimization_barrier((quest, shares))
    quests = [quest] + [swap(quest, flip) for flip in (1, 2, 3)]

    arrived = [swap(shares[flip], zed * flip) for flip in range(1, groups)]
    arrived, quests = lax.optimization_barrier((arrived, quests))
    grad, stats = call(
        functools.partial(sum_kernel, len(arrived)),
        (weights, shares[0], *arrived),
        (jax.ShapeDtypeStruct(block, bf16), jax.ShapeDtypeStruct((rows, 128), f32)),
        place=place,
    )
    stats = stats + swap(stats, core)
    stats = stats + swap(stats, pair)
    all_stats = [stats] + [swap(stats, zed * flip) for flip in range(1, groups)]

    count = queries.shape[0]
    piece = (2, feats, count)
    own_out, *sends = call(
        functools.partial(query_kernel, groups, 2 * n_hid * cols),
        (weights, *gather(grad, stats), *all_stats, *quests),
        [jax.ShapeDtypeStruct(piece, f32)] + [jax.ShapeDtypeStruct(piece, bf16)] * 3,
        [pltpu.VMEM(whole, bf16), pltpu.VMEM((2, width, 2 * count), bf16)],
        6 * 2 * 2 * count * width * cols,
        place,
        16,
    )
    arrived = [swap(send, flip) for send, flip in zip(sends, (1, 2, 3))]
    out, grad = call(
        last_kernel, (own_out, *arrived), [jax.ShapeDtypeStruct(piece[1:], bf16)] * 2
    )
    return out.T, grad.T


def silu_slope(pre):
    sigma = jax.nn.sigmoid(pre)
    return sigma * (1.0 + pre * (1.0 - sigma))


def contract_rows(left, right):
    return lax.dot_general(
        left, right, (((0,), (0,)), ((), ())), preferred_element_type=jnp.float32
    )


def contract_cols(left, right):
    return lax.dot_general(
        left, right, (((1,), (1,)), ((), ())), preferred_element_type=jnp.float32
    )


def finish(moved, wsq, msq):
    return (moved * (jnp.sqrt(wsq) / jnp.sqrt(msq + epsilon))[:, None]).astype(jnp.bfloat16)


def general(
    input_keys, input_values, input_lr, gate_weight, up_weight, down_weight, queries, out_grad, n_hid
):
    keys, values = (
        lax.all_gather(input_keys, "hid", axis=1, tiled=True),
        lax.all_gather(input_values, "hid", axis=1, tiled=True),
    )
    w_gate, w_up, w_down = (
        lax.all_gather(gate_weight, "tok", axis=0, tiled=True),
        lax.all_gather(up_weight, "tok", axis=0, tiled=True),
        lax.all_gather(down_weight, "tok", axis=0, tiled=True),
    )
    scaled = (input_lr[:, None] * values.astype(jnp.float32)).astype(jnp.bfloat16)
    key_gate = jnp.dot(keys, w_gate, preferred_element_type=jnp.float32)
    key_up = jnp.dot(keys, w_up, preferred_element_type=jnp.float32)
    gate_act = jax.nn.silu(key_gate)
    key_act = (gate_act * key_up).astype(jnp.bfloat16)
    back = jnp.dot(scaled, w_down, preferred_element_type=jnp.float32)
    d_gate = (-back * key_up * silu_slope(key_gate)).astype(jnp.bfloat16)
    d_up = (-back * gate_act).astype(jnp.bfloat16)
    width = gate_weight.shape[1]
    hidden = width * n_hid
    grads = lax.psum(
        jnp.concatenate(
            [
                contract_rows(keys, d_gate),
                contract_rows(keys, d_up),
                -contract_rows(scaled, key_act),
            ],
            axis=1,
        ),
        "tok",
    )
    olds = (w_gate, w_up, w_down)
    pieces = [grads[:, :width], grads[:, width : 2 * width], grads[:, 2 * width :]]
    weights = [old.astype(jnp.float32) for old in olds]
    renewed = []
    stats = []
    for weight, grad in zip(weights, pieces):
        stats.append(jnp.sum(weight * weight, axis=1))
        stats.append(jnp.sum(weight * grad, axis=1))
        stats.append(jnp.sum(grad * grad, axis=1))
    totals = lax.psum(
        (stats[0], stats[1], stats[2], stats[3], stats[4], stats[5], stats[6], stats[7], stats[8]),
        "hid",
    )
    for index in range(3):
        wsq = totals[3 * index] / hidden
        cross = totals[3 * index + 1] / hidden
        gsq = totals[3 * index + 2] / hidden
        scale = step_ratio * jnp.sqrt(wsq) / jnp.sqrt(gsq + epsilon)
        moved = weights[index] - scale[:, None] * pieces[index]
        msq = wsq - 2.0 * scale * cross + scale * scale * gsq
        renewed.append(finish(moved, wsq, msq))
    new_gate, new_up, new_down = (renewed[0], renewed[1], renewed[2])
    query_rows, grad_rows = (
        lax.all_gather(queries, "hid", axis=1, tiled=True),
        lax.all_gather(out_grad, "hid", axis=1, tiled=True),
    )
    query_gate = jnp.dot(query_rows, new_gate, preferred_element_type=jnp.float32)
    query_up = jnp.dot(query_rows, new_up, preferred_element_type=jnp.float32)
    query_silu = jax.nn.silu(query_gate)
    query_act = (query_silu * query_up).astype(jnp.bfloat16)
    out_part = contract_cols(query_act, new_down)
    query_back = jnp.dot(grad_rows, new_down, preferred_element_type=jnp.float32)
    q_gate_grad = (query_back * query_up * silu_slope(query_gate)).astype(jnp.bfloat16)
    q_up_grad = (query_back * query_silu).astype(jnp.bfloat16)
    grad_part = contract_cols(q_gate_grad, new_gate) + contract_cols(q_up_grad, new_up)
    out_sum, grad_sum = (
        lax.psum_scatter(
            out_part.astype(jnp.bfloat16), "hid", scatter_dimension=1, tiled=True
        ).astype(jnp.float32),
        lax.psum_scatter(
            grad_part.astype(jnp.bfloat16), "hid", scatter_dimension=1, tiled=True
        ).astype(jnp.float32),
    )
    return (out_sum.astype(jnp.bfloat16), grad_sum.astype(jnp.bfloat16))


def solution(mesh):
    n_tok, n_hid = mesh.shape["tok"], mesh.shape["hid"]

    def shards(*args):
        rows, cols = args[3].shape
        toks, count = args[0].shape[0], args[6].shape[0]
        fits = (
            n_hid == 2
            and 2 <= n_tok <= 8
            and n_tok & (n_tok - 1) == 0
            and rows % 16 == 0
            and cols % 256 == 0
            and toks % 256 == 0
            and count % 128 == 0
        )
        if fits:
            return direct(*args, n_tok, n_hid)
        return general(*args, n_hid)

    return jax.shard_map(
        shards,
        mesh=mesh,
        in_specs=(
            P(("scene", "tok"), "hid"),
            P(("scene", "tok"), "hid"),
            P(("scene", "tok")),
            P("tok", "hid"),
            P("tok", "hid"),
            P("tok", "hid"),
            P(("scene", "tok"), "hid"),
            P(("scene", "tok"), "hid"),
        ),
        out_specs=(P(("scene", "tok"), "hid"), P(("scene", "tok"), "hid")),
        check_vma=False,
    )
```

```python
import functools

import jax
import jax.numpy as jnp
from jax import lax
from jax.experimental import pallas as pl
from jax.experimental.pallas import tpu as pltpu
from jax.sharding import PartitionSpec as P

step_ratio = 0.5
epsilon = 1e-06
f32, bf16 = jnp.float32, jnp.bfloat16


def contract(left, right, left_dim, right_dim):
    return lax.dot_general(
        left, right, (((left_dim,), (right_dim,)), ((), ())), preferred_element_type=f32
    )


def gated(gate, up):
    sigma = jax.nn.sigmoid(gate)
    silu = gate * sigma
    slope = sigma * (1.0 + gate * (1.0 - sigma))
    return silu, slope * up, silu * up


def join(full, mine, other, half):
    feats = mine.shape[-2]
    full[:, pl.ds(pl.multiple_of(half * feats, feats), feats), :] = mine[...]
    full[:, pl.ds(pl.multiple_of((1 - half) * feats, feats), feats), :] = other[...]


def add_grads(tokens, weights, grads, fresh):
    total = tokens.shape[2]
    chunk = min(512, total)
    for start in range(0, total, chunk):
        key = tokens[0, :, start : start + chunk]
        val = tokens[1, :, start : start + chunk]
        gate = contract(weights[0], key, 0, 0)
        up = contract(weights[1], key, 0, 0)
        back = contract(weights[2], val, 0, 0)
        silu, slope_up, act = gated(gate, up)
        parts = (
            contract(key, (back * slope_up).astype(bf16), 1, 1),
            contract(key, (back * silu).astype(bf16), 1, 1),
            contract(val, act.astype(bf16), 1, 1),
        )
        for index, part in enumerate(parts):
            if fresh and start == 0:
                grads[index] = part
            else:
                grads[index] += part


def rows_kernel(groups, place, *refs):
    blocks, (weights,) = refs[: 2 * groups], refs[2 * groups :]
    group, side = place[0], place[1]
    for index, block in enumerate(blocks):
        flip, sided = index % groups, (side if index < groups else 1 - side)
        weights[:, rows_of((group ^ flip) * 2 + sided, block.shape[1]), :] = block[...]


def own_kernel(place, mine, other, weights, grads, tokens):
    join(tokens, mine, other, place[2])
    add_grads(tokens, weights, grads, True)


def pair_kernel(groups, place, mine, other, weights, before, *refs):
    outs, (grads, tokens) = refs[:groups], refs[groups:]
    group, half = place[0], place[2]
    grads[...] = before[...]
    join(tokens, mine, other, half)
    add_grads(tokens, weights, grads, False)
    for flip, out in enumerate(outs):
        out[...] = grads[:, rows_of(group ^ flip, out.shape[1]), :].astype(out.dtype)


def rows_of(owner, rows):
    return pl.ds(pl.multiple_of(owner * rows, rows), rows)


def sum_kernel(arrivals, place, weights, own, *refs):
    arrived, (grad_out, stats_out) = refs[:arrivals], refs[arrivals:]
    where = rows_of(place[0], own.shape[1])
    lane = lax.broadcasted_iota(jnp.int32, stats_out.shape, 1)
    stats = jnp.zeros(stats_out.shape, f32)
    for index in range(3):
        grad = own[index]
        for other in arrived:
            grad = grad + other[index].astype(f32)
        grad_out[index] = grad.astype(bf16)
        weight = weights[index, where, :].astype(f32)
        for slot, product in enumerate((weight * weight, weight * grad, grad * grad)):
            row_sum = jnp.sum(product, axis=1, keepdims=True)
            stats = jnp.where(lane == 3 * index + slot, row_sum, stats)
    stats_out[...] = stats


def query_kernel(groups, hidden, place, weights, *refs):
    grads, stats, refs = refs[:groups], refs[groups], refs[groups + 1 :]
    quests, refs = refs[:4], refs[4:]
    own_out, sends, (renewed, query) = refs[0], refs[1:4], refs[4:]
    group, side, half = place[0], place[1], place[2]
    feats, count = quests[0].shape[1:]

    for flip in range(groups):
        where = rows_of(group ^ flip, grads[0].shape[1])
        sums = stats[flip] / hidden
        for index in range(3):
            wsq = sums[:, 3 * index : 3 * index + 1]
            cross = sums[:, 3 * index + 1 : 3 * index + 2]
            gsq = sums[:, 3 * index + 2 : 3 * index + 3]
            scale = step_ratio * jnp.sqrt(wsq) / jnp.sqrt(gsq + epsilon)
            msq = wsq + 2.0 * scale * cross + scale * scale * gsq
            factor = jnp.sqrt(wsq) / jnp.sqrt(msq + epsilon)
            moved = weights[index, where, :].astype(f32) + scale * grads[flip][index].astype(f32)
            renewed[index, where, :] = (moved * factor).astype(bf16)
    for flip in range(4):
        feat = pl.ds(pl.multiple_of((half ^ (flip & 1)) * feats, feats), feats)
        span = pl.ds(pl.multiple_of((side ^ (flip >> 1)) * count, count), count)
        query[:, feat, span] = quests[flip][...]

    gate = contract(renewed[0], query[0], 0, 0)
    up = contract(renewed[1], query[0], 0, 0)
    back = contract(renewed[2], query[1], 0, 0)
    silu, slope_up, act = gated(gate, up)
    out = contract(renewed[2], act.astype(bf16), 1, 0)
    grad = contract(renewed[0], (back * slope_up).astype(bf16), 1, 0) + contract(
        renewed[1], (back * silu).astype(bf16), 1, 0
    )
    for index, whole in enumerate((out, grad)):
        for flip, target in enumerate((own_out, *sends)):
            left = jnp.where((half ^ (flip & 1)) == 0, whole[:feats], whole[feats:])
            piece = jnp.where((side ^ (flip >> 1)) == 0, left[:, :count], left[:, count:])
            target[index] = piece.astype(target.dtype)


def last_kernel(own, first, second, third, out, grad):
    for index, target in enumerate((out, grad)):
        total = own[index] + first[index].astype(f32) + second[index].astype(f32)
        target[...] = (total + third[index].astype(f32)).astype(bf16)


def call(body, operands, outs, scratch=(), flops=0, place=None, mib=4):
    specs = [pl.BlockSpec(memory_space=pltpu.VMEM)] * len(operands)
    if place is not None:
        specs, operands = [pl.BlockSpec(memory_space=pltpu.SMEM)] + specs, (place, *operands)
    moved = sum(4 * leaf.size for leaf in (*operands, *outs))
    return pl.pallas_call(
        body,
        out_shape=list(outs),
        in_specs=specs,
        out_specs=[pl.BlockSpec(memory_space=pltpu.VMEM)] * len(outs),
        scratch_shapes=list(scratch),
        compiler_params=pltpu.CompilerParams(vmem_limit_bytes=mib * 1024 * 1024),
        cost_estimate=pl.CostEstimate(flops=flops, bytes_accessed=moved, transcendentals=0),
    )(*operands)


def direct(
    input_keys, input_values, input_lr, gate_weight, up_weight, down_weight, queries, out_grad,
    n_tok, n_hid,
):
    groups = n_tok // 2
    tok, half = lax.axis_index("tok"), lax.axis_index("hid")
    group, side = tok // 2, tok % 2
    place = jnp.stack([group, side, half]).astype(jnp.int32)
    core, pair, zed = 1, 2, 4

    def swap(array, flip):
        pairs = [(i, i ^ flip) for i in range(n_tok * n_hid)]
        return lax.ppermute(array, ("tok", "hid"), pairs)

    def gather(block, soon=(), late=()):
        held, bit = {0: block}, groups // 2
        while bit > 1:
            held.update({flip | bit: swap(held[flip], zed * bit) for flip in list(held)})
            bit //= 2
        if soon:
            block, _ = lax.optimization_barrier((block, soon))
        near = swap(block, zed)
        if late:
            held, near, _ = lax.optimization_barrier((held, near, late))
        held.update({flip | 1: swap(held[flip], zed) for flip in list(held) if flip})
        held[1] = near
        return [held[flip] for flip in range(groups)]

    stacked = jnp.stack([gate_weight, up_weight, down_weight])
    cols = stacked.shape[2] // 2
    own_w = lax.dynamic_slice_in_dim(stacked, side * cols, cols, 2)
    give_w = lax.dynamic_slice_in_dim(stacked, (1 - side) * cols, cols, 2)
    vals = (input_lr[None, :] * input_values.T.astype(f32)).astype(bf16)
    tokens = jnp.stack([input_keys.T, vals])
    _, feats, toks = tokens.shape
    first = gather(own_w)
    tokens, pair_w, _ = lax.optimization_barrier((tokens, swap(give_w, pair), first[1]))
    second = gather(pair_w)
    pair_tokens = swap(tokens, pair)

    width = n_hid * feats
    rows = width // groups
    whole = (3, width, cols)
    block = (3, rows, cols)
    token_flops = 6 * 2 * toks * width * cols
    joined = pltpu.VMEM((2, width, toks), bf16)
    (weights,) = call(
        functools.partial(rows_kernel, groups),
        (*first, *second),
        (jax.ShapeDtypeStruct(whole, bf16),),
        place=place,
    )
    pair_tokens, weights = lax.optimization_barrier((pair_tokens, weights))
    (grads,) = call(
        own_kernel,
        (tokens, swap(tokens, core), weights),
        (jax.ShapeDtypeStruct(whole, f32),),
        [joined],
        token_flops,
        place,
        16,
    )
    shares = call(
        functools.partial(pair_kernel, groups),
        (pair_tokens, swap(pair_tokens, core), weights, grads),
        [jax.ShapeDtypeStruct(block, bf16 if flip & 1 else f32) for flip in range(groups)],
        [pltpu.VMEM(whole, f32), joined],
        token_flops,
        place,
        16,
    )
    quest, shares = lax.optimization_barrier((jnp.stack([queries.T, out_grad.T]), shares))
    quests = [quest] + [swap(quest, flip) for flip in (1, 2, 3)]
    held, arrived, bit = dict(enumerate(shares)), [], 1
    while bit < groups:
        for flip in sorted((f for f in held if f & bit), reverse=True):
            came = swap(held.pop(flip), zed * bit)
            if flip == bit:
                arrived.append(came)
            else:
                came, quests = lax.optimization_barrier((came, quests))
                other = (held[flip ^ bit].astype(f32) + came.astype(f32)).astype(bf16)
                held, held[flip ^ bit] = lax.optimization_barrier((held, other))
        bit *= 2
    grad, stats = call(
        functools.partial(sum_kernel, len(arrived)),
        (weights, held[0], *arrived),
        (jax.ShapeDtypeStruct(block, bf16), jax.ShapeDtypeStruct((rows, 128), f32)),
        place=place,
    )
    stats = near_stats = stats + swap(stats, core)
    stats = stats + swap(stats, pair)
    all_stats, bit = stats[None], groups // 2
    while bit:
        all_stats = jnp.stack([all_stats, swap(all_stats, zed * bit)], axis=1)
        all_stats = all_stats.reshape(-1, *stats.shape)
        bit //= 2

    count = queries.shape[0]
    piece = (2, feats, count)
    own_out, *sends = call(
        functools.partial(query_kernel, groups, 2 * n_hid * cols),
        (weights, *gather(grad, [near_stats], [stats]), all_stats, *quests),
        [jax.ShapeDtypeStruct(piece, f32)] + [jax.ShapeDtypeStruct(piece, bf16)] * 3,
        [pltpu.VMEM(whole, bf16), pltpu.VMEM((2, width, 2 * count), bf16)],
        6 * 2 * 2 * count * width * cols,
        place,
        16,
    )
    arrived = [swap(send, flip) for send, flip in zip(sends, (1, 2, 3))]
    out, grad = call(
        last_kernel, (own_out, *arrived), [jax.ShapeDtypeStruct(piece[1:], bf16)] * 2
    )
    return out.T, grad.T


def silu_slope(pre):
    sigma = jax.nn.sigmoid(pre)
    return sigma * (1.0 + pre * (1.0 - sigma))


def contract_rows(left, right):
    return lax.dot_general(
        left, right, (((0,), (0,)), ((), ())), preferred_element_type=jnp.float32
    )


def contract_cols(left, right):
    return lax.dot_general(
        left, right, (((1,), (1,)), ((), ())), preferred_element_type=jnp.float32
    )


def finish(moved, wsq, msq):
    return (moved * (jnp.sqrt(wsq) / jnp.sqrt(msq + epsilon))[:, None]).astype(jnp.bfloat16)


def general(
    input_keys, input_values, input_lr, gate_weight, up_weight, down_weight, queries, out_grad, n_hid
):
    keys, values = (
        lax.all_gather(input_keys, "hid", axis=1, tiled=True),
        lax.all_gather(input_values, "hid", axis=1, tiled=True),
    )
    w_gate, w_up, w_down = (
        lax.all_gather(gate_weight, "tok", axis=0, tiled=True),
        lax.all_gather(up_weight, "tok", axis=0, tiled=True),
        lax.all_gather(down_weight, "tok", axis=0, tiled=True),
    )
    scaled = (input_lr[:, None] * values.astype(jnp.float32)).astype(jnp.bfloat16)
    key_gate = jnp.dot(keys, w_gate, preferred_element_type=jnp.float32)
    key_up = jnp.dot(keys, w_up, preferred_element_type=jnp.float32)
    gate_act = jax.nn.silu(key_gate)
    key_act = (gate_act * key_up).astype(jnp.bfloat16)
    back = jnp.dot(scaled, w_down, preferred_element_type=jnp.float32)
    d_gate = (-back * key_up * silu_slope(key_gate)).astype(jnp.bfloat16)
    d_up = (-back * gate_act).astype(jnp.bfloat16)
    width = gate_weight.shape[1]
    hidden = width * n_hid
    grads = lax.psum(
        jnp.concatenate(
            [
                contract_rows(keys, d_gate),
                contract_rows(keys, d_up),
                -contract_rows(scaled, key_act),
            ],
            axis=1,
        ),
        "tok",
    )
    olds = (w_gate, w_up, w_down)
    pieces = [grads[:, :width], grads[:, width : 2 * width], grads[:, 2 * width :]]
    weights = [old.astype(jnp.float32) for old in olds]
    renewed = []
    stats = []
    for weight, grad in zip(weights, pieces):
        stats.append(jnp.sum(weight * weight, axis=1))
        stats.append(jnp.sum(weight * grad, axis=1))
        stats.append(jnp.sum(grad * grad, axis=1))
    totals = lax.psum(
        (stats[0], stats[1], stats[2], stats[3], stats[4], stats[5], stats[6], stats[7], stats[8]),
        "hid",
    )
    for index in range(3):
        wsq = totals[3 * index] / hidden
        cross = totals[3 * index + 1] / hidden
        gsq = totals[3 * index + 2] / hidden
        scale = step_ratio * jnp.sqrt(wsq) / jnp.sqrt(gsq + epsilon)
        moved = weights[index] - scale[:, None] * pieces[index]
        msq = wsq - 2.0 * scale * cross + scale * scale * gsq
        renewed.append(finish(moved, wsq, msq))
    new_gate, new_up, new_down = (renewed[0], renewed[1], renewed[2])
    query_rows, grad_rows = (
        lax.all_gather(queries, "hid", axis=1, tiled=True),
        lax.all_gather(out_grad, "hid", axis=1, tiled=True),
    )
    query_gate = jnp.dot(query_rows, new_gate, preferred_element_type=jnp.float32)
    query_up = jnp.dot(query_rows, new_up, preferred_element_type=jnp.float32)
    query_silu = jax.nn.silu(query_gate)
    query_act = (query_silu * query_up).astype(jnp.bfloat16)
    out_part = contract_cols(query_act, new_down)
    query_back = jnp.dot(grad_rows, new_down, preferred_element_type=jnp.float32)
    q_gate_grad = (query_back * query_up * silu_slope(query_gate)).astype(jnp.bfloat16)
    q_up_grad = (query_back * query_silu).astype(jnp.bfloat16)
    grad_part = contract_cols(q_gate_grad, new_gate) + contract_cols(q_up_grad, new_up)
    out_sum, grad_sum = (
        lax.psum_scatter(
            out_part.astype(jnp.bfloat16), "hid", scatter_dimension=1, tiled=True
        ).astype(jnp.float32),
        lax.psum_scatter(
            grad_part.astype(jnp.bfloat16), "hid", scatter_dimension=1, tiled=True
        ).astype(jnp.float32),
    )
    return (out_sum.astype(jnp.bfloat16), grad_sum.astype(jnp.bfloat16))


def solution(mesh):
    n_tok, n_hid = mesh.shape["tok"], mesh.shape["hid"]

    def shards(*args):
        rows, cols = args[3].shape
        toks, count = args[0].shape[0], args[6].shape[0]
        fits = (
            n_hid == 2
            and 2 <= n_tok <= 8
            and n_tok & (n_tok - 1) == 0
            and rows % 16 == 0
            and cols % 256 == 0
            and toks % 256 == 0
            and count % 128 == 0
        )
        if fits:
            return direct(*args, n_tok, n_hid)
        return general(*args, n_hid)

    return jax.shard_map(
        shards,
        mesh=mesh,
        in_specs=(
            P(("scene", "tok"), "hid"),
            P(("scene", "tok"), "hid"),
            P(("scene", "tok")),
            P("tok", "hid"),
            P("tok", "hid"),
            P("tok", "hid"),
            P(("scene", "tok"), "hid"),
            P(("scene", "tok"), "hid"),
        ),
        out_specs=(P(("scene", "tok"), "hid"), P(("scene", "tok"), "hid")),
        check_vma=False,
    )
```

```python
import functools

import jax
import jax.numpy as jnp
from jax import lax
from jax.experimental import pallas as pl
from jax.experimental.pallas import tpu as pltpu
from jax.sharding import PartitionSpec as P

step_ratio = 0.5
epsilon = 1e-06
f32, bf16 = jnp.float32, jnp.bfloat16


def contract(left, right, left_dim, right_dim):
    return lax.dot_general(
        left, right, (((left_dim,), (right_dim,)), ((), ())), preferred_element_type=f32
    )


def gated(gate, up):
    sigma = jax.nn.sigmoid(gate)
    silu = gate * sigma
    slope = sigma * (1.0 + gate * (1.0 - sigma))
    return silu, slope * up, silu * up


def join(full, mine, other, half):
    feats = mine.shape[-2]
    full[:, pl.ds(pl.multiple_of(half * feats, feats), feats), :] = mine[...]
    full[:, pl.ds(pl.multiple_of((1 - half) * feats, feats), feats), :] = other[...]


def add_grads(tokens, weights, grads, fresh):
    total = tokens.shape[2]
    chunk = min(512, total)
    for start in range(0, total, chunk):
        key = tokens[0, :, start : start + chunk]
        val = tokens[1, :, start : start + chunk]
        gate = contract(weights[0], key, 0, 0)
        up = contract(weights[1], key, 0, 0)
        back = contract(weights[2], val, 0, 0)
        silu, slope_up, act = gated(gate, up)
        parts = (
            contract(key, (back * slope_up).astype(bf16), 1, 1),
            contract(key, (back * silu).astype(bf16), 1, 1),
            contract(val, act.astype(bf16), 1, 1),
        )
        for index, part in enumerate(parts):
            if fresh and start == 0:
                grads[index] = part
            else:
                grads[index] += part


def rows_kernel(groups, place, *refs):
    blocks, (weights,) = refs[: 2 * groups], refs[2 * groups :]
    group, side = place[0], place[1]
    for index, block in enumerate(blocks):
        flip, sided = index % groups, (side if index < groups else 1 - side)
        weights[:, rows_of((group ^ flip) * 2 + sided, block.shape[1]), :] = block[...]


def own_kernel(place, mine, other, weights, grads, tokens):
    join(tokens, mine, other, place[2])
    add_grads(tokens, weights, grads, True)


def pair_kernel(groups, place, mine, other, weights, before, *refs):
    outs, (grads, tokens) = refs[:groups], refs[groups:]
    group, half = place[0], place[2]
    grads[...] = before[...]
    join(tokens, mine, other, half)
    add_grads(tokens, weights, grads, False)
    for flip, out in enumerate(outs):
        out[...] = grads[:, rows_of(group ^ flip, out.shape[1]), :].astype(out.dtype)


def rows_of(owner, rows):
    return pl.ds(pl.multiple_of(owner * rows, rows), rows)


def sum_kernel(arrivals, place, weights, own, *refs):
    arrived, (grad_out, stats_out) = refs[:arrivals], refs[arrivals:]
    where = rows_of(place[0], own.shape[1])
    lane = lax.broadcasted_iota(jnp.int32, stats_out.shape, 1)
    stats = jnp.zeros(stats_out.shape, f32)
    for index in range(3):
        grad = own[index]
        for other in arrived:
            grad = grad + other[index].astype(f32)
        grad_out[index] = grad.astype(bf16)
        weight = weights[index, where, :].astype(f32)
        for slot, product in enumerate((weight * weight, weight * grad, grad * grad)):
            row_sum = jnp.sum(product, axis=1, keepdims=True)
            stats = jnp.where(lane == 3 * index + slot, row_sum, stats)
    stats_out[...] = stats


def answer(renewed, query, quests, half, kept, given):
    mine, other = quests
    feats = mine.shape[1]
    join(query, mine, other, half)
    gate = contract(renewed[0], query[0], 0, 0)
    up = contract(renewed[1], query[0], 0, 0)
    back = contract(renewed[2], query[1], 0, 0)
    silu, slope_up, act = gated(gate, up)
    out = contract(renewed[2], act.astype(bf16), 1, 0)
    grad = contract(renewed[0], (back * slope_up).astype(bf16), 1, 0) + contract(
        renewed[1], (back * silu).astype(bf16), 1, 0
    )
    for index, whole in enumerate((out, grad)):
        first, second = whole[:feats], whole[feats:]
        kept[index] = jnp.where(half == 0, first, second)
        given[index] = jnp.where(half == 0, second, first).astype(bf16)


def renew_kernel(groups, hidden, place, weights, *refs):
    grads, stats, quests, refs = refs[:groups], refs[groups], refs[groups + 1 : groups + 3], refs[groups + 3 :]
    renewed, kept, given, query = refs
    for flip in range(groups):
        where = rows_of(place[0] ^ flip, grads[0].shape[1])
        sums = stats[flip] / hidden
        for index in range(3):
            wsq = sums[:, 3 * index : 3 * index + 1]
            cross = sums[:, 3 * index + 1 : 3 * index + 2]
            gsq = sums[:, 3 * index + 2 : 3 * index + 3]
            scale = step_ratio * jnp.sqrt(wsq) / jnp.sqrt(gsq + epsilon)
            msq = wsq + 2.0 * scale * cross + scale * scale * gsq
            factor = jnp.sqrt(wsq) / jnp.sqrt(msq + epsilon)
            moved = weights[index, where, :].astype(f32) + scale * grads[flip][index].astype(f32)
            renewed[index, where, :] = (moved * factor).astype(bf16)
    answer(renewed, query, quests, place[2], kept, given)


def query_kernel(place, renewed, mine, other, kept, given, query):
    answer(renewed, query, (mine, other), place[2], kept, given)


def last_kernel(kept, core, pair, out, grad):
    for index, target in enumerate((out, grad)):
        target[...] = (kept[index] + core[index].astype(f32) + pair[index].astype(f32)).astype(bf16)


def call(body, operands, outs, scratch=(), flops=0, place=None, mib=4):
    specs = [pl.BlockSpec(memory_space=pltpu.VMEM)] * len(operands)
    if place is not None:
        specs, operands = [pl.BlockSpec(memory_space=pltpu.SMEM)] + specs, (place, *operands)
    moved = sum(4 * leaf.size for leaf in (*operands, *outs))
    return pl.pallas_call(
        body,
        out_shape=list(outs),
        in_specs=specs,
        out_specs=[pl.BlockSpec(memory_space=pltpu.VMEM)] * len(outs),
        scratch_shapes=list(scratch),
        compiler_params=pltpu.CompilerParams(vmem_limit_bytes=mib * 1024 * 1024),
        cost_estimate=pl.CostEstimate(flops=flops, bytes_accessed=moved, transcendentals=0),
    )(*operands)


def direct(
    input_keys, input_values, input_lr, gate_weight, up_weight, down_weight, queries, out_grad,
    n_tok, n_hid,
):
    groups = n_tok // 2
    tok, half = lax.axis_index("tok"), lax.axis_index("hid")
    group, side = tok // 2, tok % 2
    place = jnp.stack([group, side, half]).astype(jnp.int32)
    core, pair, zed = 1, 2, 4

    def swap(array, flip):
        pairs = [(i, i ^ flip) for i in range(n_tok * n_hid)]
        return lax.ppermute(array, ("tok", "hid"), pairs)

    def gather(block, soon=(), late=()):
        held, bit = {0: block}, groups // 2
        while bit > 1:
            held.update({flip | bit: swap(held[flip], zed * bit) for flip in list(held)})
            bit //= 2
        if soon:
            block, _ = lax.optimization_barrier((block, soon))
        near = swap(block, zed)
        if late:
            held, near, _ = lax.optimization_barrier((held, near, late))
        held.update({flip | 1: swap(held[flip], zed) for flip in list(held) if flip})
        held[1] = near
        return [held[flip] for flip in range(groups)]

    stacked = jnp.stack([gate_weight, up_weight, down_weight])
    cols = stacked.shape[2] // 2
    own_w = lax.dynamic_slice_in_dim(stacked, side * cols, cols, 2)
    give_w = lax.dynamic_slice_in_dim(stacked, (1 - side) * cols, cols, 2)
    vals = (input_lr[None, :] * input_values.T.astype(f32)).astype(bf16)
    tokens = jnp.stack([input_keys.T, vals])
    _, feats, toks = tokens.shape
    first = gather(own_w)
    tokens, pair_w = lax.optimization_barrier((tokens, swap(give_w, pair)))
    pair_w, _ = lax.optimization_barrier((pair_w, first[1]))
    second = gather(pair_w)
    pair_tokens = swap(tokens, pair)

    width = n_hid * feats
    rows = width // groups
    whole = (3, width, cols)
    block = (3, rows, cols)
    token_flops = 6 * 2 * toks * width * cols
    joined = pltpu.VMEM((2, width, toks), bf16)
    (weights,) = call(
        functools.partial(rows_kernel, groups),
        (*first, *second),
        (jax.ShapeDtypeStruct(whole, bf16),),
        place=place,
    )
    pair_tokens, weights = lax.optimization_barrier((pair_tokens, weights))
    (grads,) = call(
        own_kernel,
        (tokens, swap(tokens, core), weights),
        (jax.ShapeDtypeStruct(whole, f32),),
        [joined],
        token_flops,
        place,
        16,
    )
    shares = call(
        functools.partial(pair_kernel, groups),
        (pair_tokens, swap(pair_tokens, core), weights, grads),
        [jax.ShapeDtypeStruct(block, bf16 if flip & 1 else f32) for flip in range(groups)],
        [pltpu.VMEM(whole, f32), joined],
        token_flops,
        place,
        16,
    )
    quest, shares = lax.optimization_barrier((jnp.stack([queries.T, out_grad.T]), shares))
    quests = [quest] + [swap(quest, flip) for flip in (1, 2, 3)]
    held, arrived, bit = dict(enumerate(shares)), [], 1
    while bit < groups:
        for flip in sorted((f for f in held if f & bit), reverse=True):
            came = swap(held.pop(flip), zed * bit)
            if flip == bit:
                arrived.append(came)
            else:
                came, quests = lax.optimization_barrier((came, quests))
                other = (held[flip ^ bit].astype(f32) + came.astype(f32)).astype(bf16)
                held, held[flip ^ bit] = lax.optimization_barrier((held, other))
        bit *= 2
    grad, stats = call(
        functools.partial(sum_kernel, len(arrived)),
        (weights, held[0], *arrived),
        (jax.ShapeDtypeStruct(block, bf16), jax.ShapeDtypeStruct((rows, 128), f32)),
        place=place,
    )
    stats = near_stats = stats + swap(stats, core)
    stats = stats + swap(stats, pair)
    all_stats, bit = stats[None], groups // 2
    while bit:
        all_stats = jnp.stack([all_stats, swap(all_stats, zed * bit)], axis=1)
        all_stats = all_stats.reshape(-1, *stats.shape)
        bit //= 2

    count = queries.shape[0]
    piece = (2, feats, count)
    kept_given = [jax.ShapeDtypeStruct(piece, f32), jax.ShapeDtypeStruct(piece, bf16)]
    query = pltpu.VMEM((2, width, count), bf16)
    query_flops = 6 * 2 * count * width * cols
    renewed, kept, given = call(
        functools.partial(renew_kernel, groups, 2 * n_hid * cols),
        (weights, *gather(grad, [near_stats], [stats]), all_stats, *quests[2:]),
        [jax.ShapeDtypeStruct(whole, bf16), *kept_given],
        [query],
        query_flops,
        place,
        16,
    )
    from_core, quests = lax.optimization_barrier((swap(given, core), quests))
    from_pair = swap((kept + from_core.astype(f32)).astype(bf16), pair)
    kept, given = call(
        query_kernel, (renewed, *quests[:2]), kept_given, [query], query_flops, place, 16
    )
    out, grad = call(
        last_kernel,
        (kept, swap(given, core), from_pair),
        [jax.ShapeDtypeStruct(piece[1:], bf16)] * 2,
    )
    return out.T, grad.T


def silu_slope(pre):
    sigma = jax.nn.sigmoid(pre)
    return sigma * (1.0 + pre * (1.0 - sigma))


def contract_rows(left, right):
    return lax.dot_general(
        left, right, (((0,), (0,)), ((), ())), preferred_element_type=jnp.float32
    )


def contract_cols(left, right):
    return lax.dot_general(
        left, right, (((1,), (1,)), ((), ())), preferred_element_type=jnp.float32
    )


def finish(moved, wsq, msq):
    return (moved * (jnp.sqrt(wsq) / jnp.sqrt(msq + epsilon))[:, None]).astype(jnp.bfloat16)


def general(
    input_keys, input_values, input_lr, gate_weight, up_weight, down_weight, queries, out_grad, n_hid
):
    keys, values = (
        lax.all_gather(input_keys, "hid", axis=1, tiled=True),
        lax.all_gather(input_values, "hid", axis=1, tiled=True),
    )
    w_gate, w_up, w_down = (
        lax.all_gather(gate_weight, "tok", axis=0, tiled=True),
        lax.all_gather(up_weight, "tok", axis=0, tiled=True),
        lax.all_gather(down_weight, "tok", axis=0, tiled=True),
    )
    scaled = (input_lr[:, None] * values.astype(jnp.float32)).astype(jnp.bfloat16)
    key_gate = jnp.dot(keys, w_gate, preferred_element_type=jnp.float32)
    key_up = jnp.dot(keys, w_up, preferred_element_type=jnp.float32)
    gate_act = jax.nn.silu(key_gate)
    key_act = (gate_act * key_up).astype(jnp.bfloat16)
    back = jnp.dot(scaled, w_down, preferred_element_type=jnp.float32)
    d_gate = (-back * key_up * silu_slope(key_gate)).astype(jnp.bfloat16)
    d_up = (-back * gate_act).astype(jnp.bfloat16)
    width = gate_weight.shape[1]
    hidden = width * n_hid
    grads = lax.psum(
        jnp.concatenate(
            [
                contract_rows(keys, d_gate),
                contract_rows(keys, d_up),
                -contract_rows(scaled, key_act),
            ],
            axis=1,
        ),
        "tok",
    )
    olds = (w_gate, w_up, w_down)
    pieces = [grads[:, :width], grads[:, width : 2 * width], grads[:, 2 * width :]]
    weights = [old.astype(jnp.float32) for old in olds]
    renewed = []
    stats = []
    for weight, grad in zip(weights, pieces):
        stats.append(jnp.sum(weight * weight, axis=1))
        stats.append(jnp.sum(weight * grad, axis=1))
        stats.append(jnp.sum(grad * grad, axis=1))
    totals = lax.psum(
        (stats[0], stats[1], stats[2], stats[3], stats[4], stats[5], stats[6], stats[7], stats[8]),
        "hid",
    )
    for index in range(3):
        wsq = totals[3 * index] / hidden
        cross = totals[3 * index + 1] / hidden
        gsq = totals[3 * index + 2] / hidden
        scale = step_ratio * jnp.sqrt(wsq) / jnp.sqrt(gsq + epsilon)
        moved = weights[index] - scale[:, None] * pieces[index]
        msq = wsq - 2.0 * scale * cross + scale * scale * gsq
        renewed.append(finish(moved, wsq, msq))
    new_gate, new_up, new_down = (renewed[0], renewed[1], renewed[2])
    query_rows, grad_rows = (
        lax.all_gather(queries, "hid", axis=1, tiled=True),
        lax.all_gather(out_grad, "hid", axis=1, tiled=True),
    )
    query_gate = jnp.dot(query_rows, new_gate, preferred_element_type=jnp.float32)
    query_up = jnp.dot(query_rows, new_up, preferred_element_type=jnp.float32)
    query_silu = jax.nn.silu(query_gate)
    query_act = (query_silu * query_up).astype(jnp.bfloat16)
    out_part = contract_cols(query_act, new_down)
    query_back = jnp.dot(grad_rows, new_down, preferred_element_type=jnp.float32)
    q_gate_grad = (query_back * query_up * silu_slope(query_gate)).astype(jnp.bfloat16)
    q_up_grad = (query_back * query_silu).astype(jnp.bfloat16)
    grad_part = contract_cols(q_gate_grad, new_gate) + contract_cols(q_up_grad, new_up)
    out_sum, grad_sum = (
        lax.psum_scatter(
            out_part.astype(jnp.bfloat16), "hid", scatter_dimension=1, tiled=True
        ).astype(jnp.float32),
        lax.psum_scatter(
            grad_part.astype(jnp.bfloat16), "hid", scatter_dimension=1, tiled=True
        ).astype(jnp.float32),
    )
    return (out_sum.astype(jnp.bfloat16), grad_sum.astype(jnp.bfloat16))


def solution(mesh):
    n_tok, n_hid = mesh.shape["tok"], mesh.shape["hid"]

    def shards(*args):
        rows, cols = args[3].shape
        toks, count = args[0].shape[0], args[6].shape[0]
        fits = (
            n_hid == 2
            and 2 <= n_tok <= 8
            and n_tok & (n_tok - 1) == 0
            and rows % 16 == 0
            and cols % 256 == 0
            and toks % 256 == 0
            and count % 128 == 0
        )
        if fits:
            return direct(*args, n_tok, n_hid)
        return general(*args, n_hid)

    return jax.shard_map(
        shards,
        mesh=mesh,
        in_specs=(
            P(("scene", "tok"), "hid"),
            P(("scene", "tok"), "hid"),
            P(("scene", "tok")),
            P("tok", "hid"),
            P("tok", "hid"),
            P("tok", "hid"),
            P(("scene", "tok"), "hid"),
            P(("scene", "tok"), "hid"),
        ),
        out_specs=(P(("scene", "tok"), "hid"), P(("scene", "tok"), "hid")),
        check_vma=False,
    )
```

```python
import functools

import jax
import jax.numpy as jnp
from jax import lax
from jax.experimental import pallas as pl
from jax.experimental.pallas import tpu as pltpu
from jax.sharding import PartitionSpec as P

step_ratio = 0.5
epsilon = 1e-06
f32, bf16 = jnp.float32, jnp.bfloat16


def contract(left, right, left_dim, right_dim):
    return lax.dot_general(
        left, right, (((left_dim,), (right_dim,)), ((), ())), preferred_element_type=f32
    )


def gated(gate, up):
    sigma = jax.nn.sigmoid(gate)
    silu = gate * sigma
    slope = sigma * (1.0 + gate * (1.0 - sigma))
    return silu, slope * up, silu * up


def join(full, mine, other, half):
    feats = mine.shape[-2]
    full[:, pl.ds(pl.multiple_of(half * feats, feats), feats), :] = mine[...]
    full[:, pl.ds(pl.multiple_of((1 - half) * feats, feats), feats), :] = other[...]


def gradients(tokens, weights, deltas, acts):
    cols, total = acts.shape
    chunk = min(512, total)
    for start in range(0, total, chunk):
        span = slice(start, start + chunk)
        gate = contract(weights[0], tokens[0, :, span], 0, 0)
        up = contract(weights[1], tokens[0, :, span], 0, 0)
        back = contract(weights[2], tokens[1, :, span], 0, 0)
        silu, slope_up, act = gated(gate, up)
        deltas[:cols, span] = (back * slope_up).astype(bf16)
        deltas[cols:, span] = (back * silu).astype(bf16)
        acts[:, span] = act.astype(bf16)
    both = contract(tokens[0], deltas[...], 1, 1)
    return both[:, :cols], both[:, cols:], contract(tokens[1], acts[...], 1, 1)


def rows_kernel(groups, place, *refs):
    blocks, (weights,) = refs[: 2 * groups], refs[2 * groups :]
    group, side = place[0], place[1]
    for index, block in enumerate(blocks):
        flip, sided = index % groups, (side if index < groups else 1 - side)
        weights[:, rows_of((group ^ flip) * 2 + sided, block.shape[1]), :] = block[...]


def own_kernel(place, mine, other, weights, grads, tokens, deltas, acts):
    join(tokens, mine, other, place[2])
    for index, grad in enumerate(gradients(tokens, weights, deltas, acts)):
        grads[index] = grad


def pair_kernel(groups, place, mine, other, weights, before, *refs):
    outs, (grads, tokens, deltas, acts) = refs[:groups], refs[groups:]
    join(tokens, mine, other, place[2])
    for index, grad in enumerate(gradients(tokens, weights, deltas, acts)):
        grads[index] = before[index] + grad
    for flip, out in enumerate(outs):
        out[...] = grads[:, rows_of(place[0] ^ flip, out.shape[1]), :].astype(out.dtype)


def rows_of(owner, rows):
    return pl.ds(pl.multiple_of(owner * rows, rows), rows)


def sum_kernel(arrivals, place, weights, own, *refs):
    arrived, (grad_out, stats_out) = refs[:arrivals], refs[arrivals:]
    where = rows_of(place[0], own.shape[1])
    lane = lax.broadcasted_iota(jnp.int32, stats_out.shape, 1)
    stats = jnp.zeros(stats_out.shape, f32)
    for index in range(3):
        grad = own[index]
        for other in arrived:
            grad = grad + other[index].astype(f32)
        grad_out[index] = grad.astype(bf16)
        weight = weights[index, where, :].astype(f32)
        for slot, product in enumerate((weight * weight, weight * grad, grad * grad)):
            row_sum = jnp.sum(product, axis=1, keepdims=True)
            stats = jnp.where(lane == 3 * slot + index, row_sum, stats)
    stats_out[...] = stats


def factor_kernel(hidden, here, there, factors):
    wsq = (here[...] + there[...]) / hidden
    lane = lax.broadcasted_iota(jnp.int32, wsq.shape, 1)
    lanes = wsq.shape[1]
    cross, gsq = pltpu.roll(wsq, lanes - 3, 1), pltpu.roll(wsq, lanes - 6, 1)
    scale = step_ratio * jnp.sqrt(wsq) / jnp.sqrt(gsq + epsilon)
    msq = wsq + 2.0 * scale * cross + scale * scale * gsq
    factor = jnp.sqrt(wsq) / jnp.sqrt(msq + epsilon)
    factors[...] = jnp.where(lane < 3, factor, pltpu.roll(scale * factor, 3, 1))


def answer(renewed, query, quests, half, kept, given):
    mine, other = quests
    feats = mine.shape[1]
    join(query, mine, other, half)
    gate = contract(renewed[0], query[0], 0, 0)
    up = contract(renewed[1], query[0], 0, 0)
    back = contract(renewed[2], query[1], 0, 0)
    silu, slope_up, act = gated(gate, up)
    out = contract(renewed[2], act.astype(bf16), 1, 0)
    grad = contract(renewed[0], (back * slope_up).astype(bf16), 1, 0) + contract(
        renewed[1], (back * silu).astype(bf16), 1, 0
    )
    for index, whole in enumerate((out, grad)):
        first, second = whole[:feats], whole[feats:]
        kept[index] = jnp.where(half == 0, first, second)
        given[index] = jnp.where(half == 0, second, first).astype(bf16)


def renew_kernel(groups, place, weights, *refs):
    grads, factors, quests, refs = refs[:groups], refs[groups], refs[groups + 1 : groups + 3], refs[groups + 3 :]
    renewed, kept, given, query = refs
    for flip in range(groups):
        where = rows_of(place[0] ^ flip, grads[0].shape[1])
        for index in range(3):
            old = weights[index, where, :].astype(f32) * factors[flip, :, index : index + 1]
            step = grads[flip][index].astype(f32) * factors[flip, :, 3 + index : 4 + index]
            renewed[index, where, :] = (old + step).astype(bf16)
    answer(renewed, query, quests, place[2], kept, given)


def query_kernel(place, renewed, mine, other, kept, given, query):
    answer(renewed, query, (mine, other), place[2], kept, given)


def last_kernel(kept, core, pair, out, grad):
    for index, target in enumerate((out, grad)):
        target[...] = (kept[index] + core[index].astype(f32) + pair[index].astype(f32)).astype(bf16)


def call(body, operands, outs, scratch=(), flops=0, place=None, mib=4):
    specs = [pl.BlockSpec(memory_space=pltpu.VMEM)] * len(operands)
    if place is not None:
        specs, operands = [pl.BlockSpec(memory_space=pltpu.SMEM)] + specs, (place, *operands)
    moved = sum(4 * leaf.size for leaf in (*operands, *outs))
    return pl.pallas_call(
        body,
        out_shape=list(outs),
        in_specs=specs,
        out_specs=[pl.BlockSpec(memory_space=pltpu.VMEM)] * len(outs),
        scratch_shapes=list(scratch),
        compiler_params=pltpu.CompilerParams(vmem_limit_bytes=mib * 1024 * 1024),
        cost_estimate=pl.CostEstimate(flops=flops, bytes_accessed=moved, transcendentals=0),
    )(*operands)


def direct(
    input_keys, input_values, input_lr, gate_weight, up_weight, down_weight, queries, out_grad,
    n_tok, n_hid,
):
    groups = n_tok // 2
    tok, half = lax.axis_index("tok"), lax.axis_index("hid")
    group, side = tok // 2, tok % 2
    place = jnp.stack([group, side, half]).astype(jnp.int32)
    core, pair, zed = 1, 2, 4

    def swap(array, flip):
        pairs = [(i, i ^ flip) for i in range(n_tok * n_hid)]
        return lax.ppermute(array, ("tok", "hid"), pairs)

    def gather(block, soon=(), late=()):
        held, bit = {0: block}, groups // 2
        while bit > 1:
            held.update({flip | bit: swap(held[flip], zed * bit) for flip in list(held)})
            bit //= 2
        if soon:
            block, _ = lax.optimization_barrier((block, soon))
        near = swap(block, zed)
        if late:
            held, near, _ = lax.optimization_barrier((held, near, late))
        held.update({flip | 1: swap(held[flip], zed) for flip in list(held) if flip})
        held[1] = near
        return [held[flip] for flip in range(groups)]

    stacked = jnp.stack([gate_weight, up_weight, down_weight])
    cols = stacked.shape[2] // 2
    own_w = lax.dynamic_slice_in_dim(stacked, side * cols, cols, 2)
    give_w = lax.dynamic_slice_in_dim(stacked, (1 - side) * cols, cols, 2)
    vals = (input_lr[None, :] * input_values.T.astype(f32)).astype(bf16)
    tokens = jnp.stack([input_keys.T, vals])
    _, feats, toks = tokens.shape
    first = gather(own_w)
    tokens, pair_w = lax.optimization_barrier((tokens, swap(give_w, pair)))
    second = gather(pair_w)
    pair_tokens = swap(tokens, pair)

    width = n_hid * feats
    rows = width // groups
    whole = (3, width, cols)
    block = (3, rows, cols)
    token_flops = 6 * 2 * toks * width * cols
    joined = [
        pltpu.VMEM((2, width, toks), bf16),
        pltpu.VMEM((2 * cols, toks), bf16),
        pltpu.VMEM((cols, toks), bf16),
    ]
    (weights,) = call(
        functools.partial(rows_kernel, groups),
        (*first, *second),
        (jax.ShapeDtypeStruct(whole, bf16),),
        place=place,
    )
    pair_tokens, weights = lax.optimization_barrier((pair_tokens, weights))
    (grads,) = call(
        own_kernel,
        (tokens, swap(tokens, core), weights),
        (jax.ShapeDtypeStruct(whole, f32),),
        joined,
        token_flops,
        place,
        16,
    )
    shares = call(
        functools.partial(pair_kernel, groups),
        (pair_tokens, swap(pair_tokens, core), weights, grads),
        [jax.ShapeDtypeStruct(block, bf16 if flip & 1 else f32) for flip in range(groups)],
        [pltpu.VMEM(whole, f32), *joined],
        token_flops,
        place,
        16,
    )
    quest, shares = lax.optimization_barrier((jnp.stack([queries.T, out_grad.T]), shares))
    quests = [quest] + [swap(quest, flip) for flip in (1, 2, 3)]
    held, arrived, bit = dict(enumerate(shares)), [], 1
    while bit < groups:
        for flip in sorted((f for f in held if f & bit), reverse=True):
            came = swap(held.pop(flip), zed * bit)
            if flip == bit:
                arrived.append(came)
            else:
                came, quests = lax.optimization_barrier((came, quests))
                other = (held[flip ^ bit].astype(f32) + came.astype(f32)).astype(bf16)
                held, held[flip ^ bit] = lax.optimization_barrier((held, other))
        bit *= 2
    grad, stats = call(
        functools.partial(sum_kernel, len(arrived)),
        (weights, held[0], *arrived),
        (jax.ShapeDtypeStruct(block, bf16), jax.ShapeDtypeStruct((rows, 128), f32)),
        place=place,
    )
    stats = stats + swap(stats, core)
    (factors,) = call(
        functools.partial(factor_kernel, 2 * n_hid * cols),
        (stats, swap(stats, pair)),
        (jax.ShapeDtypeStruct(stats.shape, f32),),
    )
    all_factors, bit = factors[None], groups // 2
    while bit:
        all_factors = jnp.stack([all_factors, swap(all_factors, zed * bit)], axis=1)
        all_factors = all_factors.reshape(-1, *stats.shape)
        bit //= 2

    count = queries.shape[0]
    piece = (2, feats, count)
    kept_given = [jax.ShapeDtypeStruct(piece, f32), jax.ShapeDtypeStruct(piece, bf16)]
    query = pltpu.VMEM((2, width, count), bf16)
    query_flops = 6 * 2 * count * width * cols
    renewed, kept, given = call(
        functools.partial(renew_kernel, groups),
        (weights, *gather(grad, [stats], [factors]), all_factors, *quests[2:]),
        [jax.ShapeDtypeStruct(whole, bf16), *kept_given],
        [query],
        query_flops,
        place,
        16,
    )
    from_core, quests = lax.optimization_barrier((swap(given, core), quests))
    from_pair = swap((kept + from_core.astype(f32)).astype(bf16), pair)
    kept, given = call(
        query_kernel, (renewed, *quests[:2]), kept_given, [query], query_flops, place, 16
    )
    out, grad = call(
        last_kernel,
        (kept, swap(given, core), from_pair),
        [jax.ShapeDtypeStruct(piece[1:], bf16)] * 2,
    )
    return out.T, grad.T


def silu_slope(pre):
    sigma = jax.nn.sigmoid(pre)
    return sigma * (1.0 + pre * (1.0 - sigma))


def contract_rows(left, right):
    return lax.dot_general(
        left, right, (((0,), (0,)), ((), ())), preferred_element_type=jnp.float32
    )


def contract_cols(left, right):
    return lax.dot_general(
        left, right, (((1,), (1,)), ((), ())), preferred_element_type=jnp.float32
    )


def finish(moved, wsq, msq):
    return (moved * (jnp.sqrt(wsq) / jnp.sqrt(msq + epsilon))[:, None]).astype(jnp.bfloat16)


def general(
    input_keys, input_values, input_lr, gate_weight, up_weight, down_weight, queries, out_grad, n_hid
):
    keys, values = (
        lax.all_gather(input_keys, "hid", axis=1, tiled=True),
        lax.all_gather(input_values, "hid", axis=1, tiled=True),
    )
    w_gate, w_up, w_down = (
        lax.all_gather(gate_weight, "tok", axis=0, tiled=True),
        lax.all_gather(up_weight, "tok", axis=0, tiled=True),
        lax.all_gather(down_weight, "tok", axis=0, tiled=True),
    )
    scaled = (input_lr[:, None] * values.astype(jnp.float32)).astype(jnp.bfloat16)
    key_gate = jnp.dot(keys, w_gate, preferred_element_type=jnp.float32)
    key_up = jnp.dot(keys, w_up, preferred_element_type=jnp.float32)
    gate_act = jax.nn.silu(key_gate)
    key_act = (gate_act * key_up).astype(jnp.bfloat16)
    back = jnp.dot(scaled, w_down, preferred_element_type=jnp.float32)
    d_gate = (-back * key_up * silu_slope(key_gate)).astype(jnp.bfloat16)
    d_up = (-back * gate_act).astype(jnp.bfloat16)
    width = gate_weight.shape[1]
    hidden = width * n_hid
    grads = lax.psum(
        jnp.concatenate(
            [
                contract_rows(keys, d_gate),
                contract_rows(keys, d_up),
                -contract_rows(scaled, key_act),
            ],
            axis=1,
        ),
        "tok",
    )
    olds = (w_gate, w_up, w_down)
    pieces = [grads[:, :width], grads[:, width : 2 * width], grads[:, 2 * width :]]
    weights = [old.astype(jnp.float32) for old in olds]
    renewed = []
    stats = []
    for weight, grad in zip(weights, pieces):
        stats.append(jnp.sum(weight * weight, axis=1))
        stats.append(jnp.sum(weight * grad, axis=1))
        stats.append(jnp.sum(grad * grad, axis=1))
    totals = lax.psum(
        (stats[0], stats[1], stats[2], stats[3], stats[4], stats[5], stats[6], stats[7], stats[8]),
        "hid",
    )
    for index in range(3):
        wsq = totals[3 * index] / hidden
        cross = totals[3 * index + 1] / hidden
        gsq = totals[3 * index + 2] / hidden
        scale = step_ratio * jnp.sqrt(wsq) / jnp.sqrt(gsq + epsilon)
        moved = weights[index] - scale[:, None] * pieces[index]
        msq = wsq - 2.0 * scale * cross + scale * scale * gsq
        renewed.append(finish(moved, wsq, msq))
    new_gate, new_up, new_down = (renewed[0], renewed[1], renewed[2])
    query_rows, grad_rows = (
        lax.all_gather(queries, "hid", axis=1, tiled=True),
        lax.all_gather(out_grad, "hid", axis=1, tiled=True),
    )
    query_gate = jnp.dot(query_rows, new_gate, preferred_element_type=jnp.float32)
    query_up = jnp.dot(query_rows, new_up, preferred_element_type=jnp.float32)
    query_silu = jax.nn.silu(query_gate)
    query_act = (query_silu * query_up).astype(jnp.bfloat16)
    out_part = contract_cols(query_act, new_down)
    query_back = jnp.dot(grad_rows, new_down, preferred_element_type=jnp.float32)
    q_gate_grad = (query_back * query_up * silu_slope(query_gate)).astype(jnp.bfloat16)
    q_up_grad = (query_back * query_silu).astype(jnp.bfloat16)
    grad_part = contract_cols(q_gate_grad, new_gate) + contract_cols(q_up_grad, new_up)
    out_sum, grad_sum = (
        lax.psum_scatter(
            out_part.astype(jnp.bfloat16), "hid", scatter_dimension=1, tiled=True
        ).astype(jnp.float32),
        lax.psum_scatter(
            grad_part.astype(jnp.bfloat16), "hid", scatter_dimension=1, tiled=True
        ).astype(jnp.float32),
    )
    return (out_sum.astype(jnp.bfloat16), grad_sum.astype(jnp.bfloat16))


def solution(mesh):
    n_tok, n_hid = mesh.shape["tok"], mesh.shape["hid"]

    def shards(*args):
        rows, cols = args[3].shape
        toks, count = args[0].shape[0], args[6].shape[0]
        fits = (
            n_hid == 2
            and 2 <= n_tok <= 8
            and n_tok & (n_tok - 1) == 0
            and rows % 16 == 0
            and cols % 256 == 0
            and toks % 256 == 0
            and count % 128 == 0
        )
        if fits:
            return direct(*args, n_tok, n_hid)
        return general(*args, n_hid)

    return jax.shard_map(
        shards,
        mesh=mesh,
        in_specs=(
            P(("scene", "tok"), "hid"),
            P(("scene", "tok"), "hid"),
            P(("scene", "tok")),
            P("tok", "hid"),
            P("tok", "hid"),
            P("tok", "hid"),
            P(("scene", "tok"), "hid"),
            P(("scene", "tok"), "hid"),
        ),
        out_specs=(P(("scene", "tok"), "hid"), P(("scene", "tok"), "hid")),
        check_vma=False,
    )
```

```python
import functools

import jax
import jax.numpy as jnp
from jax import lax
from jax.experimental import pallas as pl
from jax.experimental.pallas import tpu as pltpu
from jax.sharding import PartitionSpec as P

step_ratio = 0.5
epsilon = 1e-06
f32, bf16 = jnp.float32, jnp.bfloat16
LANES = 128


def contract(left, right, left_dim, right_dim):
    return lax.dot_general(
        left, right, (((left_dim,), (right_dim,)), ((), ())), preferred_element_type=f32
    )


def gated(gate, up):
    sigma = jax.nn.sigmoid(gate)
    silu = gate * sigma
    slope = sigma * (1.0 + gate * (1.0 - sigma))
    return silu, slope * up, silu * up


def join(full, mine, other, half):
    feats = mine.shape[-2]
    full[:, pl.ds(pl.multiple_of(half * feats, feats), feats), :] = mine[...]
    full[:, pl.ds(pl.multiple_of((1 - half) * feats, feats), feats), :] = other[...]


def gradients(tokens, weights, deltas, acts):
    cols, total = acts.shape
    chunk = min(512, total)
    for start in range(0, total, chunk):
        span = slice(start, start + chunk)
        gate = contract(weights[0], tokens[0, :, span], 0, 0)
        up = contract(weights[1], tokens[0, :, span], 0, 0)
        back = contract(weights[2], tokens[1, :, span], 0, 0)
        silu, slope_up, act = gated(gate, up)
        deltas[:cols, span] = (back * slope_up).astype(bf16)
        deltas[cols:, span] = (back * silu).astype(bf16)
        acts[:, span] = act.astype(bf16)
    both = contract(tokens[0], deltas[...], 1, 1)
    return both[:, :cols], both[:, cols:], contract(tokens[1], acts[...], 1, 1)


def rows_kernel(groups, place, *refs):
    blocks, (weights,) = refs[: 2 * groups], refs[2 * groups :]
    group, side = place[0], place[1]
    for index, block in enumerate(blocks):
        flip, sided = index % groups, (side if index < groups else 1 - side)
        weights[:, rows_of((group ^ flip) * 2 + sided, block.shape[1]), :] = block[...]


def own_kernel(place, mine, other, weights, grads, tokens, deltas, acts):
    join(tokens, mine, other, place[2])
    for index, grad in enumerate(gradients(tokens, weights, deltas, acts)):
        grads[index] = grad


def pair_kernel(parts, place, mine, other, weights, before, *refs):
    outs, (grads, tokens, deltas, acts) = refs[: 2 * parts], refs[2 * parts :]
    join(tokens, mine, other, place[2])
    for index, grad in enumerate(gradients(tokens, weights, deltas, acts)):
        grads[index] = before[index] + grad
    for index, out in enumerate(outs):
        part, given = index % parts, index // parts
        for spot in range(2):
            where = rows_of((place[0] ^ ((3 * spot) ^ given)) * parts + part, out.shape[2])
            out[spot] = grads[:, where, :].astype(out.dtype)


def rows_of(owner, rows):
    return pl.ds(pl.multiple_of(owner * rows, rows), rows)


def sum_kernel(parts, part, place, weights, kept, came, crossed, grad_out, stats_out):
    rows = kept.shape[2]
    lane = lax.broadcasted_iota(jnp.int32, (rows, LANES), 1)
    both = []
    for spot in range(2):
        where = rows_of((place[0] ^ (3 * spot)) * parts + part, rows)
        stats = jnp.zeros((rows, LANES), f32)
        for index in range(3):
            near = kept[spot, index] + came[spot, index].astype(f32)
            grad = near + crossed[1 - spot, index].astype(f32)
            grad_out[spot, index] = grad.astype(bf16)
            weight = weights[index, where, :].astype(f32)
            for slot, product in enumerate((weight * weight, weight * grad, grad * grad)):
                row_sum = jnp.sum(product, axis=1, keepdims=True)
                stats = jnp.where(lane == 8 * slot + index, row_sum, stats)
        both.append(stats)
    stats_out[...] = jnp.concatenate(both, axis=0).T[: stats_out.shape[0]]


def factor_kernel(hidden, here, there, factors):
    sums = (here[...] + there[...]) / hidden
    wsq, cross, gsq = sums[:, :8], sums[:, 8:16], sums[:, 16:]
    scale = step_ratio * jnp.sqrt(wsq) / jnp.sqrt(gsq + epsilon)
    msq = wsq + 2.0 * scale * cross + scale * scale * gsq
    factor = jnp.sqrt(wsq) / jnp.sqrt(msq + epsilon)
    factors[:, :8] = factor
    factors[:, 8:] = scale * factor


def answer(renewed, query, quests, half, kept, given):
    mine, other = quests
    feats = mine.shape[1]
    join(query, mine, other, half)
    gate = contract(renewed[0], query[0], 0, 0)
    up = contract(renewed[1], query[0], 0, 0)
    back = contract(renewed[2], query[1], 0, 0)
    silu, slope_up, act = gated(gate, up)
    out = contract(renewed[2], act.astype(bf16), 1, 0)
    grad = contract(renewed[0], (back * slope_up).astype(bf16), 1, 0) + contract(
        renewed[1], (back * silu).astype(bf16), 1, 0
    )
    for index, whole in enumerate((out, grad)):
        first, second = whole[:feats], whole[feats:]
        kept[index] = jnp.where(half == 0, first, second)
        given[index] = jnp.where(half == 0, second, first).astype(bf16)


def renew_kernel(parts, place, weights, *refs):
    grads, factors, quests, refs = refs[: 2 * parts], refs[2 * parts : 2 * parts + 2], refs[-6:-4], refs[-4:]
    renewed, kept, given, query = refs
    for spot in range(2):
        for near in range(2):
            for part in range(parts):
                grad = grads[near * parts + part]
                rows = grad.shape[2]
                where = rows_of((place[0] ^ ((3 * spot) ^ near)) * parts + part, rows)
                scales = factors[near][part].T[spot * rows : (spot + 1) * rows]
                for index in range(3):
                    old = weights[index, where, :].astype(f32) * scales[:, index : index + 1]
                    step = grad[spot, index].astype(f32) * scales[:, 8 + index : 9 + index]
                    renewed[index, where, :] = (old + step).astype(bf16)
    answer(renewed, query, quests, place[2], kept, given)


def query_kernel(place, renewed, mine, other, kept, given, query):
    answer(renewed, query, (mine, other), place[2], kept, given)


def last_kernel(kept, core, pair, out, grad):
    for index, target in enumerate((out, grad)):
        target[...] = (kept[index] + core[index].astype(f32) + pair[index].astype(f32)).astype(bf16)


def call(body, operands, outs, scratch=(), flops=0, place=None, mib=4):
    specs = [pl.BlockSpec(memory_space=pltpu.VMEM)] * len(operands)
    if place is not None:
        specs, operands = [pl.BlockSpec(memory_space=pltpu.SMEM)] + specs, (place, *operands)
    moved = sum(4 * leaf.size for leaf in (*operands, *outs))
    return pl.pallas_call(
        body,
        out_shape=list(outs),
        in_specs=specs,
        out_specs=[pl.BlockSpec(memory_space=pltpu.VMEM)] * len(outs),
        scratch_shapes=list(scratch),
        compiler_params=pltpu.CompilerParams(vmem_limit_bytes=mib * 1024 * 1024),
        cost_estimate=pl.CostEstimate(flops=flops, bytes_accessed=moved, transcendentals=0),
    )(*operands)


def direct(
    input_keys, input_values, input_lr, gate_weight, up_weight, down_weight, queries, out_grad,
    n_tok, n_hid,
):
    groups = n_tok // 2
    tok, half = lax.axis_index("tok"), lax.axis_index("hid")
    group, side = tok // 2, tok % 2
    place = jnp.stack([group, side, half]).astype(jnp.int32)
    core, pair, zed = 1, 2, 4

    def swap(array, flip):
        pairs = [(i, i ^ flip) for i in range(n_tok * n_hid)]
        return lax.ppermute(array, ("tok", "hid"), pairs)

    def gather(block):
        near, across = swap(block, zed), swap(block, 2 * zed)
        return [block, near, across, swap(across, zed)]

    stacked = jnp.stack([gate_weight, up_weight, down_weight])
    cols = stacked.shape[2] // 2
    own_w = lax.dynamic_slice_in_dim(stacked, side * cols, cols, 2)
    give_w = lax.dynamic_slice_in_dim(stacked, (1 - side) * cols, cols, 2)
    vals = (input_lr[None, :] * input_values.T.astype(f32)).astype(bf16)
    tokens = jnp.stack([input_keys.T, vals])
    _, feats, toks = tokens.shape
    first = gather(own_w)
    tokens, pair_w = lax.optimization_barrier((tokens, swap(give_w, pair)))
    second = gather(pair_w)
    pair_tokens = swap(tokens, pair)

    width = n_hid * feats
    rows = width // groups
    whole = (3, width, cols)
    block = (3, rows, cols)
    token_flops = 6 * 2 * toks * width * cols
    joined = [
        pltpu.VMEM((2, width, toks), bf16),
        pltpu.VMEM((2 * cols, toks), bf16),
        pltpu.VMEM((cols, toks), bf16),
    ]
    (weights,) = call(
        functools.partial(rows_kernel, groups),
        (*first, *second),
        (jax.ShapeDtypeStruct(whole, bf16),),
        place=place,
    )
    pair_tokens, weights = lax.optimization_barrier((pair_tokens, weights))
    (grads,) = call(
        own_kernel,
        (tokens, swap(tokens, core), weights),
        (jax.ShapeDtypeStruct(whole, f32),),
        joined,
        token_flops,
        place,
        16,
    )
    parts = 2
    block = (2, 3, rows // parts, cols)
    kept_given = [jax.ShapeDtypeStruct(block, f32)] * parts + [jax.ShapeDtypeStruct(block, bf16)] * parts
    shares = call(
        functools.partial(pair_kernel, parts),
        (pair_tokens, swap(pair_tokens, core), weights, grads),
        kept_given,
        [pltpu.VMEM(whole, f32), *joined],
        token_flops,
        place,
        16,
    )
    quest, shares = lax.optimization_barrier((jnp.stack([queries.T, out_grad.T]), shares))
    quests = [quest] + [swap(quest, flip) for flip in (1, 2, 3)]
    kept, came = shares[:parts], [swap(share, zed) for share in shares[parts:]]
    came[0], quests = lax.optimization_barrier((came[0], quests))
    crossed = [swap((k + c.astype(f32)).astype(bf16), 3 * zed) for k, c in zip(kept, came)]
    sums, stats = zip(
        *(
            call(
                functools.partial(sum_kernel, parts, part),
                (weights, kept[part], came[part], crossed[part]),
                (
                    jax.ShapeDtypeStruct(block, bf16),
                    jax.ShapeDtypeStruct((24, 2 * rows // parts), f32),
                ),
                place=place,
            )
            for part in range(parts)
        )
    )
    backs = [swap(part, zed) for part in sums]
    stats = jnp.stack(stats)
    there, backs[0] = lax.optimization_barrier((swap(stats, core), backs[0]))
    stats = stats + there
    (factors,) = call(
        functools.partial(factor_kernel, 2 * n_hid * cols),
        (stats, swap(stats, pair)),
        (jax.ShapeDtypeStruct((parts, 16, 2 * rows // parts), f32),),
    )

    count = queries.shape[0]
    piece = (2, feats, count)
    kept_given = [jax.ShapeDtypeStruct(piece, f32), jax.ShapeDtypeStruct(piece, bf16)]
    query = pltpu.VMEM((2, width, count), bf16)
    query_flops = 6 * 2 * count * width * cols
    renewed, kept, given = call(
        functools.partial(renew_kernel, parts),
        (weights, *sums, *backs, factors, swap(factors, zed), *quests[2:]),
        [jax.ShapeDtypeStruct(whole, bf16), *kept_given],
        [query],
        query_flops,
        place,
        16,
    )
    from_core, quests = lax.optimization_barrier((swap(given, core), quests))
    from_pair = swap((kept + from_core.astype(f32)).astype(bf16), pair)
    kept, given = call(
        query_kernel, (renewed, *quests[:2]), kept_given, [query], query_flops, place, 16
    )
    out, grad = call(
        last_kernel,
        (kept, swap(given, core), from_pair),
        [jax.ShapeDtypeStruct(piece[1:], bf16)] * 2,
    )
    return out.T, grad.T


def silu_slope(pre):
    sigma = jax.nn.sigmoid(pre)
    return sigma * (1.0 + pre * (1.0 - sigma))


def contract_rows(left, right):
    return lax.dot_general(
        left, right, (((0,), (0,)), ((), ())), preferred_element_type=jnp.float32
    )


def contract_cols(left, right):
    return lax.dot_general(
        left, right, (((1,), (1,)), ((), ())), preferred_element_type=jnp.float32
    )


def finish(moved, wsq, msq):
    return (moved * (jnp.sqrt(wsq) / jnp.sqrt(msq + epsilon))[:, None]).astype(jnp.bfloat16)


def general(
    input_keys, input_values, input_lr, gate_weight, up_weight, down_weight, queries, out_grad, n_hid
):
    keys, values = (
        lax.all_gather(input_keys, "hid", axis=1, tiled=True),
        lax.all_gather(input_values, "hid", axis=1, tiled=True),
    )
    w_gate, w_up, w_down = (
        lax.all_gather(gate_weight, "tok", axis=0, tiled=True),
        lax.all_gather(up_weight, "tok", axis=0, tiled=True),
        lax.all_gather(down_weight, "tok", axis=0, tiled=True),
    )
    scaled = (input_lr[:, None] * values.astype(jnp.float32)).astype(jnp.bfloat16)
    key_gate = jnp.dot(keys, w_gate, preferred_element_type=jnp.float32)
    key_up = jnp.dot(keys, w_up, preferred_element_type=jnp.float32)
    gate_act = jax.nn.silu(key_gate)
    key_act = (gate_act * key_up).astype(jnp.bfloat16)
    back = jnp.dot(scaled, w_down, preferred_element_type=jnp.float32)
    d_gate = (-back * key_up * silu_slope(key_gate)).astype(jnp.bfloat16)
    d_up = (-back * gate_act).astype(jnp.bfloat16)
    width = gate_weight.shape[1]
    hidden = width * n_hid
    grads = lax.psum(
        jnp.concatenate(
            [
                contract_rows(keys, d_gate),
                contract_rows(keys, d_up),
                -contract_rows(scaled, key_act),
            ],
            axis=1,
        ),
        "tok",
    )
    olds = (w_gate, w_up, w_down)
    pieces = [grads[:, :width], grads[:, width : 2 * width], grads[:, 2 * width :]]
    weights = [old.astype(jnp.float32) for old in olds]
    renewed = []
    stats = []
    for weight, grad in zip(weights, pieces):
        stats.append(jnp.sum(weight * weight, axis=1))
        stats.append(jnp.sum(weight * grad, axis=1))
        stats.append(jnp.sum(grad * grad, axis=1))
    totals = lax.psum(
        (stats[0], stats[1], stats[2], stats[3], stats[4], stats[5], stats[6], stats[7], stats[8]),
        "hid",
    )
    for index in range(3):
        wsq = totals[3 * index] / hidden
        cross = totals[3 * index + 1] / hidden
        gsq = totals[3 * index + 2] / hidden
        scale = step_ratio * jnp.sqrt(wsq) / jnp.sqrt(gsq + epsilon)
        moved = weights[index] - scale[:, None] * pieces[index]
        msq = wsq - 2.0 * scale * cross + scale * scale * gsq
        renewed.append(finish(moved, wsq, msq))
    new_gate, new_up, new_down = (renewed[0], renewed[1], renewed[2])
    query_rows, grad_rows = (
        lax.all_gather(queries, "hid", axis=1, tiled=True),
        lax.all_gather(out_grad, "hid", axis=1, tiled=True),
    )
    query_gate = jnp.dot(query_rows, new_gate, preferred_element_type=jnp.float32)
    query_up = jnp.dot(query_rows, new_up, preferred_element_type=jnp.float32)
    query_silu = jax.nn.silu(query_gate)
    query_act = (query_silu * query_up).astype(jnp.bfloat16)
    out_part = contract_cols(query_act, new_down)
    query_back = jnp.dot(grad_rows, new_down, preferred_element_type=jnp.float32)
    q_gate_grad = (query_back * query_up * silu_slope(query_gate)).astype(jnp.bfloat16)
    q_up_grad = (query_back * query_silu).astype(jnp.bfloat16)
    grad_part = contract_cols(q_gate_grad, new_gate) + contract_cols(q_up_grad, new_up)
    out_sum, grad_sum = (
        lax.psum_scatter(
            out_part.astype(jnp.bfloat16), "hid", scatter_dimension=1, tiled=True
        ).astype(jnp.float32),
        lax.psum_scatter(
            grad_part.astype(jnp.bfloat16), "hid", scatter_dimension=1, tiled=True
        ).astype(jnp.float32),
    )
    return (out_sum.astype(jnp.bfloat16), grad_sum.astype(jnp.bfloat16))


def solution(mesh):
    n_tok, n_hid = mesh.shape["tok"], mesh.shape["hid"]

    def shards(*args):
        rows, cols = args[3].shape
        toks, count = args[0].shape[0], args[6].shape[0]
        fits = (
            n_hid == 2
            and n_tok == 8
            and rows % 16 == 0
            and cols % 256 == 0
            and toks % 256 == 0
            and count % 128 == 0
        )
        if fits:
            return direct(*args, n_tok, n_hid)
        return general(*args, n_hid)

    return jax.shard_map(
        shards,
        mesh=mesh,
        in_specs=(
            P(("scene", "tok"), "hid"),
            P(("scene", "tok"), "hid"),
            P(("scene", "tok")),
            P("tok", "hid"),
            P("tok", "hid"),
            P("tok", "hid"),
            P(("scene", "tok"), "hid"),
            P(("scene", "tok"), "hid"),
        ),
        out_specs=(P(("scene", "tok"), "hid"), P(("scene", "tok"), "hid")),
        check_vma=False,
    )
```

```python
import functools

import jax
import jax.numpy as jnp
from jax import lax
from jax.experimental import pallas as pl
from jax.experimental.pallas import tpu as pltpu
from jax.sharding import PartitionSpec as P

step_ratio = 0.5
epsilon = 1e-06
f32, bf16 = jnp.float32, jnp.bfloat16
LANES = 128


def contract(left, right, left_dim, right_dim):
    return lax.dot_general(
        left, right, (((left_dim,), (right_dim,)), ((), ())), preferred_element_type=f32
    )


def gated(gate, up):
    sigma = jax.nn.sigmoid(gate)
    silu = gate * sigma
    slope = sigma * (1.0 + gate * (1.0 - sigma))
    return silu, slope * up, silu * up


def join(full, mine, other, half):
    feats = mine.shape[-2]
    full[:, pl.ds(pl.multiple_of(half * feats, feats), feats), :] = mine[...]
    full[:, pl.ds(pl.multiple_of((1 - half) * feats, feats), feats), :] = other[...]


def gradients(tokens, weights, deltas, acts):
    cols, total = acts.shape
    chunk = min(512, total)
    for start in range(0, total, chunk):
        span = slice(start, start + chunk)
        gate = contract(weights[0], tokens[0, :, span], 0, 0)
        up = contract(weights[1], tokens[0, :, span], 0, 0)
        back = contract(weights[2], tokens[1, :, span], 0, 0)
        silu, slope_up, act = gated(gate, up)
        deltas[:cols, span] = (back * slope_up).astype(bf16)
        deltas[cols:, span] = (back * silu).astype(bf16)
        acts[:, span] = act.astype(bf16)
    both = contract(tokens[0], deltas[...], 1, 1)
    return both[:, :cols], both[:, cols:], contract(tokens[1], acts[...], 1, 1)


def rows_kernel(groups, place, *refs):
    blocks, (weights,) = refs[: 2 * groups], refs[2 * groups :]
    group, side = place[0], place[1]
    for index, block in enumerate(blocks):
        flip, sided = index % groups, (side if index < groups else 1 - side)
        weights[:, rows_of((group ^ flip) * 2 + sided, block.shape[1]), :] = block[...]


def own_kernel(place, mine, other, weights, grads, tokens, deltas, acts):
    join(tokens, mine, other, place[2])
    for index, grad in enumerate(gradients(tokens, weights, deltas, acts)):
        grads[index] = grad


def pair_kernel(parts, place, mine, other, weights, before, *refs):
    outs, (grads, tokens, deltas, acts) = refs[: 2 * parts], refs[2 * parts :]
    join(tokens, mine, other, place[2])
    for index, grad in enumerate(gradients(tokens, weights, deltas, acts)):
        grads[index] = before[index] + grad
    for index, out in enumerate(outs):
        part, given = index % parts, index // parts
        for spot in range(2):
            where = rows_of((place[0] ^ ((3 * spot) ^ given)) * parts + part, out.shape[2])
            out[spot] = grads[:, where, :].astype(out.dtype)


def rows_of(owner, rows):
    return pl.ds(pl.multiple_of(owner * rows, rows), rows)


def sum_kernel(parts, part, place, weights, kept, came, crossed, grad_out, stats_out):
    rows = kept.shape[2]
    lane = lax.broadcasted_iota(jnp.int32, (rows, LANES), 1)
    both = []
    for spot in range(2):
        where = rows_of((place[0] ^ (3 * spot)) * parts + part, rows)
        stats = jnp.zeros((rows, LANES), f32)
        for index in range(3):
            near = kept[spot, index] + came[spot, index].astype(f32)
            grad = near + crossed[1 - spot, index].astype(f32)
            grad_out[spot, index] = grad.astype(bf16)
            weight = weights[index, where, :].astype(f32)
            for slot, product in enumerate((weight * weight, weight * grad, grad * grad)):
                row_sum = jnp.sum(product, axis=1, keepdims=True)
                stats = jnp.where(lane == 8 * slot + index, row_sum, stats)
        both.append(stats)
    stats_out[...] = jnp.concatenate(both, axis=0).T[: stats_out.shape[0]]


def factor_kernel(hidden, here, there, factors):
    sums = (here[...] + there[...]) / hidden
    wsq, cross, gsq = sums[:, :8], sums[:, 8:16], sums[:, 16:]
    scale = step_ratio * jnp.sqrt(wsq) / jnp.sqrt(gsq + epsilon)
    msq = wsq + 2.0 * scale * cross + scale * scale * gsq
    factor = jnp.sqrt(wsq) / jnp.sqrt(msq + epsilon)
    factors[:, :8] = factor
    factors[:, 8:] = scale * factor


def answer(renewed, query, quests, half, kept, given):
    mine, other = quests
    feats = mine.shape[1]
    join(query, mine, other, half)
    gate = contract(renewed[0], query[0], 0, 0)
    up = contract(renewed[1], query[0], 0, 0)
    back = contract(renewed[2], query[1], 0, 0)
    silu, slope_up, act = gated(gate, up)
    out = contract(renewed[2], act.astype(bf16), 1, 0)
    grad = contract(renewed[0], (back * slope_up).astype(bf16), 1, 0) + contract(
        renewed[1], (back * silu).astype(bf16), 1, 0
    )
    for index, whole in enumerate((out, grad)):
        first, second = whole[:feats], whole[feats:]
        kept[index] = jnp.where(half == 0, first, second)
        given[index] = jnp.where(half == 0, second, first).astype(bf16)


def renew_kernel(parts, place, weights, *refs):
    grads, factors, quests, refs = refs[: 2 * parts], refs[2 * parts : 2 * parts + 2], refs[-6:-4], refs[-4:]
    renewed, kept, given, query = refs
    for spot in range(2):
        for near in range(2):
            for part in range(parts):
                grad = grads[near * parts + part]
                rows = grad.shape[2]
                where = rows_of((place[0] ^ ((3 * spot) ^ near)) * parts + part, rows)
                scales = factors[near][part].T[spot * rows : (spot + 1) * rows]
                for index in range(3):
                    old = weights[index, where, :].astype(f32) * scales[:, index : index + 1]
                    step = grad[spot, index].astype(f32) * scales[:, 8 + index : 9 + index]
                    renewed[index, where, :] = (old + step).astype(bf16)
    answer(renewed, query, quests, place[2], kept, given)


def query_kernel(place, renewed, mine, other, kept, given, query):
    answer(renewed, query, (mine, other), place[2], kept, given)


def last_kernel(kept, core, pair, out, grad):
    for index, target in enumerate((out, grad)):
        target[...] = (kept[index] + core[index].astype(f32) + pair[index].astype(f32)).astype(bf16)


def call(body, operands, outs, scratch=(), flops=0, place=None, mib=4):
    specs = [pl.BlockSpec(memory_space=pltpu.VMEM)] * len(operands)
    if place is not None:
        specs, operands = [pl.BlockSpec(memory_space=pltpu.SMEM)] + specs, (place, *operands)
    moved = sum(4 * leaf.size for leaf in (*operands, *outs))
    return pl.pallas_call(
        body,
        out_shape=list(outs),
        in_specs=specs,
        out_specs=[pl.BlockSpec(memory_space=pltpu.VMEM)] * len(outs),
        scratch_shapes=list(scratch),
        compiler_params=pltpu.CompilerParams(vmem_limit_bytes=mib * 1024 * 1024),
        cost_estimate=pl.CostEstimate(flops=flops, bytes_accessed=moved, transcendentals=0),
    )(*operands)


def direct(
    input_keys, input_values, input_lr, gate_weight, up_weight, down_weight, queries, out_grad,
    n_tok, n_hid,
):
    groups = n_tok // 2
    tok, half = lax.axis_index("tok"), lax.axis_index("hid")
    group, side = tok // 2, tok % 2
    place = jnp.stack([group, side, half]).astype(jnp.int32)
    core, pair, zed = 1, 2, 4

    def swap(array, flip):
        pairs = [(i, i ^ flip) for i in range(n_tok * n_hid)]
        return lax.ppermute(array, ("tok", "hid"), pairs)

    def gather(block):
        near, across = swap(block, zed), swap(block, 2 * zed)
        return [block, near, across, swap(across, zed)]

    stacked = jnp.stack([gate_weight, up_weight, down_weight])
    cols = stacked.shape[2] // 2
    own_w = lax.dynamic_slice_in_dim(stacked, side * cols, cols, 2)
    give_w = lax.dynamic_slice_in_dim(stacked, (1 - side) * cols, cols, 2)
    vals = (input_lr[None, :] * input_values.T.astype(f32)).astype(bf16)
    tokens = jnp.stack([input_keys.T, vals])
    _, feats, toks = tokens.shape
    first = gather(own_w)
    tokens, pair_w = lax.optimization_barrier((tokens, swap(give_w, pair)))
    second = gather(pair_w)
    pair_tokens = swap(tokens, pair)

    width = n_hid * feats
    rows = width // groups
    whole = (3, width, cols)
    block = (3, rows, cols)
    token_flops = 6 * 2 * toks * width * cols
    joined = [
        pltpu.VMEM((2, width, toks), bf16),
        pltpu.VMEM((2 * cols, toks), bf16),
        pltpu.VMEM((cols, toks), bf16),
    ]
    (weights,) = call(
        functools.partial(rows_kernel, groups),
        (*first, *second),
        (jax.ShapeDtypeStruct(whole, bf16),),
        place=place,
    )
    pair_tokens, weights = lax.optimization_barrier((pair_tokens, weights))
    (grads,) = call(
        own_kernel,
        (tokens, swap(tokens, core), weights),
        (jax.ShapeDtypeStruct(whole, f32),),
        joined,
        token_flops,
        place,
        16,
    )
    parts = 2
    block = (2, 3, rows // parts, cols)
    kept_given = [jax.ShapeDtypeStruct(block, f32)] * parts + [jax.ShapeDtypeStruct(block, bf16)] * parts
    shares = call(
        functools.partial(pair_kernel, parts),
        (pair_tokens, swap(pair_tokens, core), weights, grads),
        kept_given,
        [pltpu.VMEM(whole, f32), *joined],
        token_flops,
        place,
        16,
    )
    quest, shares = lax.optimization_barrier((jnp.stack([queries.T, out_grad.T]), shares))
    quests = [quest] + [swap(quest, flip) for flip in (1, 2, 3)]
    kept, came = shares[:parts], [swap(share, zed) for share in shares[parts:]]
    came[0], quests = lax.optimization_barrier((came[0], quests))
    crossed = [swap((k + c.astype(f32)).astype(bf16), 3 * zed) for k, c in zip(kept, came)]
    sums, stats = zip(
        *(
            call(
                functools.partial(sum_kernel, parts, part),
                (weights, kept[part], came[part], crossed[part]),
                (
                    jax.ShapeDtypeStruct(block, bf16),
                    jax.ShapeDtypeStruct((24, 2 * rows // parts), f32),
                ),
                place=place,
            )
            for part in range(parts)
        )
    )
    backs = [swap(part, zed) for part in sums]
    stats = jnp.stack(stats)
    there, backs[0] = lax.optimization_barrier((swap(stats, core), backs[0]))
    stats = stats + there
    factors = [
        call(
            functools.partial(factor_kernel, 2 * n_hid * cols),
            (here, there),
            (jax.ShapeDtypeStruct((parts, 16, 2 * rows // parts), f32),),
        )[0]
        for here, there in (
            (stats, swap(stats, pair)),
            (swap(stats, zed), swap(stats, zed + pair)),
        )
    ]

    count = queries.shape[0]
    piece = (2, feats, count)
    kept_given = [jax.ShapeDtypeStruct(piece, f32), jax.ShapeDtypeStruct(piece, bf16)]
    query = pltpu.VMEM((2, width, count), bf16)
    query_flops = 6 * 2 * count * width * cols
    renewed, kept, given = call(
        functools.partial(renew_kernel, parts),
        (weights, *sums, *backs, *factors, *quests[2:]),
        [jax.ShapeDtypeStruct(whole, bf16), *kept_given],
        [query],
        query_flops,
        place,
        16,
    )
    from_core, quests = lax.optimization_barrier((swap(given, core), quests))
    from_pair = swap((kept + from_core.astype(f32)).astype(bf16), pair)
    kept, given = call(
        query_kernel, (renewed, *quests[:2]), kept_given, [query], query_flops, place, 16
    )
    out, grad = call(
        last_kernel,
        (kept, swap(given, core), from_pair),
        [jax.ShapeDtypeStruct(piece[1:], bf16)] * 2,
    )
    return out.T, grad.T


def silu_slope(pre):
    sigma = jax.nn.sigmoid(pre)
    return sigma * (1.0 + pre * (1.0 - sigma))


def contract_rows(left, right):
    return lax.dot_general(
        left, right, (((0,), (0,)), ((), ())), preferred_element_type=jnp.float32
    )


def contract_cols(left, right):
    return lax.dot_general(
        left, right, (((1,), (1,)), ((), ())), preferred_element_type=jnp.float32
    )


def finish(moved, wsq, msq):
    return (moved * (jnp.sqrt(wsq) / jnp.sqrt(msq + epsilon))[:, None]).astype(jnp.bfloat16)


def general(
    input_keys, input_values, input_lr, gate_weight, up_weight, down_weight, queries, out_grad, n_hid
):
    keys, values = (
        lax.all_gather(input_keys, "hid", axis=1, tiled=True),
        lax.all_gather(input_values, "hid", axis=1, tiled=True),
    )
    w_gate, w_up, w_down = (
        lax.all_gather(gate_weight, "tok", axis=0, tiled=True),
        lax.all_gather(up_weight, "tok", axis=0, tiled=True),
        lax.all_gather(down_weight, "tok", axis=0, tiled=True),
    )
    scaled = (input_lr[:, None] * values.astype(jnp.float32)).astype(jnp.bfloat16)
    key_gate = jnp.dot(keys, w_gate, preferred_element_type=jnp.float32)
    key_up = jnp.dot(keys, w_up, preferred_element_type=jnp.float32)
    gate_act = jax.nn.silu(key_gate)
    key_act = (gate_act * key_up).astype(jnp.bfloat16)
    back = jnp.dot(scaled, w_down, preferred_element_type=jnp.float32)
    d_gate = (-back * key_up * silu_slope(key_gate)).astype(jnp.bfloat16)
    d_up = (-back * gate_act).astype(jnp.bfloat16)
    width = gate_weight.shape[1]
    hidden = width * n_hid
    grads = lax.psum(
        jnp.concatenate(
            [
                contract_rows(keys, d_gate),
                contract_rows(keys, d_up),
                -contract_rows(scaled, key_act),
            ],
            axis=1,
        ),
        "tok",
    )
    olds = (w_gate, w_up, w_down)
    pieces = [grads[:, :width], grads[:, width : 2 * width], grads[:, 2 * width :]]
    weights = [old.astype(jnp.float32) for old in olds]
    renewed = []
    stats = []
    for weight, grad in zip(weights, pieces):
        stats.append(jnp.sum(weight * weight, axis=1))
        stats.append(jnp.sum(weight * grad, axis=1))
        stats.append(jnp.sum(grad * grad, axis=1))
    totals = lax.psum(
        (stats[0], stats[1], stats[2], stats[3], stats[4], stats[5], stats[6], stats[7], stats[8]),
        "hid",
    )
    for index in range(3):
        wsq = totals[3 * index] / hidden
        cross = totals[3 * index + 1] / hidden
        gsq = totals[3 * index + 2] / hidden
        scale = step_ratio * jnp.sqrt(wsq) / jnp.sqrt(gsq + epsilon)
        moved = weights[index] - scale[:, None] * pieces[index]
        msq = wsq - 2.0 * scale * cross + scale * scale * gsq
        renewed.append(finish(moved, wsq, msq))
    new_gate, new_up, new_down = (renewed[0], renewed[1], renewed[2])
    query_rows, grad_rows = (
        lax.all_gather(queries, "hid", axis=1, tiled=True),
        lax.all_gather(out_grad, "hid", axis=1, tiled=True),
    )
    query_gate = jnp.dot(query_rows, new_gate, preferred_element_type=jnp.float32)
    query_up = jnp.dot(query_rows, new_up, preferred_element_type=jnp.float32)
    query_silu = jax.nn.silu(query_gate)
    query_act = (query_silu * query_up).astype(jnp.bfloat16)
    out_part = contract_cols(query_act, new_down)
    query_back = jnp.dot(grad_rows, new_down, preferred_element_type=jnp.float32)
    q_gate_grad = (query_back * query_up * silu_slope(query_gate)).astype(jnp.bfloat16)
    q_up_grad = (query_back * query_silu).astype(jnp.bfloat16)
    grad_part = contract_cols(q_gate_grad, new_gate) + contract_cols(q_up_grad, new_up)
    out_sum, grad_sum = (
        lax.psum_scatter(
            out_part.astype(jnp.bfloat16), "hid", scatter_dimension=1, tiled=True
        ).astype(jnp.float32),
        lax.psum_scatter(
            grad_part.astype(jnp.bfloat16), "hid", scatter_dimension=1, tiled=True
        ).astype(jnp.float32),
    )
    return (out_sum.astype(jnp.bfloat16), grad_sum.astype(jnp.bfloat16))


def solution(mesh):
    n_tok, n_hid = mesh.shape["tok"], mesh.shape["hid"]

    def shards(*args):
        rows, cols = args[3].shape
        toks, count = args[0].shape[0], args[6].shape[0]
        fits = (
            n_hid == 2
            and n_tok == 8
            and rows % 16 == 0
            and cols % 256 == 0
            and toks % 256 == 0
            and count % 128 == 0
        )
        if fits:
            return direct(*args, n_tok, n_hid)
        return general(*args, n_hid)

    return jax.shard_map(
        shards,
        mesh=mesh,
        in_specs=(
            P(("scene", "tok"), "hid"),
            P(("scene", "tok"), "hid"),
            P(("scene", "tok")),
            P("tok", "hid"),
            P("tok", "hid"),
            P("tok", "hid"),
            P(("scene", "tok"), "hid"),
            P(("scene", "tok"), "hid"),
        ),
        out_specs=(P(("scene", "tok"), "hid"), P(("scene", "tok"), "hid")),
        check_vma=False,
    )
```

```python
import functools

import jax
import jax.numpy as jnp
from jax import lax
from jax.experimental import pallas as pl
from jax.experimental.pallas import tpu as pltpu
from jax.sharding import PartitionSpec as P

step_ratio = 0.5
epsilon = 1e-06
f32, bf16 = jnp.float32, jnp.bfloat16
LANES = 128


def contract(left, right, left_dim, right_dim):
    return lax.dot_general(
        left, right, (((left_dim,), (right_dim,)), ((), ())), preferred_element_type=f32
    )


def gated(gate, up):
    sigma = jax.nn.sigmoid(gate)
    silu = gate * sigma
    slope = sigma * (1.0 + gate * (1.0 - sigma))
    return silu, slope * up, silu * up


def join(full, mine, other, half):
    feats = mine.shape[-2]
    full[:, pl.ds(pl.multiple_of(half * feats, feats), feats), :] = mine[...]
    full[:, pl.ds(pl.multiple_of((1 - half) * feats, feats), feats), :] = other[...]


def backward(tokens, weights, deltas, acts):
    cols, total = acts.shape
    chunk = min(512, total)
    for start in range(0, total, chunk):
        span = slice(start, start + chunk)
        gate = contract(weights[0], tokens[0, :, span], 0, 0)
        up = contract(weights[1], tokens[0, :, span], 0, 0)
        back = contract(weights[2], tokens[1, :, span], 0, 0)
        silu, slope_up, act = gated(gate, up)
        deltas[:cols, span] = (back * slope_up).astype(bf16)
        deltas[cols:, span] = (back * silu).astype(bf16)
        acts[:, span] = act.astype(bf16)


def gradients(tokens, deltas, acts):
    cols = acts.shape[0]
    both = contract(tokens[0], deltas[...], 1, 1)
    return both[:, :cols], both[:, cols:], contract(tokens[1], acts[...], 1, 1)


def rows_kernel(groups, place, *refs):
    blocks, (weights,) = refs[: 2 * groups], refs[2 * groups :]
    group, side = place[0], place[1]
    for index, block in enumerate(blocks):
        flip, sided = index % groups, (side if index < groups else 1 - side)
        weights[:, rows_of((group ^ flip) * 2 + sided, block.shape[1]), :] = block[...]


def own_kernel(place, mine, other, weights, grads, tokens, deltas, acts):
    join(tokens, mine, other, place[2])
    backward(tokens, weights, deltas, acts)
    for index, grad in enumerate(gradients(tokens, deltas, acts)):
        grads[index] = grad


def owners_kernel(given, place, tokens, deltas, acts, before, *refs):
    outs, picked = refs[:-1], refs[-1]
    size = picked.shape[1] // 2
    owners = [rows_of(place[0] ^ (3 * spot) ^ given, size) for spot in range(2)]
    for spot, where in enumerate(owners):
        picked[:, spot * size : (spot + 1) * size, :] = tokens[:, where, :]
    short = size // len(outs)
    for index, grad in enumerate(gradients(picked, deltas, acts)):
        for spot, where in enumerate(owners):
            total = before[index, where, :] + grad[spot * size : (spot + 1) * size]
            for part, out in enumerate(outs):
                out[spot, index] = total[part * short : (part + 1) * short].astype(out.dtype)


def pair_kernel(place, mine, other, weights, before, *refs):
    outs, (tokens, deltas, acts, picked) = refs[:-4], refs[-4:]
    join(tokens, mine, other, place[2])
    backward(tokens, weights, deltas, acts)
    owners_kernel(1, place, tokens, deltas, acts, before, *outs, picked)


def rows_of(owner, rows):
    return pl.ds(pl.multiple_of(owner * rows, rows), rows)


def sum_kernel(parts, part, place, weights, kept, came, crossed, grad_out, stats_out):
    rows = kept.shape[2]
    lane = lax.broadcasted_iota(jnp.int32, (rows, LANES), 1)
    both = []
    for spot in range(2):
        where = rows_of((place[0] ^ (3 * spot)) * parts + part, rows)
        stats = jnp.zeros((rows, LANES), f32)
        for index in range(3):
            near = kept[spot, index] + came[spot, index].astype(f32)
            grad = near + crossed[1 - spot, index].astype(f32)
            grad_out[spot, index] = grad.astype(bf16)
            weight = weights[index, where, :].astype(f32)
            for slot, product in enumerate((weight * weight, weight * grad, grad * grad)):
                row_sum = jnp.sum(product, axis=1, keepdims=True)
                stats = jnp.where(lane == 8 * slot + index, row_sum, stats)
        both.append(stats)
    stats_out[...] = jnp.concatenate(both, axis=0).T[: stats_out.shape[0]]


def factor_kernel(hidden, here, there, factors):
    sums = (here[...] + there[...]) / hidden
    wsq, cross, gsq = sums[:, :8], sums[:, 8:16], sums[:, 16:]
    scale = step_ratio * jnp.sqrt(wsq) / jnp.sqrt(gsq + epsilon)
    msq = wsq + 2.0 * scale * cross + scale * scale * gsq
    factor = jnp.sqrt(wsq) / jnp.sqrt(msq + epsilon)
    factors[:, :8] = factor
    factors[:, 8:] = scale * factor


def answer(renewed, query, quests, half, kept, given):
    mine, other = quests
    feats = mine.shape[1]
    join(query, mine, other, half)
    gate = contract(renewed[0], query[0], 0, 0)
    up = contract(renewed[1], query[0], 0, 0)
    back = contract(renewed[2], query[1], 0, 0)
    silu, slope_up, act = gated(gate, up)
    out = contract(renewed[2], act.astype(bf16), 1, 0)
    grad = contract(renewed[0], (back * slope_up).astype(bf16), 1, 0) + contract(
        renewed[1], (back * silu).astype(bf16), 1, 0
    )
    for index, whole in enumerate((out, grad)):
        first, second = whole[:feats], whole[feats:]
        kept[index] = jnp.where(half == 0, first, second)
        given[index] = jnp.where(half == 0, second, first).astype(bf16)


def renew_kernel(parts, place, weights, *refs):
    grads, factors, quests, refs = refs[: 2 * parts], refs[2 * parts : 2 * parts + 2], refs[-6:-4], refs[-4:]
    renewed, kept, given, query = refs
    for spot in range(2):
        for near in range(2):
            for part in range(parts):
                grad = grads[near * parts + part]
                rows = grad.shape[2]
                where = rows_of((place[0] ^ ((3 * spot) ^ near)) * parts + part, rows)
                scales = factors[near][part].T[spot * rows : (spot + 1) * rows]
                for index in range(3):
                    old = weights[index, where, :].astype(f32) * scales[:, index : index + 1]
                    step = grad[spot, index].astype(f32) * scales[:, 8 + index : 9 + index]
                    renewed[index, where, :] = (old + step).astype(bf16)
    answer(renewed, query, quests, place[2], kept, given)


def query_kernel(place, renewed, mine, other, kept, given, query):
    answer(renewed, query, (mine, other), place[2], kept, given)


def last_kernel(kept, core, pair, out, grad):
    for index, target in enumerate((out, grad)):
        target[...] = (kept[index] + core[index].astype(f32) + pair[index].astype(f32)).astype(bf16)


def call(body, operands, outs, scratch=(), flops=0, place=None, mib=4):
    specs = [pl.BlockSpec(memory_space=pltpu.VMEM)] * len(operands)
    if place is not None:
        specs, operands = [pl.BlockSpec(memory_space=pltpu.SMEM)] + specs, (place, *operands)
    moved = sum(4 * leaf.size for leaf in (*operands, *outs))
    return pl.pallas_call(
        body,
        out_shape=list(outs),
        in_specs=specs,
        out_specs=[pl.BlockSpec(memory_space=pltpu.VMEM)] * len(outs),
        scratch_shapes=list(scratch),
        compiler_params=pltpu.CompilerParams(vmem_limit_bytes=mib * 1024 * 1024),
        cost_estimate=pl.CostEstimate(flops=flops, bytes_accessed=moved, transcendentals=0),
    )(*operands)


def direct(
    input_keys, input_values, input_lr, gate_weight, up_weight, down_weight, queries, out_grad,
    n_tok, n_hid,
):
    groups = n_tok // 2
    tok, half = lax.axis_index("tok"), lax.axis_index("hid")
    group, side = tok // 2, tok % 2
    place = jnp.stack([group, side, half]).astype(jnp.int32)
    core, pair, zed = 1, 2, 4

    def swap(array, flip):
        pairs = [(i, i ^ flip) for i in range(n_tok * n_hid)]
        return lax.ppermute(array, ("tok", "hid"), pairs)

    def gather(block):
        near, across = swap(block, zed), swap(block, 2 * zed)
        return [block, near, across, swap(across, zed)]

    stacked = jnp.stack([gate_weight, up_weight, down_weight])
    cols = stacked.shape[2] // 2
    own_w = lax.dynamic_slice_in_dim(stacked, side * cols, cols, 2)
    give_w = lax.dynamic_slice_in_dim(stacked, (1 - side) * cols, cols, 2)
    vals = (input_lr[None, :] * input_values.T.astype(f32)).astype(bf16)
    tokens = jnp.stack([input_keys.T, vals])
    _, feats, toks = tokens.shape
    first = gather(own_w)
    tokens, pair_w = lax.optimization_barrier((tokens, swap(give_w, pair)))
    second = gather(pair_w)
    pair_tokens = swap(tokens, pair)

    width = n_hid * feats
    rows = width // groups
    whole = (3, width, cols)
    block = (3, rows, cols)
    token_flops = 6 * 2 * toks * width * cols
    joined = [
        pltpu.VMEM((2, width, toks), bf16),
        pltpu.VMEM((2 * cols, toks), bf16),
        pltpu.VMEM((cols, toks), bf16),
    ]
    (weights,) = call(
        functools.partial(rows_kernel, groups),
        (*first, *second),
        (jax.ShapeDtypeStruct(whole, bf16),),
        place=place,
    )
    pair_tokens, weights = lax.optimization_barrier((pair_tokens, weights))
    (grads,) = call(
        own_kernel,
        (tokens, swap(tokens, core), weights),
        (jax.ShapeDtypeStruct(whole, f32),),
        joined,
        token_flops,
        place,
        16,
    )
    parts = 2
    block = (2, 3, rows // parts, cols)
    picked = pltpu.VMEM((2, 2 * rows, toks), bf16)
    *given, pair_tokens, deltas, acts = call(
        pair_kernel,
        (pair_tokens, swap(pair_tokens, core), weights, grads),
        [jax.ShapeDtypeStruct(block, bf16)] * parts
        + [jax.ShapeDtypeStruct(scratch.shape, scratch.dtype) for scratch in joined],
        [picked],
        token_flops * 3 // 4,
        place,
        16,
    )
    kept = call(
        functools.partial(owners_kernel, 0),
        (pair_tokens, deltas, acts, grads),
        [jax.ShapeDtypeStruct(block, f32)] * parts,
        [picked],
        token_flops // 4,
        place,
        16,
    )
    quest, given = lax.optimization_barrier((jnp.stack([queries.T, out_grad.T]), given))
    quests = [quest] + [swap(quest, flip) for flip in (1, 2, 3)]
    came = [swap(part, zed) for part in given]
    came[0], quests = lax.optimization_barrier((came[0], quests))
    crossed = [swap((k + c.astype(f32)).astype(bf16), 3 * zed) for k, c in zip(kept, came)]
    sums, stats = zip(
        *(
            call(
                functools.partial(sum_kernel, parts, part),
                (weights, kept[part], came[part], crossed[part]),
                (
                    jax.ShapeDtypeStruct(block, bf16),
                    jax.ShapeDtypeStruct((24, 2 * rows // parts), f32),
                ),
                place=place,
            )
            for part in range(parts)
        )
    )
    backs = [swap(part, zed) for part in sums]
    stats = jnp.stack(stats)
    there, backs[0] = lax.optimization_barrier((swap(stats, core), backs[0]))
    stats = stats + there
    factors = [
        call(
            functools.partial(factor_kernel, 2 * n_hid * cols),
            (here, there),
            (jax.ShapeDtypeStruct((parts, 16, 2 * rows // parts), f32),),
        )[0]
        for here, there in (
            (stats, swap(stats, pair)),
            (swap(stats, zed), swap(stats, zed + pair)),
        )
    ]

    count = queries.shape[0]
    piece = (2, feats, count)
    kept_given = [jax.ShapeDtypeStruct(piece, f32), jax.ShapeDtypeStruct(piece, bf16)]
    query = pltpu.VMEM((2, width, count), bf16)
    query_flops = 6 * 2 * count * width * cols
    renewed, kept, given = call(
        functools.partial(renew_kernel, parts),
        (weights, *sums, *backs, *factors, *quests[2:]),
        [jax.ShapeDtypeStruct(whole, bf16), *kept_given],
        [query],
        query_flops,
        place,
        16,
    )
    from_core, quests = lax.optimization_barrier((swap(given, core), quests))
    from_pair = swap((kept + from_core.astype(f32)).astype(bf16), pair)
    kept, given = call(
        query_kernel, (renewed, *quests[:2]), kept_given, [query], query_flops, place, 16
    )
    out, grad = call(
        last_kernel,
        (kept, swap(given, core), from_pair),
        [jax.ShapeDtypeStruct(piece[1:], bf16)] * 2,
    )
    return out.T, grad.T


def silu_slope(pre):
    sigma = jax.nn.sigmoid(pre)
    return sigma * (1.0 + pre * (1.0 - sigma))


def contract_rows(left, right):
    return lax.dot_general(
        left, right, (((0,), (0,)), ((), ())), preferred_element_type=jnp.float32
    )


def contract_cols(left, right):
    return lax.dot_general(
        left, right, (((1,), (1,)), ((), ())), preferred_element_type=jnp.float32
    )


def finish(moved, wsq, msq):
    return (moved * (jnp.sqrt(wsq) / jnp.sqrt(msq + epsilon))[:, None]).astype(jnp.bfloat16)


def general(
    input_keys, input_values, input_lr, gate_weight, up_weight, down_weight, queries, out_grad, n_hid
):
    keys, values = (
        lax.all_gather(input_keys, "hid", axis=1, tiled=True),
        lax.all_gather(input_values, "hid", axis=1, tiled=True),
    )
    w_gate, w_up, w_down = (
        lax.all_gather(gate_weight, "tok", axis=0, tiled=True),
        lax.all_gather(up_weight, "tok", axis=0, tiled=True),
        lax.all_gather(down_weight, "tok", axis=0, tiled=True),
    )
    scaled = (input_lr[:, None] * values.astype(jnp.float32)).astype(jnp.bfloat16)
    key_gate = jnp.dot(keys, w_gate, preferred_element_type=jnp.float32)
    key_up = jnp.dot(keys, w_up, preferred_element_type=jnp.float32)
    gate_act = jax.nn.silu(key_gate)
    key_act = (gate_act * key_up).astype(jnp.bfloat16)
    back = jnp.dot(scaled, w_down, preferred_element_type=jnp.float32)
    d_gate = (-back * key_up * silu_slope(key_gate)).astype(jnp.bfloat16)
    d_up = (-back * gate_act).astype(jnp.bfloat16)
    width = gate_weight.shape[1]
    hidden = width * n_hid
    grads = lax.psum(
        jnp.concatenate(
            [
                contract_rows(keys, d_gate),
                contract_rows(keys, d_up),
                -contract_rows(scaled, key_act),
            ],
            axis=1,
        ),
        "tok",
    )
    olds = (w_gate, w_up, w_down)
    pieces = [grads[:, :width], grads[:, width : 2 * width], grads[:, 2 * width :]]
    weights = [old.astype(jnp.float32) for old in olds]
    renewed = []
    stats = []
    for weight, grad in zip(weights, pieces):
        stats.append(jnp.sum(weight * weight, axis=1))
        stats.append(jnp.sum(weight * grad, axis=1))
        stats.append(jnp.sum(grad * grad, axis=1))
    totals = lax.psum(
        (stats[0], stats[1], stats[2], stats[3], stats[4], stats[5], stats[6], stats[7], stats[8]),
        "hid",
    )
    for index in range(3):
        wsq = totals[3 * index] / hidden
        cross = totals[3 * index + 1] / hidden
        gsq = totals[3 * index + 2] / hidden
        scale = step_ratio * jnp.sqrt(wsq) / jnp.sqrt(gsq + epsilon)
        moved = weights[index] - scale[:, None] * pieces[index]
        msq = wsq - 2.0 * scale * cross + scale * scale * gsq
        renewed.append(finish(moved, wsq, msq))
    new_gate, new_up, new_down = (renewed[0], renewed[1], renewed[2])
    query_rows, grad_rows = (
        lax.all_gather(queries, "hid", axis=1, tiled=True),
        lax.all_gather(out_grad, "hid", axis=1, tiled=True),
    )
    query_gate = jnp.dot(query_rows, new_gate, preferred_element_type=jnp.float32)
    query_up = jnp.dot(query_rows, new_up, preferred_element_type=jnp.float32)
    query_silu = jax.nn.silu(query_gate)
    query_act = (query_silu * query_up).astype(jnp.bfloat16)
    out_part = contract_cols(query_act, new_down)
    query_back = jnp.dot(grad_rows, new_down, preferred_element_type=jnp.float32)
    q_gate_grad = (query_back * query_up * silu_slope(query_gate)).astype(jnp.bfloat16)
    q_up_grad = (query_back * query_silu).astype(jnp.bfloat16)
    grad_part = contract_cols(q_gate_grad, new_gate) + contract_cols(q_up_grad, new_up)
    out_sum, grad_sum = (
        lax.psum_scatter(
            out_part.astype(jnp.bfloat16), "hid", scatter_dimension=1, tiled=True
        ).astype(jnp.float32),
        lax.psum_scatter(
            grad_part.astype(jnp.bfloat16), "hid", scatter_dimension=1, tiled=True
        ).astype(jnp.float32),
    )
    return (out_sum.astype(jnp.bfloat16), grad_sum.astype(jnp.bfloat16))


def solution(mesh):
    n_tok, n_hid = mesh.shape["tok"], mesh.shape["hid"]

    def shards(*args):
        rows, cols = args[3].shape
        toks, count = args[0].shape[0], args[6].shape[0]
        fits = (
            n_hid == 2
            and n_tok == 8
            and rows % 16 == 0
            and cols % 256 == 0
            and toks % 256 == 0
            and count % 128 == 0
        )
        if fits:
            return direct(*args, n_tok, n_hid)
        return general(*args, n_hid)

    return jax.shard_map(
        shards,
        mesh=mesh,
        in_specs=(
            P(("scene", "tok"), "hid"),
            P(("scene", "tok"), "hid"),
            P(("scene", "tok")),
            P("tok", "hid"),
            P("tok", "hid"),
            P("tok", "hid"),
            P(("scene", "tok"), "hid"),
            P(("scene", "tok"), "hid"),
        ),
        out_specs=(P(("scene", "tok"), "hid"), P(("scene", "tok"), "hid")),
        check_vma=False,
    )
```

```python
import functools

import jax
import jax.numpy as jnp
from jax import lax
from jax.experimental import pallas as pl
from jax.experimental.pallas import tpu as pltpu
from jax.sharding import PartitionSpec as P

step_ratio = 0.5
epsilon = 1e-06
f32, bf16 = jnp.float32, jnp.bfloat16
LANES = 128


def contract(left, right, left_dim, right_dim):
    return lax.dot_general(
        left, right, (((left_dim,), (right_dim,)), ((), ())), preferred_element_type=f32
    )


def gated(gate, up):
    sigma = jax.nn.sigmoid(gate)
    silu = gate * sigma
    slope = sigma * (1.0 + gate * (1.0 - sigma))
    return silu, slope * up, silu * up


def join(full, mine, other, half):
    feats = mine.shape[-2]
    full[:, pl.ds(pl.multiple_of(half * feats, feats), feats), :] = mine[...]
    full[:, pl.ds(pl.multiple_of((1 - half) * feats, feats), feats), :] = other[...]


def backward(tokens, weights, deltas, acts):
    cols, total = acts.shape
    chunk = min(512, total)
    for start in range(0, total, chunk):
        span = slice(start, start + chunk)
        gate = contract(weights[0], tokens[0, :, span], 0, 0)
        up = contract(weights[1], tokens[0, :, span], 0, 0)
        back = contract(weights[2], tokens[1, :, span], 0, 0)
        silu, slope_up, act = gated(gate, up)
        deltas[:cols, span] = (back * slope_up).astype(bf16)
        deltas[cols:, span] = (back * silu).astype(bf16)
        acts[:, span] = act.astype(bf16)


def gradients(tokens, deltas, acts):
    cols = acts.shape[0]
    both = contract(tokens[0], deltas[...], 1, 1)
    return both[:, :cols], both[:, cols:], contract(tokens[1], acts[...], 1, 1)


def rows_kernel(groups, place, *refs):
    blocks, (weights,) = refs[: 2 * groups], refs[2 * groups :]
    group, side = place[0], place[1]
    for index, block in enumerate(blocks):
        flip, sided = index % groups, (side if index < groups else 1 - side)
        weights[:, rows_of((group ^ flip) * 2 + sided, block.shape[1]), :] = block[...]


def own_kernel(place, mine, other, weights, grads, tokens, deltas, acts):
    join(tokens, mine, other, place[2])
    backward(tokens, weights, deltas, acts)
    for index, grad in enumerate(gradients(tokens, deltas, acts)):
        grads[index] = grad


def owners_kernel(given, place, tokens, deltas, acts, before, *refs):
    outs, picked = refs[:-1], refs[-1]
    size = picked.shape[1] // 2
    owners = [rows_of(place[0] ^ (3 * spot) ^ given, size) for spot in range(2)]
    for spot, where in enumerate(owners):
        picked[:, spot * size : (spot + 1) * size, :] = tokens[:, where, :]
    short = size // len(outs)
    for index, grad in enumerate(gradients(picked, deltas, acts)):
        for spot, where in enumerate(owners):
            total = before[index, where, :] + grad[spot * size : (spot + 1) * size]
            for part, out in enumerate(outs):
                out[spot, index] = total[part * short : (part + 1) * short].astype(out.dtype)


def pair_kernel(place, mine, other, weights, before, *refs):
    outs, (tokens, deltas, acts, picked) = refs[:-4], refs[-4:]
    join(tokens, mine, other, place[2])
    backward(tokens, weights, deltas, acts)
    owners_kernel(1, place, tokens, deltas, acts, before, *outs, picked)


def rows_of(owner, rows):
    return pl.ds(pl.multiple_of(owner * rows, rows), rows)


def kept_kernel(parts, place, tokens, deltas, acts, before, weights, *refs):
    outs, olds, picked = refs[:parts], refs[parts : 2 * parts], refs[2 * parts]
    owners_kernel(0, place, tokens, deltas, acts, before, *outs, picked)
    for part, old in enumerate(olds):
        for spot in range(2):
            where = rows_of((place[0] ^ (3 * spot)) * parts + part, old.shape[2])
            old[spot] = weights[:, where, :]


def sum_kernel(olds, kept, came, crossed, grad_out, stats_out):
    rows = kept.shape[2]
    lane = lax.broadcasted_iota(jnp.int32, (rows, LANES), 1)
    both = []
    for spot in range(2):
        stats = jnp.zeros((rows, LANES), f32)
        for index in range(3):
            near = kept[spot, index] + came[spot, index].astype(f32)
            grad = near + crossed[1 - spot, index].astype(f32)
            grad_out[spot, index] = grad.astype(bf16)
            weight = olds[spot, index].astype(f32)
            for slot, product in enumerate((weight * weight, weight * grad, grad * grad)):
                row_sum = jnp.sum(product, axis=1, keepdims=True)
                stats = jnp.where(lane == 8 * slot + index, row_sum, stats)
        both.append(stats)
    stats_out[...] = jnp.concatenate(both, axis=0).T[: stats_out.shape[0]]


def factor_kernel(hidden, here, there, factors):
    sums = (here[...] + there[...]) / hidden
    wsq, cross, gsq = sums[:, :8], sums[:, 8:16], sums[:, 16:]
    scale = step_ratio * jnp.sqrt(wsq) / jnp.sqrt(gsq + epsilon)
    msq = wsq + 2.0 * scale * cross + scale * scale * gsq
    factor = jnp.sqrt(wsq) / jnp.sqrt(msq + epsilon)
    factors[:, :8] = factor
    factors[:, 8:] = scale * factor


def answer(renewed, query, quests, half, kept, given):
    mine, other = quests
    feats = mine.shape[1]
    join(query, mine, other, half)
    gate = contract(renewed[0], query[0], 0, 0)
    up = contract(renewed[1], query[0], 0, 0)
    back = contract(renewed[2], query[1], 0, 0)
    silu, slope_up, act = gated(gate, up)
    out = contract(renewed[2], act.astype(bf16), 1, 0)
    grad = contract(renewed[0], (back * slope_up).astype(bf16), 1, 0) + contract(
        renewed[1], (back * silu).astype(bf16), 1, 0
    )
    for index, whole in enumerate((out, grad)):
        first, second = whole[:feats], whole[feats:]
        kept[index] = jnp.where(half == 0, first, second)
        given[index] = jnp.where(half == 0, second, first).astype(bf16)


def renew_kernel(parts, place, weights, *refs):
    grads, factors, quests, refs = refs[: 2 * parts], refs[2 * parts : 2 * parts + 2], refs[-6:-4], refs[-4:]
    renewed, kept, given, query = refs
    for spot in range(2):
        for near in range(2):
            for part in range(parts):
                grad = grads[near * parts + part]
                rows = grad.shape[2]
                where = rows_of((place[0] ^ ((3 * spot) ^ near)) * parts + part, rows)
                scales = factors[near][part].T[spot * rows : (spot + 1) * rows]
                for index in range(3):
                    old = weights[index, where, :].astype(f32) * scales[:, index : index + 1]
                    step = grad[spot, index].astype(f32) * scales[:, 8 + index : 9 + index]
                    renewed[index, where, :] = (old + step).astype(bf16)
    answer(renewed, query, quests, place[2], kept, given)


def query_kernel(place, renewed, mine, other, kept, given, query):
    answer(renewed, query, (mine, other), place[2], kept, given)


def last_kernel(kept, core, pair, out, grad):
    for index, target in enumerate((out, grad)):
        target[...] = (kept[index] + core[index].astype(f32) + pair[index].astype(f32)).astype(bf16)


def call(body, operands, outs, scratch=(), flops=0, place=None, mib=4):
    specs = [pl.BlockSpec(memory_space=pltpu.VMEM)] * len(operands)
    if place is not None:
        specs, operands = [pl.BlockSpec(memory_space=pltpu.SMEM)] + specs, (place, *operands)
    moved = sum(4 * leaf.size for leaf in (*operands, *outs))
    return pl.pallas_call(
        body,
        out_shape=list(outs),
        in_specs=specs,
        out_specs=[pl.BlockSpec(memory_space=pltpu.VMEM)] * len(outs),
        scratch_shapes=list(scratch),
        compiler_params=pltpu.CompilerParams(vmem_limit_bytes=mib * 1024 * 1024),
        cost_estimate=pl.CostEstimate(flops=flops, bytes_accessed=moved, transcendentals=0),
    )(*operands)


def direct(
    input_keys, input_values, input_lr, gate_weight, up_weight, down_weight, queries, out_grad,
    n_tok, n_hid,
):
    groups = n_tok // 2
    tok, half = lax.axis_index("tok"), lax.axis_index("hid")
    group, side = tok // 2, tok % 2
    place = jnp.stack([group, side, half]).astype(jnp.int32)
    core, pair, zed = 1, 2, 4

    def swap(array, flip):
        pairs = [(i, i ^ flip) for i in range(n_tok * n_hid)]
        return lax.ppermute(array, ("tok", "hid"), pairs)

    def gather(block):
        near, across = swap(block, zed), swap(block, 2 * zed)
        return [block, near, across, swap(across, zed)]

    stacked = jnp.stack([gate_weight, up_weight, down_weight])
    cols = stacked.shape[2] // 2
    own_w = lax.dynamic_slice_in_dim(stacked, side * cols, cols, 2)
    give_w = lax.dynamic_slice_in_dim(stacked, (1 - side) * cols, cols, 2)
    vals = (input_lr[None, :] * input_values.T.astype(f32)).astype(bf16)
    tokens = jnp.stack([input_keys.T, vals])
    _, feats, toks = tokens.shape
    first = gather(own_w)
    tokens, pair_w = lax.optimization_barrier((tokens, swap(give_w, pair)))
    second = gather(pair_w)
    pair_tokens = swap(tokens, pair)

    width = n_hid * feats
    rows = width // groups
    whole = (3, width, cols)
    block = (3, rows, cols)
    token_flops = 6 * 2 * toks * width * cols
    joined = [
        pltpu.VMEM((2, width, toks), bf16),
        pltpu.VMEM((2 * cols, toks), bf16),
        pltpu.VMEM((cols, toks), bf16),
    ]
    (weights,) = call(
        functools.partial(rows_kernel, groups),
        (*first, *second),
        (jax.ShapeDtypeStruct(whole, bf16),),
        place=place,
    )
    pair_tokens, weights = lax.optimization_barrier((pair_tokens, weights))
    (grads,) = call(
        own_kernel,
        (tokens, swap(tokens, core), weights),
        (jax.ShapeDtypeStruct(whole, f32),),
        joined,
        token_flops,
        place,
        16,
    )
    parts = 2
    block = (2, 3, rows // parts, cols)
    picked = pltpu.VMEM((2, 2 * rows, toks), bf16)
    *given, pair_tokens, deltas, acts = call(
        pair_kernel,
        (pair_tokens, swap(pair_tokens, core), weights, grads),
        [jax.ShapeDtypeStruct(block, bf16)] * parts
        + [jax.ShapeDtypeStruct(scratch.shape, scratch.dtype) for scratch in joined],
        [picked],
        token_flops * 3 // 4,
        place,
        16,
    )
    kept_olds = call(
        functools.partial(kept_kernel, parts),
        (pair_tokens, deltas, acts, grads, weights),
        [jax.ShapeDtypeStruct(block, f32)] * parts + [jax.ShapeDtypeStruct(block, bf16)] * parts,
        [picked],
        token_flops // 4,
        place,
        16,
    )
    kept, olds = kept_olds[:parts], kept_olds[parts:]
    quest, given = lax.optimization_barrier((jnp.stack([queries.T, out_grad.T]), given))
    quests = [quest] + [swap(quest, flip) for flip in (1, 2, 3)]
    came = [swap(part, zed) for part in given]
    came[0], quests[1:3] = lax.optimization_barrier((came[0], quests[1:3]))
    crossed = [swap((k + c.astype(f32)).astype(bf16), 3 * zed) for k, c in zip(kept, came)]
    sums, stats = zip(
        *(
            call(
                sum_kernel,
                (olds[part], kept[part], came[part], crossed[part]),
                (
                    jax.ShapeDtypeStruct(block, bf16),
                    jax.ShapeDtypeStruct((24, 2 * rows // parts), f32),
                ),
            )
            for part in range(parts)
        )
    )
    backs = [swap(part, zed) for part in sums]
    stats = jnp.stack(stats)
    there, backs[0] = lax.optimization_barrier((swap(stats, core), backs[0]))
    stats = stats + there
    factors = [
        call(
            functools.partial(factor_kernel, 2 * n_hid * cols),
            (here, there),
            (jax.ShapeDtypeStruct((parts, 16, 2 * rows // parts), f32),),
        )[0]
        for here, there in (
            (stats, swap(stats, pair)),
            (swap(stats, zed), swap(stats, zed + pair)),
        )
    ]

    count = queries.shape[0]
    piece = (2, feats, count)
    kept_given = [jax.ShapeDtypeStruct(piece, f32), jax.ShapeDtypeStruct(piece, bf16)]
    query = pltpu.VMEM((2, width, count), bf16)
    query_flops = 6 * 2 * count * width * cols
    renewed, kept, given = call(
        functools.partial(renew_kernel, parts),
        (weights, *sums, *backs, *factors, *quests[2:]),
        [jax.ShapeDtypeStruct(whole, bf16), *kept_given],
        [query],
        query_flops,
        place,
        16,
    )
    from_core, quests = lax.optimization_barrier((swap(given, core), quests))
    from_pair = swap((kept + from_core.astype(f32)).astype(bf16), pair)
    kept, given = call(
        query_kernel, (renewed, *quests[:2]), kept_given, [query], query_flops, place, 16
    )
    out, grad = call(
        last_kernel,
        (kept, swap(given, core), from_pair),
        [jax.ShapeDtypeStruct(piece[1:], bf16)] * 2,
    )
    return out.T, grad.T


def silu_slope(pre):
    sigma = jax.nn.sigmoid(pre)
    return sigma * (1.0 + pre * (1.0 - sigma))


def contract_rows(left, right):
    return lax.dot_general(
        left, right, (((0,), (0,)), ((), ())), preferred_element_type=jnp.float32
    )


def contract_cols(left, right):
    return lax.dot_general(
        left, right, (((1,), (1,)), ((), ())), preferred_element_type=jnp.float32
    )


def finish(moved, wsq, msq):
    return (moved * (jnp.sqrt(wsq) / jnp.sqrt(msq + epsilon))[:, None]).astype(jnp.bfloat16)


def general(
    input_keys, input_values, input_lr, gate_weight, up_weight, down_weight, queries, out_grad, n_hid
):
    keys, values = (
        lax.all_gather(input_keys, "hid", axis=1, tiled=True),
        lax.all_gather(input_values, "hid", axis=1, tiled=True),
    )
    w_gate, w_up, w_down = (
        lax.all_gather(gate_weight, "tok", axis=0, tiled=True),
        lax.all_gather(up_weight, "tok", axis=0, tiled=True),
        lax.all_gather(down_weight, "tok", axis=0, tiled=True),
    )
    scaled = (input_lr[:, None] * values.astype(jnp.float32)).astype(jnp.bfloat16)
    key_gate = jnp.dot(keys, w_gate, preferred_element_type=jnp.float32)
    key_up = jnp.dot(keys, w_up, preferred_element_type=jnp.float32)
    gate_act = jax.nn.silu(key_gate)
    key_act = (gate_act * key_up).astype(jnp.bfloat16)
    back = jnp.dot(scaled, w_down, preferred_element_type=jnp.float32)
    d_gate = (-back * key_up * silu_slope(key_gate)).astype(jnp.bfloat16)
    d_up = (-back * gate_act).astype(jnp.bfloat16)
    width = gate_weight.shape[1]
    hidden = width * n_hid
    grads = lax.psum(
        jnp.concatenate(
            [
                contract_rows(keys, d_gate),
                contract_rows(keys, d_up),
                -contract_rows(scaled, key_act),
            ],
            axis=1,
        ),
        "tok",
    )
    olds = (w_gate, w_up, w_down)
    pieces = [grads[:, :width], grads[:, width : 2 * width], grads[:, 2 * width :]]
    weights = [old.astype(jnp.float32) for old in olds]
    renewed = []
    stats = []
    for weight, grad in zip(weights, pieces):
        stats.append(jnp.sum(weight * weight, axis=1))
        stats.append(jnp.sum(weight * grad, axis=1))
        stats.append(jnp.sum(grad * grad, axis=1))
    totals = lax.psum(
        (stats[0], stats[1], stats[2], stats[3], stats[4], stats[5], stats[6], stats[7], stats[8]),
        "hid",
    )
    for index in range(3):
        wsq = totals[3 * index] / hidden
        cross = totals[3 * index + 1] / hidden
        gsq = totals[3 * index + 2] / hidden
        scale = step_ratio * jnp.sqrt(wsq) / jnp.sqrt(gsq + epsilon)
        moved = weights[index] - scale[:, None] * pieces[index]
        msq = wsq - 2.0 * scale * cross + scale * scale * gsq
        renewed.append(finish(moved, wsq, msq))
    new_gate, new_up, new_down = (renewed[0], renewed[1], renewed[2])
    query_rows, grad_rows = (
        lax.all_gather(queries, "hid", axis=1, tiled=True),
        lax.all_gather(out_grad, "hid", axis=1, tiled=True),
    )
    query_gate = jnp.dot(query_rows, new_gate, preferred_element_type=jnp.float32)
    query_up = jnp.dot(query_rows, new_up, preferred_element_type=jnp.float32)
    query_silu = jax.nn.silu(query_gate)
    query_act = (query_silu * query_up).astype(jnp.bfloat16)
    out_part = contract_cols(query_act, new_down)
    query_back = jnp.dot(grad_rows, new_down, preferred_element_type=jnp.float32)
    q_gate_grad = (query_back * query_up * silu_slope(query_gate)).astype(jnp.bfloat16)
    q_up_grad = (query_back * query_silu).astype(jnp.bfloat16)
    grad_part = contract_cols(q_gate_grad, new_gate) + contract_cols(q_up_grad, new_up)
    out_sum, grad_sum = (
        lax.psum_scatter(
            out_part.astype(jnp.bfloat16), "hid", scatter_dimension=1, tiled=True
        ).astype(jnp.float32),
        lax.psum_scatter(
            grad_part.astype(jnp.bfloat16), "hid", scatter_dimension=1, tiled=True
        ).astype(jnp.float32),
    )
    return (out_sum.astype(jnp.bfloat16), grad_sum.astype(jnp.bfloat16))


def solution(mesh):
    n_tok, n_hid = mesh.shape["tok"], mesh.shape["hid"]

    def shards(*args):
        rows, cols = args[3].shape
        toks, count = args[0].shape[0], args[6].shape[0]
        fits = (
            n_hid == 2
            and n_tok == 8
            and rows % 16 == 0
            and cols % 256 == 0
            and toks % 256 == 0
            and count % 128 == 0
        )
        if fits:
            return direct(*args, n_tok, n_hid)
        return general(*args, n_hid)

    return jax.shard_map(
        shards,
        mesh=mesh,
        in_specs=(
            P(("scene", "tok"), "hid"),
            P(("scene", "tok"), "hid"),
            P(("scene", "tok")),
            P("tok", "hid"),
            P("tok", "hid"),
            P("tok", "hid"),
            P(("scene", "tok"), "hid"),
            P(("scene", "tok"), "hid"),
        ),
        out_specs=(P(("scene", "tok"), "hid"), P(("scene", "tok"), "hid")),
        check_vma=False,
    )
```

```python
import functools

import jax
import jax.numpy as jnp
from jax import lax
from jax.experimental import pallas as pl
from jax.experimental.pallas import tpu as pltpu
from jax.sharding import PartitionSpec as P

step_ratio = 0.5
epsilon = 1e-06
f32, bf16 = jnp.float32, jnp.bfloat16
LANES = 128


def contract(left, right, left_dim, right_dim):
    return lax.dot_general(
        left, right, (((left_dim,), (right_dim,)), ((), ())), preferred_element_type=f32
    )


def gated(gate, up):
    sigma = jax.nn.sigmoid(gate)
    silu = gate * sigma
    slope = sigma * (1.0 + gate * (1.0 - sigma))
    return silu, slope * up, silu * up


def join(full, mine, other, half):
    feats = mine.shape[-2]
    full[:, pl.ds(pl.multiple_of(half * feats, feats), feats), :] = mine[...]
    full[:, pl.ds(pl.multiple_of((1 - half) * feats, feats), feats), :] = other[...]


def backward(tokens, weights, deltas, acts):
    cols, total = acts.shape
    chunk = min(512, total)
    for start in range(0, total, chunk):
        span = slice(start, start + chunk)
        gate = contract(weights[0], tokens[0, :, span], 0, 0)
        up = contract(weights[1], tokens[0, :, span], 0, 0)
        back = contract(weights[2], tokens[1, :, span], 0, 0)
        silu, slope_up, act = gated(gate, up)
        deltas[:cols, span] = (back * slope_up).astype(bf16)
        deltas[cols:, span] = (back * silu).astype(bf16)
        acts[:, span] = act.astype(bf16)


def gradients(tokens, deltas, acts):
    cols = acts.shape[0]
    both = contract(tokens[0], deltas[...], 1, 1)
    return both[:, :cols], both[:, cols:], contract(tokens[1], acts[...], 1, 1)


def rows_kernel(groups, place, *refs):
    blocks, (weights,) = refs[: 2 * groups], refs[2 * groups :]
    group, side = place[0], place[1]
    for index, block in enumerate(blocks):
        flip, sided = index % groups, (side if index < groups else 1 - side)
        weights[:, rows_of((group ^ flip) * 2 + sided, block.shape[1]), :] = block[...]


def own_kernel(place, mine, other, weights, grads, tokens, deltas, acts):
    join(tokens, mine, other, place[2])
    backward(tokens, weights, deltas, acts)
    for index, grad in enumerate(gradients(tokens, deltas, acts)):
        grads[index] = grad


def owners_kernel(given, place, tokens, deltas, acts, before, *refs):
    outs, picked = refs[:-1], refs[-1]
    size = picked.shape[1] // 2
    owners = [rows_of(place[0] ^ (3 * spot) ^ given, size) for spot in range(2)]
    for spot, where in enumerate(owners):
        picked[:, spot * size : (spot + 1) * size, :] = tokens[:, where, :]
    short = size // len(outs)
    for index, grad in enumerate(gradients(picked, deltas, acts)):
        for spot, where in enumerate(owners):
            total = before[index, where, :] + grad[spot * size : (spot + 1) * size]
            for part, out in enumerate(outs):
                out[spot, index] = total[part * short : (part + 1) * short].astype(out.dtype)


def pair_kernel(place, mine, other, weights, before, *refs):
    outs, (tokens, deltas, acts, picked) = refs[:-4], refs[-4:]
    join(tokens, mine, other, place[2])
    backward(tokens, weights, deltas, acts)
    owners_kernel(1, place, tokens, deltas, acts, before, *outs, picked)


def rows_of(owner, rows):
    return pl.ds(pl.multiple_of(owner * rows, rows), rows)


def kept_kernel(parts, place, tokens, deltas, acts, before, weights, *refs):
    outs, olds, picked = refs[:parts], refs[parts : 2 * parts], refs[2 * parts]
    owners_kernel(0, place, tokens, deltas, acts, before, *outs, picked)
    for part, old in enumerate(olds):
        for spot in range(2):
            where = rows_of((place[0] ^ (3 * spot)) * parts + part, old.shape[2])
            old[spot] = weights[:, where, :]


def sum_kernel(olds, kept, came, crossed, grad_out, stats_out):
    rows = kept.shape[2]
    lane = lax.broadcasted_iota(jnp.int32, (rows, LANES), 1)
    both = []
    for spot in range(2):
        stats = jnp.zeros((rows, LANES), f32)
        for index in range(3):
            near = kept[spot, index] + came[spot, index].astype(f32)
            grad = near + crossed[1 - spot, index].astype(f32)
            grad_out[spot, index] = grad.astype(bf16)
            weight = olds[spot, index].astype(f32)
            for slot, product in enumerate((weight * weight, weight * grad, grad * grad)):
                row_sum = jnp.sum(product, axis=1, keepdims=True)
                stats = jnp.where(lane == 8 * slot + index, row_sum, stats)
        both.append(stats)
    stats_out[...] = jnp.concatenate(both, axis=0).T[: stats_out.shape[0]]


def factor_kernel(hidden, here, there, factors):
    sums = (here[...] + there[...]) / hidden
    wsq, cross, gsq = sums[:, :8], sums[:, 8:16], sums[:, 16:]
    scale = step_ratio * jnp.sqrt(wsq) / jnp.sqrt(gsq + epsilon)
    msq = wsq + 2.0 * scale * cross + scale * scale * gsq
    factor = jnp.sqrt(wsq) / jnp.sqrt(msq + epsilon)
    factors[:, :8] = factor
    factors[:, 8:] = scale * factor


def answer(renewed, query, quests, half, kept, given):
    mine, other = quests
    feats = mine.shape[1]
    join(query, mine, other, half)
    gate = contract(renewed[0], query[0], 0, 0)
    up = contract(renewed[1], query[0], 0, 0)
    back = contract(renewed[2], query[1], 0, 0)
    silu, slope_up, act = gated(gate, up)
    out = contract(renewed[2], act.astype(bf16), 1, 0)
    grad = contract(renewed[0], (back * slope_up).astype(bf16), 1, 0) + contract(
        renewed[1], (back * silu).astype(bf16), 1, 0
    )
    for index, whole in enumerate((out, grad)):
        first, second = whole[:feats], whole[feats:]
        kept[index] = jnp.where(half == 0, first, second)
        given[index] = jnp.where(half == 0, second, first).astype(bf16)


def renew_kernel(parts, place, weights, *refs):
    grads, factors, quests, refs = refs[: 2 * parts], refs[2 * parts : 2 * parts + 2], refs[-6:-4], refs[-4:]
    renewed, kept, given, query = refs
    for spot in range(2):
        for near in range(2):
            for part in range(parts):
                grad = grads[near * parts + part]
                rows = grad.shape[2]
                where = rows_of((place[0] ^ ((3 * spot) ^ near)) * parts + part, rows)
                scales = factors[near][part].T[spot * rows : (spot + 1) * rows]
                for index in range(3):
                    old = weights[index, where, :].astype(f32) * scales[:, index : index + 1]
                    step = grad[spot, index].astype(f32) * scales[:, 8 + index : 9 + index]
                    renewed[index, where, :] = (old + step).astype(bf16)
    answer(renewed, query, quests, place[2], kept, given)


def query_kernel(place, renewed, mine, other, kept, given, query):
    answer(renewed, query, (mine, other), place[2], kept, given)


def last_kernel(kept, core, pair, out, grad):
    for index, target in enumerate((out, grad)):
        target[...] = (kept[index] + core[index].astype(f32) + pair[index].astype(f32)).astype(bf16)


def call(body, operands, outs, scratch=(), flops=0, place=None, mib=4):
    specs = [pl.BlockSpec(memory_space=pltpu.VMEM)] * len(operands)
    if place is not None:
        inner, body = body, lambda *refs: inner(place(), *refs)
    moved = sum(4 * leaf.size for leaf in (*operands, *outs))
    return pl.pallas_call(
        body,
        out_shape=list(outs),
        in_specs=specs,
        out_specs=[pl.BlockSpec(memory_space=pltpu.VMEM)] * len(outs),
        scratch_shapes=list(scratch),
        compiler_params=pltpu.CompilerParams(vmem_limit_bytes=mib * 1024 * 1024),
        cost_estimate=pl.CostEstimate(flops=flops, bytes_accessed=moved, transcendentals=0),
    )(*operands)


def direct(
    input_keys, input_values, input_lr, gate_weight, up_weight, down_weight, queries, out_grad,
    n_tok, n_hid,
):
    groups = n_tok // 2
    tok, half = lax.axis_index("tok"), lax.axis_index("hid")
    group, side = tok // 2, tok % 2

    def place():
        spot = lax.axis_index("tok")
        return spot >> 1, spot & 1, lax.axis_index("hid")

    core, pair, zed = 1, 2, 4

    def swap(array, flip):
        pairs = [(i, i ^ flip) for i in range(n_tok * n_hid)]
        return lax.ppermute(array, ("tok", "hid"), pairs)

    def gather(block):
        near, across = swap(block, zed), swap(block, 2 * zed)
        return [block, near, across, swap(across, zed)]

    stacked = jnp.stack([gate_weight, up_weight, down_weight])
    cols = stacked.shape[2] // 2
    own_w = lax.dynamic_slice_in_dim(stacked, side * cols, cols, 2)
    give_w = lax.dynamic_slice_in_dim(stacked, (1 - side) * cols, cols, 2)
    vals = (input_lr[None, :] * input_values.T.astype(f32)).astype(bf16)
    tokens = jnp.stack([input_keys.T, vals])
    _, feats, toks = tokens.shape
    first = gather(own_w)
    tokens, pair_w = lax.optimization_barrier((tokens, swap(give_w, pair)))
    second = gather(pair_w)
    pair_tokens = swap(tokens, pair)

    width = n_hid * feats
    rows = width // groups
    whole = (3, width, cols)
    block = (3, rows, cols)
    token_flops = 6 * 2 * toks * width * cols
    joined = [
        pltpu.VMEM((2, width, toks), bf16),
        pltpu.VMEM((2 * cols, toks), bf16),
        pltpu.VMEM((cols, toks), bf16),
    ]
    (weights,) = call(
        functools.partial(rows_kernel, groups),
        (*first, *second),
        (jax.ShapeDtypeStruct(whole, bf16),),
        place=place,
    )
    pair_tokens, weights = lax.optimization_barrier((pair_tokens, weights))
    (grads,) = call(
        own_kernel,
        (tokens, swap(tokens, core), weights),
        (jax.ShapeDtypeStruct(whole, f32),),
        joined,
        token_flops,
        place,
        16,
    )
    parts = 2
    block = (2, 3, rows // parts, cols)
    picked = pltpu.VMEM((2, 2 * rows, toks), bf16)
    *given, pair_tokens, deltas, acts = call(
        pair_kernel,
        (pair_tokens, swap(pair_tokens, core), weights, grads),
        [jax.ShapeDtypeStruct(block, bf16)] * parts
        + [jax.ShapeDtypeStruct(scratch.shape, scratch.dtype) for scratch in joined],
        [picked],
        token_flops * 3 // 4,
        place,
        16,
    )
    kept_olds = call(
        functools.partial(kept_kernel, parts),
        (pair_tokens, deltas, acts, grads, weights),
        [jax.ShapeDtypeStruct(block, f32)] * parts + [jax.ShapeDtypeStruct(block, bf16)] * parts,
        [picked],
        token_flops // 4,
        place,
        16,
    )
    kept, olds = kept_olds[:parts], kept_olds[parts:]
    quest, given = lax.optimization_barrier((jnp.stack([queries.T, out_grad.T]), given))
    quests = [quest] + [swap(quest, flip) for flip in (1, 2, 3)]
    came = [swap(part, zed) for part in given]
    came[0], quests[1:3] = lax.optimization_barrier((came[0], quests[1:3]))
    crossed = [swap((k + c.astype(f32)).astype(bf16), 3 * zed) for k, c in zip(kept, came)]
    sums, stats = zip(
        *(
            call(
                sum_kernel,
                (olds[part], kept[part], came[part], crossed[part]),
                (
                    jax.ShapeDtypeStruct(block, bf16),
                    jax.ShapeDtypeStruct((24, 2 * rows // parts), f32),
                ),
            )
            for part in range(parts)
        )
    )
    backs = [swap(part, zed) for part in sums]
    stats = jnp.stack(stats)
    there, backs[0] = lax.optimization_barrier((swap(stats, core), backs[0]))
    stats = stats + there
    factors = [
        call(
            functools.partial(factor_kernel, 2 * n_hid * cols),
            (here, there),
            (jax.ShapeDtypeStruct((parts, 16, 2 * rows // parts), f32),),
        )[0]
        for here, there in (
            (stats, swap(stats, pair)),
            (swap(stats, zed), swap(stats, zed + pair)),
        )
    ]

    count = queries.shape[0]
    piece = (2, feats, count)
    kept_given = [jax.ShapeDtypeStruct(piece, f32), jax.ShapeDtypeStruct(piece, bf16)]
    query = pltpu.VMEM((2, width, count), bf16)
    query_flops = 6 * 2 * count * width * cols
    renewed, kept, given = call(
        functools.partial(renew_kernel, parts),
        (weights, *sums, *backs, *factors, *quests[2:]),
        [jax.ShapeDtypeStruct(whole, bf16), *kept_given],
        [query],
        query_flops,
        place,
        16,
    )
    from_core, quests = lax.optimization_barrier((swap(given, core), quests))
    from_pair = swap((kept + from_core.astype(f32)).astype(bf16), pair)
    kept, given = call(
        query_kernel, (renewed, *quests[:2]), kept_given, [query], query_flops, place, 16
    )
    out, grad = call(
        last_kernel,
        (kept, swap(given, core), from_pair),
        [jax.ShapeDtypeStruct(piece[1:], bf16)] * 2,
    )
    return out.T, grad.T


def silu_slope(pre):
    sigma = jax.nn.sigmoid(pre)
    return sigma * (1.0 + pre * (1.0 - sigma))


def contract_rows(left, right):
    return lax.dot_general(
        left, right, (((0,), (0,)), ((), ())), preferred_element_type=jnp.float32
    )


def contract_cols(left, right):
    return lax.dot_general(
        left, right, (((1,), (1,)), ((), ())), preferred_element_type=jnp.float32
    )


def finish(moved, wsq, msq):
    return (moved * (jnp.sqrt(wsq) / jnp.sqrt(msq + epsilon))[:, None]).astype(jnp.bfloat16)


def general(
    input_keys, input_values, input_lr, gate_weight, up_weight, down_weight, queries, out_grad, n_hid
):
    keys, values = (
        lax.all_gather(input_keys, "hid", axis=1, tiled=True),
        lax.all_gather(input_values, "hid", axis=1, tiled=True),
    )
    w_gate, w_up, w_down = (
        lax.all_gather(gate_weight, "tok", axis=0, tiled=True),
        lax.all_gather(up_weight, "tok", axis=0, tiled=True),
        lax.all_gather(down_weight, "tok", axis=0, tiled=True),
    )
    scaled = (input_lr[:, None] * values.astype(jnp.float32)).astype(jnp.bfloat16)
    key_gate = jnp.dot(keys, w_gate, preferred_element_type=jnp.float32)
    key_up = jnp.dot(keys, w_up, preferred_element_type=jnp.float32)
    gate_act = jax.nn.silu(key_gate)
    key_act = (gate_act * key_up).astype(jnp.bfloat16)
    back = jnp.dot(scaled, w_down, preferred_element_type=jnp.float32)
    d_gate = (-back * key_up * silu_slope(key_gate)).astype(jnp.bfloat16)
    d_up = (-back * gate_act).astype(jnp.bfloat16)
    width = gate_weight.shape[1]
    hidden = width * n_hid
    grads = lax.psum(
        jnp.concatenate(
            [
                contract_rows(keys, d_gate),
                contract_rows(keys, d_up),
                -contract_rows(scaled, key_act),
            ],
            axis=1,
        ),
        "tok",
    )
    olds = (w_gate, w_up, w_down)
    pieces = [grads[:, :width], grads[:, width : 2 * width], grads[:, 2 * width :]]
    weights = [old.astype(jnp.float32) for old in olds]
    renewed = []
    stats = []
    for weight, grad in zip(weights, pieces):
        stats.append(jnp.sum(weight * weight, axis=1))
        stats.append(jnp.sum(weight * grad, axis=1))
        stats.append(jnp.sum(grad * grad, axis=1))
    totals = lax.psum(
        (stats[0], stats[1], stats[2], stats[3], stats[4], stats[5], stats[6], stats[7], stats[8]),
        "hid",
    )
    for index in range(3):
        wsq = totals[3 * index] / hidden
        cross = totals[3 * index + 1] / hidden
        gsq = totals[3 * index + 2] / hidden
        scale = step_ratio * jnp.sqrt(wsq) / jnp.sqrt(gsq + epsilon)
        moved = weights[index] - scale[:, None] * pieces[index]
        msq = wsq - 2.0 * scale * cross + scale * scale * gsq
        renewed.append(finish(moved, wsq, msq))
    new_gate, new_up, new_down = (renewed[0], renewed[1], renewed[2])
    query_rows, grad_rows = (
        lax.all_gather(queries, "hid", axis=1, tiled=True),
        lax.all_gather(out_grad, "hid", axis=1, tiled=True),
    )
    query_gate = jnp.dot(query_rows, new_gate, preferred_element_type=jnp.float32)
    query_up = jnp.dot(query_rows, new_up, preferred_element_type=jnp.float32)
    query_silu = jax.nn.silu(query_gate)
    query_act = (query_silu * query_up).astype(jnp.bfloat16)
    out_part = contract_cols(query_act, new_down)
    query_back = jnp.dot(grad_rows, new_down, preferred_element_type=jnp.float32)
    q_gate_grad = (query_back * query_up * silu_slope(query_gate)).astype(jnp.bfloat16)
    q_up_grad = (query_back * query_silu).astype(jnp.bfloat16)
    grad_part = contract_cols(q_gate_grad, new_gate) + contract_cols(q_up_grad, new_up)
    out_sum, grad_sum = (
        lax.psum_scatter(
            out_part.astype(jnp.bfloat16), "hid", scatter_dimension=1, tiled=True
        ).astype(jnp.float32),
        lax.psum_scatter(
            grad_part.astype(jnp.bfloat16), "hid", scatter_dimension=1, tiled=True
        ).astype(jnp.float32),
    )
    return (out_sum.astype(jnp.bfloat16), grad_sum.astype(jnp.bfloat16))


def solution(mesh):
    n_tok, n_hid = mesh.shape["tok"], mesh.shape["hid"]

    def shards(*args):
        rows, cols = args[3].shape
        toks, count = args[0].shape[0], args[6].shape[0]
        fits = (
            n_hid == 2
            and n_tok == 8
            and rows % 16 == 0
            and cols % 256 == 0
            and toks % 256 == 0
            and count % 128 == 0
        )
        if fits:
            return direct(*args, n_tok, n_hid)
        return general(*args, n_hid)

    return jax.shard_map(
        shards,
        mesh=mesh,
        in_specs=(
            P(("scene", "tok"), "hid"),
            P(("scene", "tok"), "hid"),
            P(("scene", "tok")),
            P("tok", "hid"),
            P("tok", "hid"),
            P("tok", "hid"),
            P(("scene", "tok"), "hid"),
            P(("scene", "tok"), "hid"),
        ),
        out_specs=(P(("scene", "tok"), "hid"), P(("scene", "tok"), "hid")),
        check_vma=False,
    )
```

```python
import functools

import jax
import jax.numpy as jnp
from jax import lax
from jax.experimental import pallas as pl
from jax.experimental.pallas import tpu as pltpu
from jax.sharding import PartitionSpec as P

step_ratio = 0.5
epsilon = 1e-06
f32, bf16 = jnp.float32, jnp.bfloat16
LANES = 128


def contract(left, right, left_dim, right_dim):
    return lax.dot_general(
        left, right, (((left_dim,), (right_dim,)), ((), ())), preferred_element_type=f32
    )


def gated(gate, up):
    sigma = 0.5 * jnp.tanh(0.5 * gate) + 0.5
    silu = gate * sigma
    slope = sigma + silu * (1.0 - sigma)
    return silu, slope * up, silu * up


def join(full, mine, other, half):
    feats = mine.shape[-2]
    full[:, pl.ds(pl.multiple_of(half * feats, feats), feats), :] = mine[...]
    full[:, pl.ds(pl.multiple_of((1 - half) * feats, feats), feats), :] = other[...]


def backward(tokens, weights, deltas, acts):
    cols, total = acts.shape
    chunk = min(512, total)
    for start in range(0, total, chunk):
        span = slice(start, start + chunk)
        gate = contract(weights[0], tokens[0, :, span], 0, 0)
        up = contract(weights[1], tokens[0, :, span], 0, 0)
        back = contract(weights[2], tokens[1, :, span], 0, 0)
        silu, slope_up, act = gated(gate, up)
        deltas[:cols, span] = (back * slope_up).astype(bf16)
        deltas[cols:, span] = (back * silu).astype(bf16)
        acts[:, span] = act.astype(bf16)


def gradients(tokens, deltas, acts):
    cols = acts.shape[0]
    both = contract(tokens[0], deltas[...], 1, 1)
    return both[:, :cols], both[:, cols:], contract(tokens[1], acts[...], 1, 1)


def rows_kernel(groups, place, *refs):
    blocks, (weights,) = refs[: 2 * groups], refs[2 * groups :]
    group, side = place[0], place[1]
    for index, block in enumerate(blocks):
        flip, sided = index % groups, (side if index < groups else 1 - side)
        weights[:, rows_of((group ^ flip) * 2 + sided, block.shape[1]), :] = block[...]


def own_kernel(place, mine, other, weights, grads, tokens, deltas, acts):
    join(tokens, mine, other, place[2])
    backward(tokens, weights, deltas, acts)
    for index, grad in enumerate(gradients(tokens, deltas, acts)):
        grads[index] = grad


def owners_kernel(given, place, tokens, deltas, acts, before, *refs):
    outs, picked = refs[:-1], refs[-1]
    size = picked.shape[1] // 2
    owners = [rows_of(place[0] ^ (3 * spot) ^ given, size) for spot in range(2)]
    for spot, where in enumerate(owners):
        picked[:, spot * size : (spot + 1) * size, :] = tokens[:, where, :]
    short = size // len(outs)
    for index, grad in enumerate(gradients(picked, deltas, acts)):
        for spot, where in enumerate(owners):
            total = before[index, where, :] + grad[spot * size : (spot + 1) * size]
            for part, out in enumerate(outs):
                out[spot, index] = total[part * short : (part + 1) * short].astype(out.dtype)


def pair_kernel(place, mine, other, weights, before, *refs):
    outs, (tokens, deltas, acts, picked) = refs[:-4], refs[-4:]
    join(tokens, mine, other, place[2])
    backward(tokens, weights, deltas, acts)
    owners_kernel(1, place, tokens, deltas, acts, before, *outs, picked)


def rows_of(owner, rows):
    return pl.ds(pl.multiple_of(owner * rows, rows), rows)


def kept_kernel(parts, place, tokens, deltas, acts, before, weights, *refs):
    outs, olds, picked = refs[:parts], refs[parts : 2 * parts], refs[2 * parts]
    owners_kernel(0, place, tokens, deltas, acts, before, *outs, picked)
    for part, old in enumerate(olds):
        for spot in range(2):
            where = rows_of((place[0] ^ (3 * spot)) * parts + part, old.shape[2])
            old[spot] = weights[:, where, :]


def sum_kernel(olds, kept, came, crossed, grad_out, stats_out):
    rows = kept.shape[2]
    lane = lax.broadcasted_iota(jnp.int32, (rows, LANES), 1)
    both = []
    for spot in range(2):
        stats = jnp.zeros((rows, LANES), f32)
        for index in range(3):
            near = kept[spot, index] + came[spot, index].astype(f32)
            grad = near + crossed[1 - spot, index].astype(f32)
            grad_out[spot, index] = grad.astype(bf16)
            weight = olds[spot, index].astype(f32)
            for slot, product in enumerate((weight * weight, weight * grad, grad * grad)):
                row_sum = jnp.sum(product, axis=1, keepdims=True)
                stats = jnp.where(lane == 8 * slot + index, row_sum, stats)
        both.append(stats)
    stats_out[...] = jnp.concatenate(both, axis=0).T[: stats_out.shape[0]]


def factor_kernel(hidden, here, there, factors):
    sums = (here[...] + there[...]) / hidden
    wsq, cross, gsq = sums[:, :8], sums[:, 8:16], sums[:, 16:]
    scale = step_ratio * jnp.sqrt(wsq) / jnp.sqrt(gsq + epsilon)
    msq = wsq + 2.0 * scale * cross + scale * scale * gsq
    factor = jnp.sqrt(wsq) / jnp.sqrt(msq + epsilon)
    factors[:, :8] = factor
    factors[:, 8:] = scale * factor


def answer(renewed, query, quests, half, kept, given):
    mine, other = quests
    feats = mine.shape[1]
    join(query, mine, other, half)
    gate = contract(renewed[0], query[0], 0, 0)
    up = contract(renewed[1], query[0], 0, 0)
    back = contract(renewed[2], query[1], 0, 0)
    silu, slope_up, act = gated(gate, up)
    out = contract(renewed[2], act.astype(bf16), 1, 0)
    grad = contract(renewed[0], (back * slope_up).astype(bf16), 1, 0) + contract(
        renewed[1], (back * silu).astype(bf16), 1, 0
    )
    for index, whole in enumerate((out, grad)):
        first, second = whole[:feats], whole[feats:]
        kept[index] = jnp.where(half == 0, first, second)
        given[index] = jnp.where(half == 0, second, first).astype(bf16)


def renew_kernel(parts, place, weights, *refs):
    grads, factors, quests, refs = refs[: 2 * parts], refs[2 * parts : 2 * parts + 2], refs[-6:-4], refs[-4:]
    renewed, kept, given, query = refs
    for spot in range(2):
        for near in range(2):
            for part in range(parts):
                grad = grads[near * parts + part]
                rows = grad.shape[2]
                where = rows_of((place[0] ^ ((3 * spot) ^ near)) * parts + part, rows)
                scales = factors[near][part].T[spot * rows : (spot + 1) * rows]
                for index in range(3):
                    old = weights[index, where, :].astype(f32) * scales[:, index : index + 1]
                    step = grad[spot, index].astype(f32) * scales[:, 8 + index : 9 + index]
                    renewed[index, where, :] = (old + step).astype(bf16)
    answer(renewed, query, quests, place[2], kept, given)


def query_kernel(place, renewed, mine, other, kept, given, query):
    answer(renewed, query, (mine, other), place[2], kept, given)


def last_kernel(kept, core, pair, out, grad):
    for index, target in enumerate((out, grad)):
        target[...] = (kept[index] + core[index].astype(f32) + pair[index].astype(f32)).astype(bf16)


def call(body, operands, outs, scratch=(), flops=0, place=None, mib=4):
    specs = [pl.BlockSpec(memory_space=pltpu.VMEM)] * len(operands)
    if place is not None:
        inner, body = body, lambda *refs: inner(place(), *refs)
    moved = sum(4 * leaf.size for leaf in (*operands, *outs))
    return pl.pallas_call(
        body,
        out_shape=list(outs),
        in_specs=specs,
        out_specs=[pl.BlockSpec(memory_space=pltpu.VMEM)] * len(outs),
        scratch_shapes=list(scratch),
        compiler_params=pltpu.CompilerParams(vmem_limit_bytes=mib * 1024 * 1024),
        cost_estimate=pl.CostEstimate(flops=flops, bytes_accessed=moved, transcendentals=0),
    )(*operands)


def direct(
    input_keys, input_values, input_lr, gate_weight, up_weight, down_weight, queries, out_grad,
    n_tok, n_hid,
):
    groups = n_tok // 2
    tok, half = lax.axis_index("tok"), lax.axis_index("hid")
    group, side = tok // 2, tok % 2

    def place():
        spot = lax.axis_index("tok")
        return spot >> 1, spot & 1, lax.axis_index("hid")

    core, pair, zed = 1, 2, 4

    def swap(array, flip):
        pairs = [(i, i ^ flip) for i in range(n_tok * n_hid)]
        return lax.ppermute(array, ("tok", "hid"), pairs)

    def gather(block):
        near, across = swap(block, zed), swap(block, 2 * zed)
        return [block, near, across, swap(across, zed)]

    stacked = jnp.stack([gate_weight, up_weight, down_weight])
    cols = stacked.shape[2] // 2
    own_w = lax.dynamic_slice_in_dim(stacked, side * cols, cols, 2)
    give_w = lax.dynamic_slice_in_dim(stacked, (1 - side) * cols, cols, 2)
    vals = (input_lr[None, :] * input_values.T.astype(f32)).astype(bf16)
    tokens = jnp.stack([input_keys.T, vals])
    _, feats, toks = tokens.shape
    first = gather(own_w)
    tokens, pair_w = lax.optimization_barrier((tokens, swap(give_w, pair)))
    second = gather(pair_w)
    pair_tokens = swap(tokens, pair)

    width = n_hid * feats
    rows = width // groups
    whole = (3, width, cols)
    block = (3, rows, cols)
    token_flops = 6 * 2 * toks * width * cols
    joined = [
        pltpu.VMEM((2, width, toks), bf16),
        pltpu.VMEM((2 * cols, toks), bf16),
        pltpu.VMEM((cols, toks), bf16),
    ]
    (weights,) = call(
        functools.partial(rows_kernel, groups),
        (*first, *second),
        (jax.ShapeDtypeStruct(whole, bf16),),
        place=place,
    )
    pair_tokens, weights = lax.optimization_barrier((pair_tokens, weights))
    (grads,) = call(
        own_kernel,
        (tokens, swap(tokens, core), weights),
        (jax.ShapeDtypeStruct(whole, f32),),
        joined,
        token_flops,
        place,
        16,
    )
    parts = 2
    block = (2, 3, rows // parts, cols)
    picked = pltpu.VMEM((2, 2 * rows, toks), bf16)
    *given, pair_tokens, deltas, acts = call(
        pair_kernel,
        (pair_tokens, swap(pair_tokens, core), weights, grads),
        [jax.ShapeDtypeStruct(block, bf16)] * parts
        + [jax.ShapeDtypeStruct(scratch.shape, scratch.dtype) for scratch in joined],
        [picked],
        token_flops * 3 // 4,
        place,
        16,
    )
    kept_olds = call(
        functools.partial(kept_kernel, parts),
        (pair_tokens, deltas, acts, grads, weights),
        [jax.ShapeDtypeStruct(block, f32)] * parts + [jax.ShapeDtypeStruct(block, bf16)] * parts,
        [picked],
        token_flops // 4,
        place,
        16,
    )
    kept, olds = kept_olds[:parts], kept_olds[parts:]
    quest, given = lax.optimization_barrier((jnp.stack([queries.T, out_grad.T]), given))
    quests = [quest] + [swap(quest, flip) for flip in (1, 2, 3)]
    came = [swap(part, zed) for part in given]
    came[0], quests[1:3] = lax.optimization_barrier((came[0], quests[1:3]))
    crossed = [swap((k + c.astype(f32)).astype(bf16), 3 * zed) for k, c in zip(kept, came)]
    sums, stats = zip(
        *(
            call(
                sum_kernel,
                (olds[part], kept[part], came[part], crossed[part]),
                (
                    jax.ShapeDtypeStruct(block, bf16),
                    jax.ShapeDtypeStruct((24, 2 * rows // parts), f32),
                ),
            )
            for part in range(parts)
        )
    )
    backs = [swap(part, zed) for part in sums]
    stats = jnp.stack(stats)
    there, backs[0] = lax.optimization_barrier((swap(stats, core), backs[0]))
    stats = stats + there
    factors = [
        call(
            functools.partial(factor_kernel, 2 * n_hid * cols),
            (here, there),
            (jax.ShapeDtypeStruct((parts, 16, 2 * rows // parts), f32),),
        )[0]
        for here, there in (
            (stats, swap(stats, pair)),
            (swap(stats, zed), swap(stats, zed + pair)),
        )
    ]

    count = queries.shape[0]
    piece = (2, feats, count)
    kept_given = [jax.ShapeDtypeStruct(piece, f32), jax.ShapeDtypeStruct(piece, bf16)]
    query = pltpu.VMEM((2, width, count), bf16)
    query_flops = 6 * 2 * count * width * cols
    renewed, kept, given = call(
        functools.partial(renew_kernel, parts),
        (weights, *sums, *backs, *factors, *quests[2:]),
        [jax.ShapeDtypeStruct(whole, bf16), *kept_given],
        [query],
        query_flops,
        place,
        16,
    )
    from_core, quests = lax.optimization_barrier((swap(given, core), quests))
    from_pair = swap((kept + from_core.astype(f32)).astype(bf16), pair)
    kept, given = call(
        query_kernel, (renewed, *quests[:2]), kept_given, [query], query_flops, place, 16
    )
    out, grad = call(
        last_kernel,
        (kept, swap(given, core), from_pair),
        [jax.ShapeDtypeStruct(piece[1:], bf16)] * 2,
    )
    return out.T, grad.T


def silu_slope(pre):
    sigma = jax.nn.sigmoid(pre)
    return sigma * (1.0 + pre * (1.0 - sigma))


def contract_rows(left, right):
    return lax.dot_general(
        left, right, (((0,), (0,)), ((), ())), preferred_element_type=jnp.float32
    )


def contract_cols(left, right):
    return lax.dot_general(
        left, right, (((1,), (1,)), ((), ())), preferred_element_type=jnp.float32
    )


def finish(moved, wsq, msq):
    return (moved * (jnp.sqrt(wsq) / jnp.sqrt(msq + epsilon))[:, None]).astype(jnp.bfloat16)


def general(
    input_keys, input_values, input_lr, gate_weight, up_weight, down_weight, queries, out_grad, n_hid
):
    keys, values = (
        lax.all_gather(input_keys, "hid", axis=1, tiled=True),
        lax.all_gather(input_values, "hid", axis=1, tiled=True),
    )
    w_gate, w_up, w_down = (
        lax.all_gather(gate_weight, "tok", axis=0, tiled=True),
        lax.all_gather(up_weight, "tok", axis=0, tiled=True),
        lax.all_gather(down_weight, "tok", axis=0, tiled=True),
    )
    scaled = (input_lr[:, None] * values.astype(jnp.float32)).astype(jnp.bfloat16)
    key_gate = jnp.dot(keys, w_gate, preferred_element_type=jnp.float32)
    key_up = jnp.dot(keys, w_up, preferred_element_type=jnp.float32)
    gate_act = jax.nn.silu(key_gate)
    key_act = (gate_act * key_up).astype(jnp.bfloat16)
    back = jnp.dot(scaled, w_down, preferred_element_type=jnp.float32)
    d_gate = (-back * key_up * silu_slope(key_gate)).astype(jnp.bfloat16)
    d_up = (-back * gate_act).astype(jnp.bfloat16)
    width = gate_weight.shape[1]
    hidden = width * n_hid
    grads = lax.psum(
        jnp.concatenate(
            [
                contract_rows(keys, d_gate),
                contract_rows(keys, d_up),
                -contract_rows(scaled, key_act),
            ],
            axis=1,
        ),
        "tok",
    )
    olds = (w_gate, w_up, w_down)
    pieces = [grads[:, :width], grads[:, width : 2 * width], grads[:, 2 * width :]]
    weights = [old.astype(jnp.float32) for old in olds]
    renewed = []
    stats = []
    for weight, grad in zip(weights, pieces):
        stats.append(jnp.sum(weight * weight, axis=1))
        stats.append(jnp.sum(weight * grad, axis=1))
        stats.append(jnp.sum(grad * grad, axis=1))
    totals = lax.psum(
        (stats[0], stats[1], stats[2], stats[3], stats[4], stats[5], stats[6], stats[7], stats[8]),
        "hid",
    )
    for index in range(3):
        wsq = totals[3 * index] / hidden
        cross = totals[3 * index + 1] / hidden
        gsq = totals[3 * index + 2] / hidden
        scale = step_ratio * jnp.sqrt(wsq) / jnp.sqrt(gsq + epsilon)
        moved = weights[index] - scale[:, None] * pieces[index]
        msq = wsq - 2.0 * scale * cross + scale * scale * gsq
        renewed.append(finish(moved, wsq, msq))
    new_gate, new_up, new_down = (renewed[0], renewed[1], renewed[2])
    query_rows, grad_rows = (
        lax.all_gather(queries, "hid", axis=1, tiled=True),
        lax.all_gather(out_grad, "hid", axis=1, tiled=True),
    )
    query_gate = jnp.dot(query_rows, new_gate, preferred_element_type=jnp.float32)
    query_up = jnp.dot(query_rows, new_up, preferred_element_type=jnp.float32)
    query_silu = jax.nn.silu(query_gate)
    query_act = (query_silu * query_up).astype(jnp.bfloat16)
    out_part = contract_cols(query_act, new_down)
    query_back = jnp.dot(grad_rows, new_down, preferred_element_type=jnp.float32)
    q_gate_grad = (query_back * query_up * silu_slope(query_gate)).astype(jnp.bfloat16)
    q_up_grad = (query_back * query_silu).astype(jnp.bfloat16)
    grad_part = contract_cols(q_gate_grad, new_gate) + contract_cols(q_up_grad, new_up)
    out_sum, grad_sum = (
        lax.psum_scatter(
            out_part.astype(jnp.bfloat16), "hid", scatter_dimension=1, tiled=True
        ).astype(jnp.float32),
        lax.psum_scatter(
            grad_part.astype(jnp.bfloat16), "hid", scatter_dimension=1, tiled=True
        ).astype(jnp.float32),
    )
    return (out_sum.astype(jnp.bfloat16), grad_sum.astype(jnp.bfloat16))


def solution(mesh):
    n_tok, n_hid = mesh.shape["tok"], mesh.shape["hid"]

    def shards(*args):
        rows, cols = args[3].shape
        toks, count = args[0].shape[0], args[6].shape[0]
        fits = (
            n_hid == 2
            and n_tok == 8
            and rows % 16 == 0
            and cols % 256 == 0
            and toks % 256 == 0
            and count % 128 == 0
        )
        if fits:
            return direct(*args, n_tok, n_hid)
        return general(*args, n_hid)

    return jax.shard_map(
        shards,
        mesh=mesh,
        in_specs=(
            P(("scene", "tok"), "hid"),
            P(("scene", "tok"), "hid"),
            P(("scene", "tok")),
            P("tok", "hid"),
            P("tok", "hid"),
            P("tok", "hid"),
            P(("scene", "tok"), "hid"),
            P(("scene", "tok"), "hid"),
        ),
        out_specs=(P(("scene", "tok"), "hid"), P(("scene", "tok"), "hid")),
        check_vma=False,
    )
```

```python
import functools

import jax
import jax.numpy as jnp
from jax import lax
from jax.experimental import pallas as pl
from jax.experimental.pallas import tpu as pltpu
from jax.sharding import PartitionSpec as P

step_ratio = 0.5
epsilon = 1e-06
f32, bf16 = jnp.float32, jnp.bfloat16
LANES = 128


def contract(left, right, left_dim, right_dim):
    return lax.dot_general(
        left, right, (((left_dim,), (right_dim,)), ((), ())), preferred_element_type=f32
    )


def gated(gate, up):
    sigma = 0.5 * jnp.tanh(0.5 * gate) + 0.5
    silu = gate * sigma
    slope = sigma + silu * (1.0 - sigma)
    return silu, slope * up, silu * up


def join(full, mine, other, half):
    feats = mine.shape[-2]
    full[:, pl.ds(pl.multiple_of(half * feats, feats), feats), :] = mine[...]
    full[:, pl.ds(pl.multiple_of((1 - half) * feats, feats), feats), :] = other[...]


def backward(tokens, weights, deltas, acts):
    cols, total = acts.shape
    chunk = min(512, total)
    for start in range(0, total, chunk):
        span = slice(start, start + chunk)
        gate = contract(weights[0], tokens[0, :, span], 0, 0)
        up = contract(weights[1], tokens[0, :, span], 0, 0)
        back = contract(weights[2], tokens[1, :, span], 0, 0)
        silu, slope_up, act = gated(gate, up)
        deltas[:cols, span] = (back * slope_up).astype(bf16)
        deltas[cols:, span] = (back * silu).astype(bf16)
        acts[:, span] = act.astype(bf16)


def gradients(tokens, deltas, acts):
    cols = acts.shape[0]
    both = contract(tokens[0], deltas[...], 1, 1)
    return both[:, :cols], both[:, cols:], contract(tokens[1], acts[...], 1, 1)


def rows_kernel(groups, place, *refs):
    blocks, (weights,) = refs[: 2 * groups], refs[2 * groups :]
    group, side = place[0], place[1]
    for index, block in enumerate(blocks):
        flip, sided = index % groups, (side if index < groups else 1 - side)
        weights[:, rows_of((group ^ flip) * 2 + sided, block.shape[1]), :] = block[...]


def own_kernel(place, mine, other, weights, grads, tokens, deltas, acts):
    join(tokens, mine, other, place[2])
    backward(tokens, weights, deltas, acts)
    for index, grad in enumerate(gradients(tokens, deltas, acts)):
        grads[index] = grad


def owners_kernel(given, place, tokens, deltas, acts, before, *refs):
    outs, picked = refs[:-1], refs[-1]
    size = picked.shape[1] // 2
    owners = [rows_of(place[0] ^ (3 * spot) ^ given, size) for spot in range(2)]
    for spot, where in enumerate(owners):
        picked[:, spot * size : (spot + 1) * size, :] = tokens[:, where, :]
    short = size // len(outs)
    for index, grad in enumerate(gradients(picked, deltas, acts)):
        for spot, where in enumerate(owners):
            total = before[index, where, :] + grad[spot * size : (spot + 1) * size]
            for part, out in enumerate(outs):
                out[spot, index] = total[part * short : (part + 1) * short].astype(out.dtype)


def pair_kernel(place, mine, other, weights, before, *refs):
    outs, (tokens, deltas, acts, picked) = refs[:-4], refs[-4:]
    join(tokens, mine, other, place[2])
    backward(tokens, weights, deltas, acts)
    owners_kernel(1, place, tokens, deltas, acts, before, *outs, picked)


def rows_of(owner, rows):
    return pl.ds(pl.multiple_of(owner * rows, rows), rows)


def kept_kernel(parts, place, tokens, deltas, acts, before, weights, *refs):
    outs, olds, picked = refs[:parts], refs[parts : 2 * parts], refs[2 * parts]
    owners_kernel(0, place, tokens, deltas, acts, before, *outs, picked)
    for part, old in enumerate(olds):
        for spot in range(2):
            where = rows_of((place[0] ^ (3 * spot)) * parts + part, old.shape[2])
            old[spot] = weights[:, where, :]


def sum_kernel(olds, kept, came, crossed, grad_out, stats_out):
    rows = kept.shape[2]
    lane = lax.broadcasted_iota(jnp.int32, (rows, LANES), 1)
    both = []
    for spot in range(2):
        stats = jnp.zeros((rows, LANES), f32)
        for index in range(3):
            near = kept[spot, index] + came[spot, index].astype(f32)
            grad = near + crossed[1 - spot, index].astype(f32)
            grad_out[spot, index] = grad.astype(bf16)
            weight = olds[spot, index].astype(f32)
            for slot, product in enumerate((weight * weight, weight * grad, grad * grad)):
                row_sum = jnp.sum(product, axis=1, keepdims=True)
                stats = jnp.where(lane == 8 * slot + index, row_sum, stats)
        both.append(stats)
    stats_out[...] = jnp.concatenate(both, axis=0).T[: stats_out.shape[0]]


def factor_kernel(hidden, here, there, factors):
    sums = (here[...] + there[...]) / hidden
    wsq, cross, gsq = sums[:, :8], sums[:, 8:16], sums[:, 16:]
    scale = step_ratio * jnp.sqrt(wsq) / jnp.sqrt(gsq + epsilon)
    msq = wsq + 2.0 * scale * cross + scale * scale * gsq
    factor = jnp.sqrt(wsq) / jnp.sqrt(msq + epsilon)
    factors[:, :8] = factor
    factors[:, 8:] = scale * factor


def factors_kernel(hidden, here, there, near, near_there, own, others):
    factor_kernel(hidden, here, there, own)
    factor_kernel(hidden, near, near_there, others)


def answer(renewed, query, quests, half, kept, given):
    mine, other = quests
    feats = mine.shape[1]
    join(query, mine, other, half)
    gate = contract(renewed[0], query[0], 0, 0)
    up = contract(renewed[1], query[0], 0, 0)
    back = contract(renewed[2], query[1], 0, 0)
    silu, slope_up, act = gated(gate, up)
    out = contract(renewed[2], act.astype(bf16), 1, 0)
    grad = contract(renewed[0], (back * slope_up).astype(bf16), 1, 0) + contract(
        renewed[1], (back * silu).astype(bf16), 1, 0
    )
    for index, whole in enumerate((out, grad)):
        first, second = whole[:feats], whole[feats:]
        kept[index] = jnp.where(half == 0, first, second)
        given[index] = jnp.where(half == 0, second, first).astype(bf16)


def renew_kernel(parts, place, weights, *refs):
    grads, factors, quests, refs = refs[: 2 * parts], refs[2 * parts : 2 * parts + 2], refs[-6:-4], refs[-4:]
    renewed, kept, given, query = refs
    for spot in range(2):
        for near in range(2):
            for part in range(parts):
                grad = grads[near * parts + part]
                rows = grad.shape[2]
                where = rows_of((place[0] ^ ((3 * spot) ^ near)) * parts + part, rows)
                scales = factors[near][part].T[spot * rows : (spot + 1) * rows]
                for index in range(3):
                    old = weights[index, where, :].astype(f32) * scales[:, index : index + 1]
                    step = grad[spot, index].astype(f32) * scales[:, 8 + index : 9 + index]
                    renewed[index, where, :] = (old + step).astype(bf16)
    answer(renewed, query, quests, place[2], kept, given)


def query_kernel(place, renewed, mine, other, kept, given, query):
    answer(renewed, query, (mine, other), place[2], kept, given)


def last_kernel(kept, core, pair, out, grad):
    for index, target in enumerate((out, grad)):
        target[...] = (kept[index] + core[index].astype(f32) + pair[index].astype(f32)).astype(bf16)


def call(body, operands, outs, scratch=(), flops=0, place=None, mib=4):
    specs = [pl.BlockSpec(memory_space=pltpu.VMEM)] * len(operands)
    if place is not None:
        inner, body = body, lambda *refs: inner(place(), *refs)
    moved = sum(4 * leaf.size for leaf in (*operands, *outs))
    return pl.pallas_call(
        body,
        out_shape=list(outs),
        in_specs=specs,
        out_specs=[pl.BlockSpec(memory_space=pltpu.VMEM)] * len(outs),
        scratch_shapes=list(scratch),
        compiler_params=pltpu.CompilerParams(vmem_limit_bytes=mib * 1024 * 1024),
        cost_estimate=pl.CostEstimate(flops=flops, bytes_accessed=moved, transcendentals=0),
    )(*operands)


def direct(
    input_keys, input_values, input_lr, gate_weight, up_weight, down_weight, queries, out_grad,
    n_tok, n_hid,
):
    groups = n_tok // 2
    tok, half = lax.axis_index("tok"), lax.axis_index("hid")
    group, side = tok // 2, tok % 2

    def place():
        spot = lax.axis_index("tok")
        return spot >> 1, spot & 1, lax.axis_index("hid")

    core, pair, zed = 1, 2, 4

    def swap(array, flip):
        pairs = [(i, i ^ flip) for i in range(n_tok * n_hid)]
        return lax.ppermute(array, ("tok", "hid"), pairs)

    def gather(block):
        near, across = swap(block, zed), swap(block, 2 * zed)
        return [block, near, across, swap(across, zed)]

    stacked = jnp.stack([gate_weight, up_weight, down_weight])
    cols = stacked.shape[2] // 2
    own_w = lax.dynamic_slice_in_dim(stacked, side * cols, cols, 2)
    give_w = lax.dynamic_slice_in_dim(stacked, (1 - side) * cols, cols, 2)
    vals = (input_lr[None, :] * input_values.T.astype(f32)).astype(bf16)
    tokens = jnp.stack([input_keys.T, vals])
    _, feats, toks = tokens.shape
    first = gather(own_w)
    tokens, pair_w = lax.optimization_barrier((tokens, swap(give_w, pair)))
    second = gather(pair_w)
    pair_tokens = swap(tokens, pair)

    width = n_hid * feats
    rows = width // groups
    whole = (3, width, cols)
    block = (3, rows, cols)
    token_flops = 6 * 2 * toks * width * cols
    joined = [
        pltpu.VMEM((2, width, toks), bf16),
        pltpu.VMEM((2 * cols, toks), bf16),
        pltpu.VMEM((cols, toks), bf16),
    ]
    (weights,) = call(
        functools.partial(rows_kernel, groups),
        (*first, *second),
        (jax.ShapeDtypeStruct(whole, bf16),),
        place=place,
    )
    pair_tokens, weights = lax.optimization_barrier((pair_tokens, weights))
    (grads,) = call(
        own_kernel,
        (tokens, swap(tokens, core), weights),
        (jax.ShapeDtypeStruct(whole, f32),),
        joined,
        token_flops,
        place,
        16,
    )
    parts = 2
    block = (2, 3, rows // parts, cols)
    picked = pltpu.VMEM((2, 2 * rows, toks), bf16)
    *given, pair_tokens, deltas, acts = call(
        pair_kernel,
        (pair_tokens, swap(pair_tokens, core), weights, grads),
        [jax.ShapeDtypeStruct(block, bf16)] * parts
        + [jax.ShapeDtypeStruct(scratch.shape, scratch.dtype) for scratch in joined],
        [picked],
        token_flops * 3 // 4,
        place,
        16,
    )
    kept_olds = call(
        functools.partial(kept_kernel, parts),
        (pair_tokens, deltas, acts, grads, weights),
        [jax.ShapeDtypeStruct(block, f32)] * parts + [jax.ShapeDtypeStruct(block, bf16)] * parts,
        [picked],
        token_flops // 4,
        place,
        16,
    )
    kept, olds = kept_olds[:parts], kept_olds[parts:]
    quest, given = lax.optimization_barrier((jnp.stack([queries.T, out_grad.T]), given))
    quests = [quest] + [swap(quest, flip) for flip in (1, 2, 3)]
    came = [swap(part, zed) for part in given]
    came[0], quests[1:3] = lax.optimization_barrier((came[0], quests[1:3]))
    crossed = [swap((k + c.astype(f32)).astype(bf16), 3 * zed) for k, c in zip(kept, came)]
    sums, stats = zip(
        *(
            call(
                sum_kernel,
                (olds[part], kept[part], came[part], crossed[part]),
                (
                    jax.ShapeDtypeStruct(block, bf16),
                    jax.ShapeDtypeStruct((24, 2 * rows // parts), f32),
                ),
            )
            for part in range(parts)
        )
    )
    backs = [swap(part, zed) for part in sums]
    stats = jnp.stack(stats)
    there, backs[0] = lax.optimization_barrier((swap(stats, core), backs[0]))
    stats = stats + there
    shared = jax.ShapeDtypeStruct((parts, 16, 2 * rows // parts), f32)
    factors = call(
        functools.partial(factors_kernel, 2 * n_hid * cols),
        (stats, swap(stats, pair), swap(stats, zed), swap(stats, zed + pair)),
        (shared, shared),
    )

    count = queries.shape[0]
    piece = (2, feats, count)
    kept_given = [jax.ShapeDtypeStruct(piece, f32), jax.ShapeDtypeStruct(piece, bf16)]
    query = pltpu.VMEM((2, width, count), bf16)
    query_flops = 6 * 2 * count * width * cols
    renewed, kept, given = call(
        functools.partial(renew_kernel, parts),
        (weights, *sums, *backs, *factors, *quests[2:]),
        [jax.ShapeDtypeStruct(whole, bf16), *kept_given],
        [query],
        query_flops,
        place,
        16,
    )
    from_core, quests = lax.optimization_barrier((swap(given, core), quests))
    from_pair = swap((kept + from_core.astype(f32)).astype(bf16), pair)
    kept, given = call(
        query_kernel, (renewed, *quests[:2]), kept_given, [query], query_flops, place, 16
    )
    out, grad = call(
        last_kernel,
        (kept, swap(given, core), from_pair),
        [jax.ShapeDtypeStruct(piece[1:], bf16)] * 2,
    )
    return out.T, grad.T


def silu_slope(pre):
    sigma = jax.nn.sigmoid(pre)
    return sigma * (1.0 + pre * (1.0 - sigma))


def contract_rows(left, right):
    return lax.dot_general(
        left, right, (((0,), (0,)), ((), ())), preferred_element_type=jnp.float32
    )


def contract_cols(left, right):
    return lax.dot_general(
        left, right, (((1,), (1,)), ((), ())), preferred_element_type=jnp.float32
    )


def finish(moved, wsq, msq):
    return (moved * (jnp.sqrt(wsq) / jnp.sqrt(msq + epsilon))[:, None]).astype(jnp.bfloat16)


def general(
    input_keys, input_values, input_lr, gate_weight, up_weight, down_weight, queries, out_grad, n_hid
):
    keys, values = (
        lax.all_gather(input_keys, "hid", axis=1, tiled=True),
        lax.all_gather(input_values, "hid", axis=1, tiled=True),
    )
    w_gate, w_up, w_down = (
        lax.all_gather(gate_weight, "tok", axis=0, tiled=True),
        lax.all_gather(up_weight, "tok", axis=0, tiled=True),
        lax.all_gather(down_weight, "tok", axis=0, tiled=True),
    )
    scaled = (input_lr[:, None] * values.astype(jnp.float32)).astype(jnp.bfloat16)
    key_gate = jnp.dot(keys, w_gate, preferred_element_type=jnp.float32)
    key_up = jnp.dot(keys, w_up, preferred_element_type=jnp.float32)
    gate_act = jax.nn.silu(key_gate)
    key_act = (gate_act * key_up).astype(jnp.bfloat16)
    back = jnp.dot(scaled, w_down, preferred_element_type=jnp.float32)
    d_gate = (-back * key_up * silu_slope(key_gate)).astype(jnp.bfloat16)
    d_up = (-back * gate_act).astype(jnp.bfloat16)
    width = gate_weight.shape[1]
    hidden = width * n_hid
    grads = lax.psum(
        jnp.concatenate(
            [
                contract_rows(keys, d_gate),
                contract_rows(keys, d_up),
                -contract_rows(scaled, key_act),
            ],
            axis=1,
        ),
        "tok",
    )
    olds = (w_gate, w_up, w_down)
    pieces = [grads[:, :width], grads[:, width : 2 * width], grads[:, 2 * width :]]
    weights = [old.astype(jnp.float32) for old in olds]
    renewed = []
    stats = []
    for weight, grad in zip(weights, pieces):
        stats.append(jnp.sum(weight * weight, axis=1))
        stats.append(jnp.sum(weight * grad, axis=1))
        stats.append(jnp.sum(grad * grad, axis=1))
    totals = lax.psum(
        (stats[0], stats[1], stats[2], stats[3], stats[4], stats[5], stats[6], stats[7], stats[8]),
        "hid",
    )
    for index in range(3):
        wsq = totals[3 * index] / hidden
        cross = totals[3 * index + 1] / hidden
        gsq = totals[3 * index + 2] / hidden
        scale = step_ratio * jnp.sqrt(wsq) / jnp.sqrt(gsq + epsilon)
        moved = weights[index] - scale[:, None] * pieces[index]
        msq = wsq - 2.0 * scale * cross + scale * scale * gsq
        renewed.append(finish(moved, wsq, msq))
    new_gate, new_up, new_down = (renewed[0], renewed[1], renewed[2])
    query_rows, grad_rows = (
        lax.all_gather(queries, "hid", axis=1, tiled=True),
        lax.all_gather(out_grad, "hid", axis=1, tiled=True),
    )
    query_gate = jnp.dot(query_rows, new_gate, preferred_element_type=jnp.float32)
    query_up = jnp.dot(query_rows, new_up, preferred_element_type=jnp.float32)
    query_silu = jax.nn.silu(query_gate)
    query_act = (query_silu * query_up).astype(jnp.bfloat16)
    out_part = contract_cols(query_act, new_down)
    query_back = jnp.dot(grad_rows, new_down, preferred_element_type=jnp.float32)
    q_gate_grad = (query_back * query_up * silu_slope(query_gate)).astype(jnp.bfloat16)
    q_up_grad = (query_back * query_silu).astype(jnp.bfloat16)
    grad_part = contract_cols(q_gate_grad, new_gate) + contract_cols(q_up_grad, new_up)
    out_sum, grad_sum = (
        lax.psum_scatter(
            out_part.astype(jnp.bfloat16), "hid", scatter_dimension=1, tiled=True
        ).astype(jnp.float32),
        lax.psum_scatter(
            grad_part.astype(jnp.bfloat16), "hid", scatter_dimension=1, tiled=True
        ).astype(jnp.float32),
    )
    return (out_sum.astype(jnp.bfloat16), grad_sum.astype(jnp.bfloat16))


def solution(mesh):
    n_tok, n_hid = mesh.shape["tok"], mesh.shape["hid"]

    def shards(*args):
        rows, cols = args[3].shape
        toks, count = args[0].shape[0], args[6].shape[0]
        fits = (
            n_hid == 2
            and n_tok == 8
            and rows % 16 == 0
            and cols % 256 == 0
            and toks % 256 == 0
            and count % 128 == 0
        )
        if fits:
            return direct(*args, n_tok, n_hid)
        return general(*args, n_hid)

    return jax.shard_map(
        shards,
        mesh=mesh,
        in_specs=(
            P(("scene", "tok"), "hid"),
            P(("scene", "tok"), "hid"),
            P(("scene", "tok")),
            P("tok", "hid"),
            P("tok", "hid"),
            P("tok", "hid"),
            P(("scene", "tok"), "hid"),
            P(("scene", "tok"), "hid"),
        ),
        out_specs=(P(("scene", "tok"), "hid"), P(("scene", "tok"), "hid")),
        check_vma=False,
    )
```
